32 devices in a mesh: stack: 4 (over y, x), plane: 4 (over z), phys: 2 (over core).
Axes of the slice: x: 2, y: 2, z: 4, core: 2. Of those that a mesh axis runs over, the one named last changes fastest.
Arguments:
- thermal_offset: float32 [256, 64, 512], P('stack', 'plane', 'phys'), may hold values from -6 to 6
- volume_power_source: float32 [256, 64, 512], P('stack', 'plane', 'phys'), may hold values from -0.024 to 0.024
- substance_code: int32 [256, 64, 512], P('stack', 'plane', 'phys'), may hold values from 0 to 4
- creeping_joint_flag: int32 [256, 64, 512], P('stack', 'plane', 'phys'), may hold values 0 or 1
- imposed_overall_distortion: float32 [256, 64, 512], P('stack', 'plane', 'phys'), may hold values from -1 to 1
- plastic_distortion: float32 [256, 64, 512], P('stack', 'plane', 'phys'), may hold values from -3 to 3
- anand_hardness: float32 [256, 64, 512], P('stack', 'plane', 'phys'), may hold values from 0.8 to 2.4
Outputs:
- new_temperature: float32 [256, 64, 512], P('stack', 'plane', 'phys')
- new_creep_strain: float32 [256, 64, 512], P('stack', 'plane', 'phys')
- new_resistance: float32 [256, 64, 512], P('stack', 'plane', 'phys')
- stress_residual: float32 [256, 64, 512], P('stack', 'plane', 'phys')
The draws below stay inside these ranges and needn't reach their ends.
Inputs may be any that keep to these rules, and one draw needn't show every extreme that they name: `substance_code`: material of each cell: 0 die, 1 underfill, 2 solder ball, 3 substrate, 4 board.
All inputs are finite; a program needn't handle non-finite values. No bound on the sum of `creeping_joint_flag` on one device may be relied on, other than what follows from the above.
Results may differ from the reference program's by a relative error of at most 0.0003.
Values sent between devices are 32-bit elements; how exact they have to be, the bound alone decides.
No kernel may reach another device: no remote copies, remote signals or barrier semaphores. Data moves between devices by JAX's collectives and lax.ppermute only.
A program may use at most 128 MiB of HBM per device.

```python
import math
import jax
import jax.numpy as jnp
from jax import lax

TSTEPS = 3
STACK_LEVELS = 256
COUNT_ALONG_X = 64
COUNT_ALONG_Y = 512


def draw_volume_power_source(key, part):
    shape_all = (STACK_LEVELS, COUNT_ALONG_X, COUNT_ALONG_Y)
    return jnp.clip(0.004 * jax.random.normal(key, shape_all, jnp.float32), -0.024, 0.024)


def with_ends(drawn, rng, low, high):
    longest = drawn.shape.index(max(drawn.shape))
    spots = []
    for shift in (0, 1):
        where = [jax.random.randint(jax.random.fold_in(rng, axis), (), 0, length) for axis, length in enumerate(drawn.shape)]
        where[longest] = (where[longest] + shift) % drawn.shape[longest]
        spots.append(tuple(where))
    return drawn.at[spots[0]].set(low).at[spots[1]].set(high)


def block_levels(own_key, dims, shards, least, high):
    loudness, own = 1.0, jax.random.fold_in(own_key, 6)
    for position, blocks in shards:
        draws = jnp.exp(jax.random.uniform(jax.random.fold_in(own, position), (blocks,), jnp.float32, least / len(shards), high / len(shards)))
        loudness = loudness * jnp.repeat(draws, dims[position] // blocks).reshape([-1 if axis == position else 1 for axis in range(len(dims))])
    return loudness


def bell_draw(rng, extent, deviation, bound, shards=(), held_as=jnp.bfloat16):
    gain = block_levels(rng, extent, shards, -0.22, 0.18) if shards else 1.0
    array = jax.random.normal(rng, extent, jnp.float32) * deviation * gain
    return jnp.minimum(jnp.maximum(array, -bound), bound).astype(held_as)


def setup_inputs(seed: int = 0) -> dict:
    streams_of = jax.random.split(jax.random.key(seed), 8)
    thermal_offset = bell_draw(streams_of[0], (STACK_LEVELS, COUNT_ALONG_X, COUNT_ALONG_Y), 1.0, 6.0, ((0, 4), (1, 4), (2, 2)), jnp.float32)
    volume_power_source = draw_volume_power_source(jax.random.fold_in(streams_of[7], 71), 0)
    substance_code = with_ends(jax.random.randint(streams_of[2], (STACK_LEVELS, COUNT_ALONG_X, COUNT_ALONG_Y), 0, 5), jax.random.fold_in(streams_of[2], 1), 0, 4).astype(jnp.int32)
    creeping_joint_flag = with_ends((jax.random.randint(streams_of[3], (STACK_LEVELS, COUNT_ALONG_X, COUNT_ALONG_Y), 0, 2) < 1).astype(jnp.int32), jax.random.fold_in(streams_of[3], 1), 0, 1)
    imposed_overall_distortion = jnp.clip(jax.random.uniform(streams_of[4], (STACK_LEVELS, COUNT_ALONG_X, COUNT_ALONG_Y), jnp.float32, -1.0, 1.0) * block_levels(streams_of[4], (STACK_LEVELS, COUNT_ALONG_X, COUNT_ALONG_Y), ((0, 4), (1, 4), (2, 2)), -0.4, 0.0), -1.0, 1.0)
    plastic_distortion = bell_draw(streams_of[5], (STACK_LEVELS, COUNT_ALONG_X, COUNT_ALONG_Y), 0.3, 3.0, ((0, 4), (1, 4), (2, 2)), jnp.float32)
    anand_hardness = jnp.clip(jnp.exp(math.log(2.4) - 1.0986123 * jax.random.uniform(streams_of[6], (STACK_LEVELS, COUNT_ALONG_X, COUNT_ALONG_Y), jnp.float32) ** block_levels(streams_of[6], (STACK_LEVELS, COUNT_ALONG_X, COUNT_ALONG_Y), ((0, 4), (1, 4), (2, 2)), -0.2, 0.2)), 0.8, 2.4)
    return dict(thermal_offset=thermal_offset, volume_power_source=volume_power_source, substance_code=substance_code, creeping_joint_flag=creeping_joint_flag, imposed_overall_distortion=imposed_overall_distortion, plastic_distortion=plastic_distortion, anand_hardness=anand_hardness)


k_table = (4.0, 0.6, 2.5, 1.2, 0.8)
cap_table = (1.6, 1.8, 1.7, 2.0, 1.9)
mod_table = (1.5, 0.6, 0.9, 1.2, 0.8)
expand_table = (0.1, 0.3, 0.25, 0.15, 0.2)
cap_unit = 0.0003
lat_unit = 1.2e-05
h_conv = 0.05
creep_rate = 0.05
stress_mult = 0.5
act_energy = 2.0
sat_value = 2.0
sat_power = 0.1

def lookup(substance_code, values_table):
    result = jnp.zeros(substance_code.shape, jnp.float32)
    for entry_index, entry_value in enumerate(values_table):
        result = result + jnp.where(substance_code == entry_index, jnp.float32(entry_value), jnp.float32(0.0))
    return result

def conductance(first_k, second_k):
    return 2.0 * first_k * second_k / (first_k + second_k)

def lateral_flow(field_pad, conduct_pad):
    center = field_pad[:, 1:-1, 1:-1]
    center_k = conduct_pad[:, 1:-1, 1:-1]
    width_x = center.shape[1]
    width_y = center.shape[2]
    total_flow = jnp.zeros(center.shape, jnp.float32)
    for shift_x, shift_y in ((2, 1), (0, 1), (1, 2), (1, 0)):
        near_field = field_pad[:, shift_x:shift_x + width_x, shift_y:shift_y + width_y]
        near_k = conduct_pad[:, shift_x:shift_x + width_x, shift_y:shift_y + width_y]
        total_flow = total_flow + lat_unit * conductance(center_k, near_k) * (near_field - center)
    return total_flow

def vertical_terms(conduct_pad, capacity, global_rows, total_rows):
    inner_k = conduct_pad[:, 1:-1, 1:-1]
    center = inner_k[1:-1]
    lower_band = -conductance(inner_k[:-2], center)
    upper_band = -conductance(inner_k[2:], center)
    edge_loss = jnp.where((global_rows == 0) | (global_rows == total_rows - 1), jnp.float32(h_conv), jnp.float32(0.0))
    main_band = capacity - lower_band - upper_band + edge_loss
    return (lower_band, main_band, upper_band)

def thomas(lower_band, main_band, upper_band, right_side):
    zero_rows = jnp.zeros(main_band.shape[1:], jnp.float32)

    def forward(state_carry, row_data):
        c_prev, d_prev = state_carry
        a_row, b_row, c_row, d_row = row_data
        pivot_value = b_row - a_row * c_prev
        c_new = c_row / pivot_value
        d_new = (d_row - a_row * d_prev) / pivot_value
        return ((c_new, d_new), (c_new, d_new))
    _, (c_mod, d_mod) = lax.scan(forward, (zero_rows, zero_rows), (lower_band, main_band, upper_band, right_side))

    def backward(next_value, row_data):
        c_row, d_row = row_data
        x_row = d_row - c_row * next_value
        return (x_row, x_row)
    _, solution = lax.scan(backward, zero_rows, (c_mod, d_mod), reverse=True)
    return solution

def creep_update(current_reading, substance_code, creeping_joint_flag, imposed_overall_distortion, plastic_distortion, anand_hardness):
    modulus = lookup(substance_code, mod_table)
    expansion = lookup(substance_code, expand_table)
    tangential_traction = modulus * (imposed_overall_distortion - plastic_distortion - expansion * current_reading)
    absolute = 1.5 + 0.5 * jnp.tanh(0.25 * current_reading)
    arrhenius = jnp.exp(-act_energy / absolute)
    drive_term = jnp.sinh(stress_mult * jnp.abs(tangential_traction) / anand_hardness)
    rate_term = creep_rate * arrhenius * drive_term
    saturation = sat_value * (0.5 + drive_term) ** sat_power
    gap_term = 1.0 - anand_hardness / saturation
    active = creeping_joint_flag == 1
    creep_new = jnp.where(active, plastic_distortion + jnp.sign(tangential_traction) * rate_term, plastic_distortion)
    resist_new = jnp.where(active, anand_hardness + gap_term * jnp.sqrt(jnp.abs(gap_term)) * rate_term, anand_hardness)
    stress_new = modulus * (imposed_overall_distortion - creep_new - expansion * current_reading)
    return (creep_new, resist_new, stress_new)

def stress_balance(padded):
    center = padded[1:-1, 1:-1, 1:-1]
    total_sum = padded[2:, 1:-1, 1:-1] + padded[:-2, 1:-1, 1:-1]
    total_sum = total_sum + padded[1:-1, 2:, 1:-1] + padded[1:-1, :-2, 1:-1]
    total_sum = total_sum + padded[1:-1, 1:-1, 2:] + padded[1:-1, 1:-1, :-2]
    return total_sum - 6.0 * center

def reference(thermal_offset, volume_power_source, substance_code, creeping_joint_flag, imposed_overall_distortion, plastic_distortion, anand_hardness):
    conduct = lookup(substance_code, k_table)
    capacity = cap_unit * lookup(substance_code, cap_table)
    conduct_pad = jnp.pad(conduct, 1)
    global_rows = lax.broadcasted_iota(jnp.int32, (STACK_LEVELS, 1, 1), 0)
    lower_band, main_band, upper_band = vertical_terms(conduct_pad, capacity, global_rows, STACK_LEVELS)
    lateral_k = conduct_pad[1:-1]
    current_reading = thermal_offset
    tangential_traction = jnp.zeros_like(thermal_offset)
    for time_step in range(TSTEPS):
        field_pad = jnp.pad(current_reading, ((0, 0), (1, 1), (1, 1)))
        right_side = capacity * current_reading + lateral_flow(field_pad, lateral_k) + volume_power_source
        current_reading = thomas(lower_band, main_band, upper_band, right_side)
        plastic_distortion, anand_hardness, tangential_traction = creep_update(current_reading, substance_code, creeping_joint_flag, imposed_overall_distortion, plastic_distortion, anand_hardness)
    residual = stress_balance(jnp.pad(tangential_traction, 1))
    return (current_reading, plastic_distortion, anand_hardness, residual)
```

```python
import functools

import jax
import jax.numpy as jnp
from jax import lax
from jax.experimental import pallas as pl
from jax.experimental.pallas import tpu as pltpu
from jax.sharding import PartitionSpec as P

TSTEPS = 3

k_table = (4.0, 0.6, 2.5, 1.2, 0.8)
cap_table = (1.6, 1.8, 1.7, 2.0, 1.9)
mod_table = (1.5, 0.6, 0.9, 1.2, 0.8)
expand_table = (0.1, 0.3, 0.25, 0.15, 0.2)
cap_unit = 0.0003
lat_unit = 1.2e-05
h_conv = 0.05
creep_rate = 0.05
log2e = 1.4426950408889634
inv_e = 0.36787944117144233

LANES = 128
SUB = 8
F32 = jnp.float32


def loop(count, body, init, unroll=4, reverse=False):
    while count % unroll:
        unroll -= 1

    def group(step, carry):
        for j in range(unroll):
            place = step * unroll + j
            carry = body(count - 1 - place if reverse else place, carry)
        return carry

    return lax.fori_loop(0, count // unroll, group, init)


def rcp(x):
    return pl.reciprocal(x, approx=True)


def by_code(code, table, scale=1.0):
    result = jnp.full(code.shape, table[4] * scale, F32)
    for entry in range(4):
        result = jnp.where(code == entry, F32(table[entry] * scale), result)
    return result


def cap_by_k(k):
    result = jnp.full(k.shape, cap_unit * cap_table[4], F32)
    for entry in range(4):
        result = jnp.where(k == F32(k_table[entry]), F32(cap_unit * cap_table[entry]), result)
    return result


def conductance(p, q, scale=1.0):
    return (2.0 * scale) * p * q * rcp(jnp.maximum(p + q, 1e-6))


def call(body, ins, outs, name, flops=0, scratch=()):
    spec = pl.BlockSpec(memory_space=pltpu.VMEM)
    size = sum(a.size * 4 for a in ins) + sum(4 * functools.reduce(lambda x, y: x * y, s) for s in outs)
    return pl.pallas_call(
        body,
        in_specs=[spec] * len(ins),
        out_specs=[spec] * len(outs),
        out_shape=[jax.ShapeDtypeStruct(s, F32) for s in outs],
        scratch_shapes=list(scratch),
        compiler_params=pltpu.CompilerParams(vmem_limit_bytes=16 * 2**20),
        cost_estimate=pl.CostEstimate(flops=flops, bytes_accessed=size, transcendentals=0),
        name=name,
    )(*ins)


def pair_swaps(axis):
    count = lax.axis_size(axis)
    first = [(i, i + 1) for i in range(0, count - 1, 2)]
    second = [(i, i + 1) for i in range(1, count - 1, 2)]
    return [pairs + [(b, a) for a, b in pairs] for pairs in (first, second)]


def even(axis):
    return lax.rem(lax.axis_index(axis), 2) == 0


def edge_rows(t_ref, q_ref, code_ref, a_ref, b_ref):
    x = t_ref.shape[1]
    is_even = even("plane")

    def side(near, far, beyond):
        k1 = by_code(code_ref[:, near, :], k_table)
        k2 = by_code(code_ref[:, far, :], k_table)
        k3 = by_code(code_ref[:, beyond, :], k_table)
        t2 = t_ref[:, far, :]
        flow = conductance(k2, k3, lat_unit) * (t_ref[:, beyond, :] - t2)
        return (t_ref[:, near, :], t2, k1, k2, q_ref[:, near, :], q_ref[:, far, :] + flow)

    top = side(x - 1, x - 2, x - 3)
    bottom = side(0, 1, 2)
    for i in range(6):
        a_ref[i] = jnp.where(is_even, top[i], bottom[i])
        b_ref[i] = jnp.where(is_even, bottom[i], top[i])


def factor_rows(get_k, capm_extra, levels, out):
    cap_ref, w_ref, r_ref, yr_ref, left_ref, g_ref = out
    first_extra, last_extra = capm_extra
    zero = jnp.zeros(w_ref.shape[1:], F32)

    def forward(i, carry):
        ws, y, k_here = carry
        k_next = get_k(jnp.minimum(i + 1, levels - 1))
        cap = cap_by_k(k_here)
        cap_ref[i] = cap
        extra = jnp.where(i == 0, first_extra, 0.0) + jnp.where(i == levels - 1, last_extra, 0.0)
        s = cap + extra + ws
        u = jnp.where(i == levels - 1, 0.0, conductance(k_here, k_next))
        r = rcp(s + u)
        w = u * r
        w_ref[i] = w
        r_ref[i] = r
        yr_ref[i] = y * r
        return (w * s, y * w, k_next)

    k_first = get_k(0)
    _, _, k_last = loop(levels, forward, (zero, zero + 1.0, k_first))

    def backward(i, left):
        left = yr_ref[i] + w_ref[i] * left
        left_ref[i] = left
        return left

    left = loop(levels, backward, zero, reverse=True)
    g_ref[0] = left + 0.5 * rcp(jnp.maximum(k_first, 1e-3))
    g_ref[1] = yr_ref[levels - 1]
    g_ref[2] = r_ref[levels - 1] + 0.5 * rcp(jnp.maximum(k_last, 1e-3))


def end_losses():
    place, count = lax.axis_index("stack"), lax.axis_size("stack")
    return (jnp.where(place == 0, F32(h_conv), F32(0.0)), jnp.where(place == count - 1, F32(h_conv), F32(0.0)))


def factor_main(code_ref, k_ref, *out):
    def get_k(i):
        return by_code(code_ref[i], k_table)

    def keep(i, carry):
        k_ref[i] = get_k(i)
        return carry

    levels = code_ref.shape[0]
    loop(levels, keep, 0)
    factor_rows(lambda i: k_ref[i], end_losses(), levels, out)


def lane_edge(tile_pair, i, pack):
    low, high = tile_pair
    at_low = lax.axis_index("phys") == 1
    edge = jnp.where(at_low, low, high)
    shift = jnp.where(at_low, i, lax.rem(i + 1, LANES))
    lane = lax.broadcasted_iota(jnp.int32, edge.shape, 1)
    return jnp.where(lane == i, pltpu.roll(edge, shift, 1), pack)


def lane_unedge(pack, i):
    at_low = lax.axis_index("phys") == 1
    shift = jnp.where(at_low, lax.rem(LANES - i, LANES), LANES - 1 - i)
    moved = pltpu.roll(pack, shift, 1)
    lane = lax.broadcasted_iota(jnp.int32, pack.shape, 1)
    return (jnp.where((lane == 0) & at_low, moved, 0.0), jnp.where((lane == LANES - 1) & (~at_low), moved, 0.0))


def add_lane_edges(value, pack, i):
    low, high = lane_unedge(pack, i)
    tiles = [value[:, j : j + LANES] for j in range(0, value.shape[1], LANES)]
    tiles[0] = tiles[0] + low
    tiles[-1] = tiles[-1] + high
    return jnp.concatenate(tiles, axis=1)


def assemble_halo(a_ref, b_ref, k_ref, t_ref, kh_ref, th_ref, qh_ref, pack_ref):
    is_even = even("plane")
    levels, x, width = k_ref.shape
    row = lax.broadcasted_iota(jnp.int32, (SUB, width), 0)

    def level(i, carry):
        pack_t, pack_k = carry
        halos = []
        for first, ref in ((0, th_ref), (2, kh_ref), (4, qh_ref)):
            values = []
            for j in (first, first + 1):
                a = a_ref[j, pl.ds(i, 1), :]
                b = b_ref[j, pl.ds(i, 1), :]
                values.append((jnp.where(is_even, a, b), jnp.where(is_even, b, a)))
            halo = jnp.where(row == 0, values[0][0], 0.0)
            halo = jnp.where(row == 1, values[1][0], halo)
            halo = jnp.where(row == SUB - 1, values[0][1], halo)
            halo = jnp.where(row == SUB - 2, values[1][1], halo)
            ref[i] = halo
            halos.append(halo)
        t = jnp.concatenate([t_ref[i], halos[0]], axis=0)
        k = jnp.concatenate([k_ref[i], halos[1]], axis=0)
        pack_t = lane_edge((t[:, :LANES], t[:, width - LANES :]), i, pack_t)
        pack_k = lane_edge((k[:, :LANES], k[:, width - LANES :]), i, pack_k)
        return (pack_t, pack_k)

    zero = jnp.zeros((x + SUB, LANES), F32)
    pack_t, pack_k = loop(levels, level, (zero, zero))
    pack_ref[0] = pack_t
    pack_ref[1] = pack_k


def factor_halo(k_ref, kh_ref, gx_ref, gxh_ref, gy_ref, gyh_ref, *out):
    levels, x, width = k_ref.shape
    lane = lax.broadcasted_iota(jnp.int32, (x + SUB, width), 1)

    def lateral(i, carry):
        k = jnp.concatenate([k_ref[i], kh_ref[i]], axis=0)
        gx = conductance(k, pltpu.roll(k, x + SUB - 1, 0), lat_unit)
        gy = conductance(k, pltpu.roll(k, width - 1, 1), lat_unit)
        gy = jnp.where(lane == width - 1, 0.0, gy)
        gx_ref[i], gxh_ref[i] = gx[:x], gx[x:]
        gy_ref[i], gyh_ref[i] = gy[:x], gy[x:]
        return carry

    loop(levels, lateral, 0)
    factor_rows(lambda i: kh_ref[i], end_losses(), levels, out)


def both(main_ref, halo_ref, i):
    return jnp.concatenate([main_ref[i], halo_ref[i]], axis=0)


def right_side(send_g, last, *refs):
    (t, th, q, qh, cap, caph, gx, gxh, gy, gyh, w, wh, r, rh, left, lefth, own, other, own_k, other_k) = refs[:20]
    refs = refs[20:]
    if send_g:
        g, gh = refs[:2]
        refs = refs[2:]
    levels, x, width = t.shape
    if last:
        z, send = refs
    else:
        z, zh, send = refs
    rows = x if last else x + SUB
    flow = conductance(own_k[...], other_k[...], lat_unit) * (other[...] - own[...])

    def pick(main_ref, halo_ref, i):
        return main_ref[i] if last else both(main_ref, halo_ref, i)

    def level(i, carry):
        wy, bf = carry
        temp = both(t, th, i)
        fy = both(gy, gyh, i) * (pltpu.roll(temp, width - 1, 1) - temp)
        fx = both(gx, gxh, i) * (pltpu.roll(temp, x + SUB - 1, 0) - temp)
        lateral = fx - pltpu.roll(fx, 1, 0) + fy - pltpu.roll(fy, 1, 1)
        lateral = add_lane_edges(lateral, flow, i)[:rows]
        rhs = pick(cap, caph, i) * temp[:rows] + pick(q, qh, i) + lateral
        y = rhs + wy
        zz = y * pick(r, rh, i)
        z[i] = zz[:x]
        if not last:
            zh[i] = zz[x:]
        return (pick(w, wh, i) * y, bf + pick(left, lefth, i) * rhs)

    zero = jnp.zeros((rows, width), F32)
    _, bf = loop(levels, level, (zero, zero))
    send[0] = bf
    send[1] = pick(z, None if last else zh, levels - 1)
    if send_g:
        for j in range(3):
            send[2 + j] = both(g, gh, j)


def interface_flows(g_sets, b_sets, rows, place, count):
    def at(sets, entry, block):
        value = sets[0][entry][:rows]
        for j in range(1, count):
            value = jnp.where((place ^ j) == block, sets[j][entry][:rows], value)
        return value

    diag, off, rhs = [], [], []
    for j in range(count - 1):
        diag.append(at(g_sets, 4, j) + at(g_sets, 2, j + 1))
        off.append(at(g_sets, 3, j + 1))
        rhs.append(at(b_sets, 0, j + 1) - at(b_sets, 1, j))
    ups, vals = [], []
    for j in range(count - 1):
        pivot, value = diag[j], rhs[j]
        if j:
            pivot = pivot - off[j - 1] * ups[j - 1]
            value = value + off[j - 1] * vals[j - 1]
        inverse = rcp(pivot)
        ups.append(off[j] * inverse)
        vals.append(value * inverse)
    flows = [None] * (count - 1)
    for j in reversed(range(count - 1)):
        flows[j] = vals[j] if j == count - 2 else vals[j] + ups[j] * flows[j + 1]
    return flows


def column_solve(count, first, last, *refs):
    g_sets, refs = refs[:count], refs[count:]
    if first:
        b_sets = g_sets
    else:
        b_sets, refs = refs[:count], refs[count:]
    if last:
        z, w, r, yr, t = refs
    else:
        z, zh, w, wh, r, rh, yr, yrh, t, th, pack_ref = refs
    levels, x, width = z.shape
    rows = x if last else x + SUB
    place = lax.axis_index("stack")

    def pick(main_ref, halo_ref, i):
        return main_ref[i] if last else both(main_ref, halo_ref, i)

    flows = interface_flows(g_sets, b_sets, rows, place, count)
    zero = jnp.zeros((rows, width), F32)
    top, bottom = zero, zero
    for j in range(count - 1):
        top = jnp.where(place == j + 1, -flows[j], top)
        bottom = jnp.where(place == j, flows[j], bottom)

    def level(i, carry):
        add, pack = carry
        value = pick(z, None if last else zh, i) + top * pick(yr, None if last else yrh, i) + add
        t[i] = value[:x]
        if not last:
            th[i] = value[x:]
            pack = lane_edge((value[:, :LANES], value[:, width - LANES :]), i, pack)
        below = jnp.maximum(i - 1, 0)
        return (pick(w, None if last else wh, below) * value, pack)

    init = (bottom * pick(r, None if last else rh, levels - 1), jnp.zeros((rows, LANES), F32))
    _, pack = loop(levels, level, init, reverse=True)
    if not last:
        pack_ref[...] = pack


def prepare_creep(code_ref, flag_ref, mod_ref, exp_ref, rate_ref):
    def level(i, carry):
        code = code_ref[i]
        mod_ref[i] = by_code(code, mod_table)
        exp_ref[i] = by_code(code, expand_table)
        rate_ref[i] = jnp.where(flag_ref[i] == 1, F32(0.5 * creep_rate * inv_e), F32(0.0))
        return carry

    loop(code_ref.shape[0], level, 0)


def creep_cells(temp, mod, exp, rate, dist, creep, hard):
    elastic = dist - exp * temp
    drive = jnp.exp2((0.5 * log2e) * mod * (elastic - creep) * rcp(hard))
    drive = drive - rcp(drive)
    size = jnp.abs(drive)
    rate = rate * jnp.exp2(-log2e * rcp(jnp.exp2((0.5 * log2e) * temp + 1.0) + 1.0))
    gap = 1.0 - hard * jnp.exp2(-0.1 * jnp.log2(1.0 + size) - 0.9)
    gap_size = jnp.abs(gap)
    root = gap_size * lax.rsqrt(jnp.maximum(gap_size, 1e-30))
    creep = creep + rate * drive
    hard = hard + gap * root * (rate * size)
    return (elastic, creep, hard)


def creep_step(t, mod, exp, rate, dist, creep, hard, creep_out, hard_out):
    def level(i, carry):
        _, creep_out[i], hard_out[i] = creep_cells(t[i], mod[i], exp[i], rate[i], dist[i], creep[i], hard[i])
        return carry

    loop(t.shape[0], level, 0, unroll=2)


def creep_last(t, mod, exp, rate, dist, creep, hard, creep_out, hard_out, s, xa, xb, za, zb, pack_ref):
    levels, x, width = t.shape

    def level(i, pack):
        m = mod[i]
        elastic, new, hard_out[i] = creep_cells(t[i], m, exp[i], rate[i], dist[i], creep[i], hard[i])
        creep_out[i] = new
        stress = m * (elastic - new)
        s[i] = stress
        return lane_edge((stress[:, :LANES], stress[:, width - LANES :]), i, pack)

    pack_ref[...] = loop(levels, level, jnp.zeros((x, LANES), F32), unroll=2)
    is_even = even("plane")
    top, bottom = s[:, x - 1, :], s[:, 0, :]
    xa[...] = jnp.where(is_even, top, bottom)
    xb[...] = jnp.where(is_even, bottom, top)
    is_even = even("stack")
    za[...] = jnp.where(is_even, s[levels - 1], s[0])
    zb[...] = jnp.where(is_even, s[0], s[levels - 1])


def balance(s, xa, xb, za, zb, other, out):
    levels, x, width = s.shape
    plane_even, stack_even = even("plane"), even("stack")
    row = lax.broadcasted_iota(jnp.int32, (x, width), 0)
    lane = lax.broadcasted_iota(jnp.int32, (x, width), 1)
    z_after = jnp.where(stack_even, za[...], zb[...])
    z_before = jnp.where(stack_even, zb[...], za[...])

    def level(i, before):
        here = s[i]
        a, b = xa[pl.ds(i, 1), :], xb[pl.ds(i, 1), :]
        upper, lower = jnp.where(plane_even, a, b), jnp.where(plane_even, b, a)
        after = jnp.where(i == levels - 1, z_after, s[jnp.minimum(i + 1, levels - 1)])
        total = before + after - 6.0 * here
        total = total + jnp.where(row == 0, lower, pltpu.roll(here, 1, 0))
        total = total + jnp.where(row == x - 1, upper, pltpu.roll(here, x - 1, 0))
        total = total + jnp.where(lane == 0, 0.0, pltpu.roll(here, 1, 1))
        total = total + jnp.where(lane == width - 1, 0.0, pltpu.roll(here, width - 1, 1))
        out[i] = add_lane_edges(total, other[...], i)
        return here

    loop(levels, level, z_before)


def per_device(temp, source, code, flag, distortion, creep, hard):
    levels, x, width = temp.shape
    count = lax.axis_size("stack")
    if lax.axis_size("phys") != 2 or count & (count - 1) or levels > LANES or x % SUB or width % LANES:
        raise ValueError("unsupported sizes")
    main, halo = (levels, x, width), (levels, SUB, width)
    cells = levels * x * width
    swap = [(0, 1), (1, 0)]
    plane_swaps, stack_swaps = pair_swaps("plane"), pair_swaps("stack")
    peers = [[(i, i ^ j) for i in range(count)] for j in range(1, count)]

    rows_a, rows_b = call(edge_rows, (temp, source, code), [(6, levels, width)] * 2, "edge_rows", cells)
    rows_a = lax.ppermute(rows_a, "plane", plane_swaps[0])
    rows_b = lax.ppermute(rows_b, "plane", plane_swaps[1])
    k, *fact = call(factor_main, (code,), [main] * 6 + [(3, x, width)], "factor_main", 20 * cells)
    kh, th, qh, pack = call(
        assemble_halo, (rows_a, rows_b, k, temp), [halo] * 3 + [(2, x + SUB, LANES)], "assemble_halo", 3 * cells
    )
    other = lax.ppermute(pack, "phys", swap)
    gx, gxh, gy, gyh, *facth = call(
        factor_halo, (k, kh), [main, halo, main, halo] + [halo] * 5 + [(3, SUB, width)], "factor_halo", 20 * cells
    )
    own_k, other_k, own, other = pack[1], other[1], pack[0], other[0]
    cap, w, r, yr, left, g = fact
    caph, wh, rh, yrh, lefth, gh = facth
    mod, exp, rate = call(prepare_creep, (code, flag), [main] * 3, "prepare_creep", 10 * cells)

    rows = x + SUB
    for step in range(TSTEPS):
        first, last = step == 0, step == TSTEPS - 1
        ins = [temp, th, source, qh, cap, caph, gx, gxh, gy, gyh, w, wh, r, rh, left, lefth, own, other, own_k, other_k]
        ins += [g, gh] if first else []
        send = (5 if first else 2, x if last else rows, width)
        outs = call(
            functools.partial(right_side, first, last), ins, [main, send] if last else [main, halo, send], "right_side", 30 * cells
        )
        z, zh, own_b = outs[0], outs[1], outs[-1]
        b_sets = [own_b] + [lax.ppermute(own_b, "stack", peer) for peer in peers]
        if first:
            g_sets = b_sets
        if step:
            creep, hard = call(
                creep_step, (temp, mod, exp, rate, distortion, creep, hard), [main] * 2, "creep_step", 60 * cells
            )
        ins = list(g_sets) + ([] if first else b_sets)
        if last:
            (temp,) = call(
                functools.partial(column_solve, count, first, last), ins + [z, w, r, yr], [main], "column_solve", 10 * cells
            )
        else:
            temp, th, own = call(
                functools.partial(column_solve, count, first, last),
                ins + [z, zh, w, wh, r, rh, yr, yrh],
                [main, halo, (rows, LANES)],
                "column_solve",
                10 * cells,
            )
            other = lax.ppermute(own, "phys", swap)

    creep, hard, stress, xa, xb, za, zb, pack = call(
        creep_last,
        (temp, mod, exp, rate, distortion, creep, hard),
        [main] * 3 + [(levels, width)] * 2 + [(x, width)] * 2 + [(x, LANES)],
        "creep_last",
        60 * cells,
    )
    xa = lax.ppermute(xa, "plane", plane_swaps[0])
    xb = lax.ppermute(xb, "plane", plane_swaps[1])
    za = lax.ppermute(za, "stack", stack_swaps[0])
    zb = lax.ppermute(zb, "stack", stack_swaps[1])
    other = lax.ppermute(pack, "phys", swap)
    (residual,) = call(balance, (stress, xa, xb, za, zb, other), [main], "balance", 10 * cells)
    return (temp, creep, hard, residual)


def solution(mesh):
    spec = P("stack", "plane", "phys")
    return jax.shard_map(per_device, mesh=mesh, in_specs=(spec,) * 7, out_specs=(spec,) * 4, check_vma=False)
```

```python
import functools

import jax
import jax.numpy as jnp
from jax import lax
from jax.experimental import pallas as pl
from jax.experimental.pallas import tpu as pltpu
from jax.sharding import PartitionSpec as P

TSTEPS = 3

k_table = (4.0, 0.6, 2.5, 1.2, 0.8)
cap_table = (1.6, 1.8, 1.7, 2.0, 1.9)
mod_table = (1.5, 0.6, 0.9, 1.2, 0.8)
expand_table = (0.1, 0.3, 0.25, 0.15, 0.2)
cap_unit = 0.0003
lat_unit = 1.2e-05
h_conv = 0.05
creep_rate = 0.05
log2e = 1.4426950408889634
inv_e = 0.36787944117144233

LANES = 128
SUB = 8
F32 = jnp.float32


def loop(count, body, init, unroll=16, reverse=False):
    while count % unroll:
        unroll -= 1

    def group(step, carry):
        for j in range(unroll):
            place = step * unroll + j
            carry = body(count - 1 - place if reverse else place, carry)
        return carry

    return lax.fori_loop(0, count // unroll, group, init)


def rcp(x):
    return pl.reciprocal(x, approx=True)


def by_code(code, table, scale=1.0):
    result = jnp.full(code.shape, table[4] * scale, F32)
    for entry in range(4):
        result = jnp.where(code == entry, F32(table[entry] * scale), result)
    return result


def cap_by_k(k):
    result = jnp.full(k.shape, cap_unit * cap_table[4], F32)
    for entry in range(4):
        result = jnp.where(k == F32(k_table[entry]), F32(cap_unit * cap_table[entry]), result)
    return result


def conductance(p, q, scale=1.0):
    return (2.0 * scale) * p * q * rcp(jnp.maximum(p + q, 1e-6))


VMEM = pl.BlockSpec(memory_space=pltpu.VMEM)
HBM = pl.BlockSpec(memory_space=pltpu.HBM)
ANY = pl.BlockSpec(memory_space=pl.ANY)


def call(body, ins, outs, name, flops=0, scratch=(), after=(), in_hbm=0, out_hbm=0, aliases=None, vmem=16):
    n_in, n_after = len(ins), len(after)

    def kernel(*refs):
        body(*refs[:n_in], *refs[n_in + n_after :])

    outs = [o if isinstance(o, jax.ShapeDtypeStruct) else jax.ShapeDtypeStruct(o, F32) for o in outs]
    size = sum(a.size * 4 for a in list(ins) + outs)
    return pl.pallas_call(
        kernel if after else body,
        in_specs=[HBM] * in_hbm + [VMEM] * (n_in - in_hbm) + [ANY] * n_after,
        out_specs=[HBM] * out_hbm + [VMEM] * (len(outs) - out_hbm),
        out_shape=outs,
        scratch_shapes=list(scratch),
        input_output_aliases=aliases or {},
        compiler_params=pltpu.CompilerParams(vmem_limit_bytes=vmem * 2**20),
        cost_estimate=pl.CostEstimate(flops=flops, bytes_accessed=size, transcendentals=0),
        name=name,
    )(*ins, *after)


def pair_swaps(axis):
    count = lax.axis_size(axis)
    first = [(i, i + 1) for i in range(0, count - 1, 2)]
    second = [(i, i + 1) for i in range(1, count - 1, 2)]
    return [pairs + [(b, a) for a, b in pairs] for pairs in (first, second)]


def even(axis):
    return lax.rem(lax.axis_index(axis), 2) == 0


def edge_rows(t_in, code_in, q_in, a_ref, b_ref, t, code, q, sem):
    levels, x, width = t_in.shape
    rows = (x - 1, x - 2, x - 3, 0, 1, 2)
    copies = []
    for j, row in enumerate(rows):
        for entry, (source, held) in enumerate(((t_in, t), (code_in, code), (q_in, q))):
            if entry < 2 or j % 3 < 2:
                copies.append(pltpu.make_async_copy(source.at[:, row, :], held.at[j], sem.at[entry, j]))
    for copy in copies:
        copy.start()
    for copy in copies:
        copy.wait()
    is_even = even("plane")

    def side(near):
        k1, k2, k3 = (by_code(code[near + j], k_table) for j in range(3))
        flow = conductance(k2, k3, lat_unit) * (t[near + 2] - t[near + 1])
        return (t[near], t[near + 1], k1, k2, q[near], q[near + 1] + flow)

    top, bottom = side(0), side(3)
    for i in range(6):
        a_ref[i] = jnp.where(is_even, top[i], bottom[i])
        b_ref[i] = jnp.where(is_even, bottom[i], top[i])


def edge_layers(code, flag, dist, creep, hard, g, a_ref, b_ref):
    last = code.shape[0] - 1
    is_even = even("stack")
    for j in range(3):
        a_ref[j] = g[j]
        b_ref[j] = g[j]
    for j, source in enumerate((code, flag, dist, creep, hard)):
        after, before = source[last].astype(F32), source[0].astype(F32)
        a_ref[3 + j] = jnp.where(is_even, after, before)
        b_ref[3 + j] = jnp.where(is_even, before, after)


def factor_rows(get_k, capm_extra, levels, out):
    cap_ref, w_ref, r_ref, yr_ref, left_ref, g_ref = out
    first_extra, last_extra = capm_extra
    zero = jnp.zeros(w_ref.shape[1:], F32)

    def forward(i, carry):
        ws, y, k_here = carry
        k_next = get_k(jnp.minimum(i + 1, levels - 1))
        cap = cap_by_k(k_here)
        cap_ref[i] = cap
        extra = jnp.where(i == 0, first_extra, 0.0) + jnp.where(i == levels - 1, last_extra, 0.0)
        s = cap + extra + ws
        u = jnp.where(i == levels - 1, 0.0, conductance(k_here, k_next))
        r = rcp(s + u)
        w = u * r
        w_ref[i] = w
        r_ref[i] = r
        yr_ref[i] = y * r
        return (w * s, y * w, k_next)

    k_first = get_k(0)
    _, _, k_last = loop(levels, forward, (zero, zero + 1.0, k_first))

    def backward(i, left):
        left = yr_ref[i] + w_ref[i] * left
        left_ref[i] = left
        return left

    left = loop(levels, backward, zero, reverse=True)
    g_ref[0] = left + 0.5 * rcp(jnp.maximum(k_first, 1e-3))
    g_ref[1] = yr_ref[levels - 1]
    g_ref[2] = r_ref[levels - 1] + 0.5 * rcp(jnp.maximum(k_last, 1e-3))


def end_losses():
    place, count = lax.axis_index("stack"), lax.axis_size("stack")
    return (jnp.where(place == 0, F32(h_conv), F32(0.0)), jnp.where(place == count - 1, F32(h_conv), F32(0.0)))


def lane_edge(tile_pair, i, pack):
    low, high = tile_pair
    at_low = lax.axis_index("phys") == 1
    edge = jnp.where(at_low, low, high)
    shift = jnp.where(at_low, i, lax.rem(i + 1, LANES))
    lane = lax.broadcasted_iota(jnp.int32, edge.shape, 1)
    return jnp.where(lane == i, pltpu.roll(edge, shift, 1), pack)


def lane_unedge(pack, i):
    at_low = lax.axis_index("phys") == 1
    shift = jnp.where(at_low, lax.rem(LANES - i, LANES), LANES - 1 - i)
    moved = pltpu.roll(pack, shift, 1)
    lane = lax.broadcasted_iota(jnp.int32, pack.shape, 1)
    return (jnp.where((lane == 0) & at_low, moved, 0.0), jnp.where((lane == LANES - 1) & (~at_low), moved, 0.0))


def add_lane_edges(value, pack, i):
    low, high = lane_unedge(pack, i)
    tiles = [value[:, j : j + LANES] for j in range(0, value.shape[1], LANES)]
    tiles[0] = tiles[0] + low
    tiles[-1] = tiles[-1] + high
    return jnp.concatenate(tiles, axis=1)


def factor_main(code_ref, t_ref, gx_ref, gy_ref, pack_ref, k_ref, *out):
    levels, x, width = t_ref.shape
    row = lax.broadcasted_iota(jnp.int32, (x, width), 0)
    lane = lax.broadcasted_iota(jnp.int32, (x, width), 1)

    def lateral(i, carry):
        pack_t, pack_k = carry
        k = by_code(code_ref[i], k_table)
        k_ref[i] = k
        gx = conductance(k, pltpu.roll(k, x - 1, 0), lat_unit)
        gx_ref[i] = jnp.where(row == x - 1, 0.0, gx)
        gy = conductance(k, pltpu.roll(k, width - 1, 1), lat_unit)
        gy_ref[i] = jnp.where(lane == width - 1, 0.0, gy)
        t = t_ref[i]
        pack_t = lane_edge((t[:, :LANES], t[:, width - LANES :]), i, pack_t)
        pack_k = lane_edge((k[:, :LANES], k[:, width - LANES :]), i, pack_k)
        return (pack_t, pack_k)

    zero = jnp.zeros((x, LANES), F32)
    pack_ref[0], pack_ref[1] = loop(levels, lateral, (zero, zero))
    factor_rows(lambda i: k_ref[i], end_losses(), levels, out)


def assemble_halo(a_ref, b_ref, kh_ref, th_ref, qh_ref, pack_ref):
    is_even = even("plane")
    levels, _, width = kh_ref.shape
    row = lax.broadcasted_iota(jnp.int32, (SUB, width), 0)
    a_rows = [row == jnp.where(is_even, j, SUB - 1 - j) for j in (0, 1)]
    b_rows = [row == jnp.where(is_even, SUB - 1 - j, j) for j in (0, 1)]

    def level(i, carry):
        pack_t, pack_k = carry
        halos = []
        for first, ref in ((0, th_ref), (2, kh_ref), (4, qh_ref)):
            halo = jnp.zeros((SUB, width), F32)
            for source, rows in ((a_ref, a_rows), (b_ref, b_rows)):
                for j in (0, 1):
                    halo = jnp.where(rows[j], source[first + j, pl.ds(i, 1), :], halo)
            ref[i] = halo
            halos.append(halo)
        t, k = halos[0], halos[1]
        pack_t = lane_edge((t[:, :LANES], t[:, width - LANES :]), i, pack_t)
        pack_k = lane_edge((k[:, :LANES], k[:, width - LANES :]), i, pack_k)
        return (pack_t, pack_k)

    zero = jnp.zeros((SUB, LANES), F32)
    pack_ref[0], pack_ref[1] = loop(levels, level, (zero, zero))


def factor_halo(k_ref, kh_ref, gx_in, gx_ref, gxh_ref, gyh_ref, *out):
    levels, x, width = k_ref.shape
    row = lax.broadcasted_iota(jnp.int32, (SUB, width), 0)
    lane = lax.broadcasted_iota(jnp.int32, (SUB, width), 1)

    def lateral(i, carry):
        k = kh_ref[i]
        k_next = jnp.where(row == SUB - 1, k_ref[i, 0:1, :], pltpu.roll(k, SUB - 1, 0))
        gxh_ref[i] = conductance(k, k_next, lat_unit)
        gx_ref[i, x - 1 : x, :] = conductance(k_ref[i, x - 1 : x, :], k[0:1], lat_unit)
        gy = conductance(k, pltpu.roll(k, width - 1, 1), lat_unit)
        gyh_ref[i] = jnp.where(lane == width - 1, 0.0, gy)
        return carry

    loop(levels, lateral, 0)
    factor_rows(lambda i: kh_ref[i], end_losses(), levels, out)


def both(main_ref, halo_ref, i):
    return jnp.concatenate([main_ref[i], halo_ref[i]], axis=0)


def right_side(first, last, *refs):
    (t, th, q, qh, cap, caph, gx, gxh, gy, gyh, w, wh, r, rh, left, lefth, km, kh, other_km, other_kh) = refs[:20]
    refs = refs[20:]
    own_k = jnp.concatenate([km[1], kh[1]], axis=0)
    other_k = jnp.concatenate([other_km[1], other_kh[1]], axis=0)
    if first:
        gh, refs = refs[0], refs[1:]
        own = jnp.concatenate([km[0], kh[0]], axis=0)
        other = jnp.concatenate([other_km[0], other_kh[0]], axis=0)
    else:
        own, other = refs[0][...], refs[1][...]
        refs = refs[2:]
    levels, x, width = t.shape
    if last:
        z, send = refs
    else:
        z, zh, send = refs
    rows = x if last else x + SUB
    flow = conductance(own_k, other_k, lat_unit) * (other - own)
    flow = flow[:rows]

    def pick(main_ref, halo_ref, i):
        return main_ref[i] if last else both(main_ref, halo_ref, i)

    def level(i, carry):
        wy, bf = carry
        temp = both(t, th, i)
        here = temp[:rows]
        fy = pick(gy, gyh, i) * (pltpu.roll(here, width - 1, 1) - here)
        fx = both(gx, gxh, i) * (pltpu.roll(temp, x + SUB - 1, 0) - temp)
        lateral = (fx - pltpu.roll(fx, 1, 0))[:rows] + fy - pltpu.roll(fy, 1, 1)
        lateral = add_lane_edges(lateral, flow, i)
        rhs = pick(cap, caph, i) * here + pick(q, qh, i) + lateral
        y = rhs + wy
        zz = y * pick(r, rh, i)
        z[i] = zz[:x]
        if not last:
            zh[i] = zz[x:]
        return (pick(w, wh, i) * y, bf + pick(left, lefth, i) * rhs)

    zero = jnp.zeros((rows, width), F32)
    _, bf = loop(levels, level, (zero, zero), unroll=16 if last else 8)
    parts = [bf, pick(z, None if last else zh, levels - 1)]
    groups = [part[j : j + SUB] for part in parts for j in range(0, x, SUB)]
    if not last:
        groups.append(packed(*[part[x:] for part in parts]))
    if first:
        groups += [packed(gh[0], gh[1]), packed(gh[2], gh[2])]
    for j, group in enumerate(groups):
        send[j] = group


def packed(a, b):
    row = lax.broadcasted_iota(jnp.int32, a.shape, 0)
    return jnp.where((row >= 2) & (row < 6), pltpu.roll(b, 4, 0), a)


def block_flows(g_sets, h_sets, b_sets, x, rows):
    place, count = lax.axis_index("stack"), lax.axis_size("stack")

    def at(sets, block, read):
        value = read(sets[0])
        for j in range(1, count):
            value = jnp.where((place ^ j) == block, read(sets[j]), value)
        return value

    def ends(block):
        group = at(b_sets, block, lambda ref: ref[0 : 2 * x // SUB])
        group = group.reshape(2, x, group.shape[-1])
        if rows == x:
            return (group[0], group[1])
        tail = at(b_sets, block, lambda ref: ref[2 * x // SUB])
        return (
            jnp.concatenate([group[0], tail], axis=0),
            jnp.concatenate([group[1], pltpu.roll(tail, 4, 0)], axis=0),
        )

    def responses(block):
        group = at(g_sets, block, lambda ref: ref[0:3])
        if rows == x:
            return group
        tail = at(h_sets, block, lambda ref: ref[2 * x // SUB + 1 : 2 * x // SUB + 3])
        tails = (tail[0], pltpu.roll(tail[0], 4, 0), tail[1])
        return [jnp.concatenate([group[j], tails[j]], axis=0) for j in range(3)]

    end = [ends(block) for block in range(count)]
    g = [responses(block) for block in range(count)]
    ups, flows = [], []
    for j in range(count - 1):
        pivot = g[j][2] + g[j + 1][0]
        value = end[j + 1][0] - end[j][1]
        if j:
            pivot = pivot - g[j][1] * ups[j - 1]
            value = value + g[j][1] * flows[j - 1]
        inverse = rcp(pivot)
        ups.append(g[j + 1][1] * inverse)
        flows.append(value * inverse)
    for j in reversed(range(count - 2)):
        flows[j] = flows[j] + ups[j] * flows[j + 1]
    top = jnp.zeros_like(flows[0])
    bottom = top
    for j in range(count - 1):
        top = jnp.where(place == j + 1, -flows[j], top)
        bottom = jnp.where(place == j, flows[j], bottom)
    return top, bottom


def beside(edge, flow, k_edge, code_beside):
    return edge + flow * (0.5 * rcp(k_edge) + 0.5 * rcp(by_code(code_beside, k_table)))


def layers_beside(za, zb):
    is_even = even("stack")
    sides = []
    for j in (0, 1):
        value = [jnp.where(is_even, (zb, za)[j][3 + e], (za, zb)[j][3 + e]) for e in range(5)]
        value[4] = jnp.maximum(value[4], 0.1)
        sides.append(value)
    return sides


def rate_by_flag(active):
    return jnp.where(active, F32(0.5 * creep_rate * inv_e), F32(0.0))


def column_solve(count, first, *refs):
    g_sets, h_sets, refs = refs[:count], refs[count : 2 * count], refs[2 * count :]
    b_sets = h_sets
    if not first:
        b_sets, refs = refs[:count], refs[count:]
    z, zh, w, wh, r, rh, yr, yrh, t, th, pack_ref, flow_ref = refs
    levels, x, width = z.shape
    rows = x + SUB
    top, bottom = block_flows(g_sets, h_sets, b_sets, x, rows)
    flow_ref[0], flow_ref[1] = top[:x], bottom[:x]

    def level(i, carry):
        add, pack = carry
        value = both(z, zh, i) + top * both(yr, yrh, i) + add
        t[i] = value[:x]
        th[i] = value[x:]
        pack = lane_edge((value[:, :LANES], value[:, width - LANES :]), i, pack)
        return (both(w, wh, jnp.maximum(i - 1, 0)) * value, pack)

    init = (bottom * both(r, rh, levels - 1), jnp.zeros((rows, LANES), F32))
    _, pack_ref[...] = loop(levels, level, init, reverse=True)


def prepare_creep(code_ref, flag_ref, mod, exp, rate):
    def level(i, carry):
        code = code_ref[i]
        mod[i] = by_code(code, mod_table)
        exp[i] = by_code(code, expand_table)
        rate[i] = rate_by_flag(flag_ref[i] == 1)
        return carry

    loop(code_ref.shape[0], level, 0)


def creep_cells(temp, mod, exp, rate, dist, creep, hard):
    elastic = dist - exp * temp
    drive = jnp.exp2((0.5 * log2e) * mod * (elastic - creep) * rcp(hard))
    drive = drive - rcp(drive)
    size = jnp.abs(drive)
    rate = rate * jnp.exp2(-log2e * rcp(jnp.exp2((0.5 * log2e) * temp + 1.0) + 1.0))
    gap = 1.0 - hard * jnp.exp2(-0.1 * jnp.log2(1.0 + size) - 0.9)
    gap_size = jnp.abs(gap)
    root = gap_size * lax.rsqrt(jnp.maximum(gap_size, 1e-30))
    creep = creep + rate * drive
    hard = hard + gap * root * (rate * size)
    return (elastic, creep, hard)


def creep_beside(t, flow, k, za, zb, state):
    ends, results = (0, t.shape[0] - 1), []
    for j, (code, flag, dist, creep, hard) in enumerate(layers_beside(za, zb)):
        if state is not None:
            creep, hard = state[j], state[2 + j]
        temp = beside(t[ends[j]], flow[j], k[ends[j]], code)
        mod = by_code(code, mod_table)
        cells = creep_cells(temp, mod, by_code(code, expand_table), rate_by_flag(flag == 1.0), dist, creep, hard)
        results.append((*cells, mod))
    return results


def creep_step(first, *refs):
    main, refs = refs[:7], refs[7:]
    flow, k, za, zb = refs[:4]
    state, out = (None, refs[4:]) if first else (refs[4], refs[5:])

    def level(i, carry):
        _, out[0][i], out[1][i] = creep_cells(*[ref[i] for ref in main])
        return carry

    loop(main[0].shape[0], level, 0, unroll=8)
    for j, (_, creep, hard, _) in enumerate(creep_beside(main[0], flow, k, za, zb, state)):
        out[2][j] = creep
        out[2][2 + j] = hard


def solve_and_creep(count, *refs):
    g_sets, b_sets, refs = refs[:count], refs[count : 2 * count], refs[2 * count :]
    z, w, r, yr, k, za, zb, state = refs[:8]
    mod, exp, rate, dist, creep, hard = refs[8:14]
    t, creep_out, hard_out, s, zs, xa, xb, pack_ref = refs[14:]
    levels, x, width = z.shape
    top, bottom = block_flows(g_sets, None, b_sets, x, x)

    def level(i, carry):
        add, pack = carry
        value = z[i] + top * yr[i] + add
        t[i] = value
        m = mod[i]
        elastic, new, hard_out[i] = creep_cells(value, m, exp[i], rate[i], dist[i], creep[i], hard[i])
        creep_out[i] = new
        stress = m * (elastic - new)
        s[i] = stress
        pack = lane_edge((stress[:, :LANES], stress[:, width - LANES :]), i, pack)
        return (w[jnp.maximum(i - 1, 0)] * value, pack)

    init = (bottom * r[levels - 1], jnp.zeros((x, LANES), F32))
    _, pack_ref[...] = loop(levels, level, init, unroll=8, reverse=True)
    place = lax.axis_index("stack")
    for j, (elastic, new, _, m) in enumerate(creep_beside(t, (top, bottom), k, za, zb, state)):
        zs[j] = jnp.where(place == (0, count - 1)[j], 0.0, m * (elastic - new))
    is_even = even("plane")
    upper, lower = s[:, x - 1, :], s[:, 0, :]
    xa[...] = jnp.where(is_even, upper, lower)
    xb[...] = jnp.where(is_even, lower, upper)


def balance_inside(s, zs, t, creep, hard, t_out, creep_out, hard_out, inside, sem):
    copies = [
        pltpu.make_async_copy(held, out, sem.at[j])
        for j, (held, out) in enumerate(((t, t_out), (creep, creep_out), (hard, hard_out)))
    ]
    for copy in copies:
        copy.start()
    levels, x, width = s.shape
    row = lax.broadcasted_iota(jnp.int32, (x, width), 0)
    lane = lax.broadcasted_iota(jnp.int32, (x, width), 1)

    def level(i, before):
        here = s[i]
        after = jnp.where(i == levels - 1, zs[1], s[jnp.minimum(i + 1, levels - 1)])
        total = before + after - 6.0 * here
        total = total + jnp.where(row == 0, 0.0, pltpu.roll(here, 1, 0))
        total = total + jnp.where(row == x - 1, 0.0, pltpu.roll(here, x - 1, 0))
        total = total + jnp.where(lane == 0, 0.0, pltpu.roll(here, 1, 1))
        inside[i] = total + jnp.where(lane == width - 1, 0.0, pltpu.roll(here, width - 1, 1))
        return here

    loop(levels, level, zs[0])
    for copy in copies:
        copy.wait()


def balance_edges(inside, xa, xb, other, out, held, sem):
    levels, x, width = inside.shape
    is_even = even("plane")
    row = lax.broadcasted_iota(jnp.int32, (x, width), 0)
    a_row = row == jnp.where(is_even, x - 1, 0)
    b_row = row == jnp.where(is_even, 0, x - 1)
    chunks = sem.shape[0]
    part = levels // chunks
    copies = []
    for chunk in range(chunks):

        def level(j, carry, chunk=chunk):
            i = chunk * part + j
            total = inside[i] + jnp.where(a_row, xa[pl.ds(i, 1), :], 0.0)
            total = total + jnp.where(b_row, xb[pl.ds(i, 1), :], 0.0)
            held[i] = add_lane_edges(total, other[...], i)
            return carry

        loop(part, level, 0)
        place = pl.ds(chunk * part, part)
        copies.append(pltpu.make_async_copy(held.at[place], out.at[place], sem.at[chunk]))
        copies[-1].start()
    for copy in copies:
        copy.wait()


def per_device(temp, source, code, flag, distortion, creep, hard):
    levels, x, width = temp.shape
    count = lax.axis_size("stack")
    if lax.axis_size("phys") != 2 or count != 4 or levels > LANES or x % SUB or width % LANES:
        raise ValueError("unsupported sizes")
    main, halo, layers = (levels, x, width), (levels, SUB, width), (2, x, width)
    cells = levels * x * width
    swap = [(0, 1), (1, 0)]
    plane_swaps = pair_swaps("plane")
    peers = [[(i, i ^ j) for i in range(count)] for j in range(1, count)]
    dma = pltpu.SemaphoreType.DMA

    edge = (6, levels, width)
    rows_a, rows_b = call(
        edge_rows,
        (temp, code, source),
        [edge] * 2,
        "edge_rows",
        cells,
        [pltpu.VMEM(edge, F32), pltpu.VMEM(edge, jnp.int32), pltpu.VMEM(edge, F32), dma((3, 6))],
        in_hbm=3,
        vmem=60,
    )
    rows_a = lax.ppermute(rows_a, "plane", plane_swaps[0])
    rows_b = lax.ppermute(rows_b, "plane", plane_swaps[1])
    gx, gy, pack, k, *fact = call(
        factor_main, (code, temp), [main, main, (2, x, LANES)] + [main] * 6 + [(3, x, width)], "factor_main", 40 * cells
    )
    cap, w, r, yr, left, g = fact
    other_pack = lax.ppermute(pack, "phys", swap)
    za, zb = call(edge_layers, (code, flag, distortion, creep, hard, g), [(8, x, width)] * 2, "edge_layers", cells)
    za, g_two, zb = lax.ppermute(za, "stack", peers[0]), lax.ppermute(g, "stack", peers[1]), lax.ppermute(zb, "stack", peers[2])
    g_sets = [g, za, g_two, zb]
    mod, exp, rate = call(prepare_creep, (code, flag), [main] * 3, "prepare_creep", 10 * cells)

    kh, th, qh, packh = call(
        assemble_halo, (rows_a, rows_b), [halo] * 3 + [(2, SUB, LANES)], "assemble_halo", cells, after=(rate, other_pack)
    )
    other_packh = lax.ppermute(packh, "phys", swap)
    gx, gxh, gyh, caph, wh, rh, yrh, lefth, gh = call(
        factor_halo,
        (k, kh, gx),
        [main, halo, halo] + [halo] * 5 + [(3, SUB, width)],
        "factor_halo",
        20 * cells,
        aliases={2: 0},
    )

    rows = x + SUB
    own = other = state = None
    for step in range(TSTEPS):
        first, last = step == 0, step == TSTEPS - 1
        ins = [temp, th, source, qh, cap, caph, gx, gxh, gy, gyh, w, wh, r, rh, left, lefth]
        ins += [pack, packh, other_pack, other_packh]
        ins += [gh] if first else [own, other]
        send = (2 * x // SUB + (3 if first else 0 if last else 1), SUB, width)
        outs = call(
            functools.partial(right_side, first, last), ins, [main, send] if last else [main, halo, send], "right_side", 30 * cells
        )
        z, zh, own_b = outs[0], outs[1], outs[-1]
        b_sets = [own_b] + [lax.ppermute(own_b, "stack", peer) for peer in peers]
        if first:
            h_sets = b_sets
        else:
            creep, hard, state = call(
                functools.partial(creep_step, step == 1),
                [temp, mod, exp, rate, distortion, creep, hard, flow, k, za, zb] + ([] if step == 1 else [state]),
                [main] * 2 + [(4, x, width)],
                "creep_step",
                60 * cells,
            )
        if last:
            break
        temp, th, own, flow = call(
            functools.partial(column_solve, count, first),
            g_sets + h_sets + ([] if first else b_sets) + [z, zh, w, wh, r, rh, yr, yrh],
            [main, halo, (rows, LANES), layers],
            "column_solve",
            10 * cells,
            after=() if first else (creep,),
        )
        other = lax.ppermute(own, "phys", swap)

    temp, creep, hard, stress, zs, xa, xb, pack = call(
        functools.partial(solve_and_creep, count),
        g_sets + b_sets + [z, w, r, yr, k, za, zb, state, mod, exp, rate, distortion, creep, hard],
        [main] * 4 + [layers] + [(levels, width)] * 2 + [(x, LANES)],
        "solve_and_creep",
        70 * cells,
    )
    xa = lax.ppermute(xa, "plane", plane_swaps[0])
    xb = lax.ppermute(xb, "plane", plane_swaps[1])
    other = lax.ppermute(pack, "phys", swap)
    temp, creep, hard, inside = call(
        balance_inside, (stress, zs, temp, creep, hard), [main] * 4, "balance_inside", 20 * cells, [dma((3,))], out_hbm=3
    )
    (residual,) = call(
        balance_edges,
        (inside, xa, xb, other),
        [main],
        "balance_edges",
        10 * cells,
        [pltpu.VMEM(main, F32), dma((4,))],
        out_hbm=1,
    )
    return (temp, creep, hard, residual)


def solution(mesh):
    spec = P("stack", "plane", "phys")
    return jax.shard_map(per_device, mesh=mesh, in_specs=(spec,) * 7, out_specs=(spec,) * 4, check_vma=False)
```

```python
import functools

import jax
import jax.numpy as jnp
from jax import lax
from jax.experimental import pallas as pl
from jax.experimental.pallas import tpu as pltpu
from jax.sharding import PartitionSpec as P

TSTEPS = 3

k_table = (4.0, 0.6, 2.5, 1.2, 0.8)
cap_table = (1.6, 1.8, 1.7, 2.0, 1.9)
mod_table = (1.5, 0.6, 0.9, 1.2, 0.8)
expand_table = (0.1, 0.3, 0.25, 0.15, 0.2)
cap_unit = 0.0003
lat_unit = 1.2e-05
h_conv = 0.05
creep_rate = 0.05
log2e = 1.4426950408889634
inv_e = 0.36787944117144233

LANES = 128
SUB = 8
F32 = jnp.float32


def loop(count, body, init, unroll=16, reverse=False):
    while count % unroll:
        unroll -= 1

    def group(step, carry):
        for j in range(unroll):
            place = step * unroll + j
            carry = body(count - 1 - place if reverse else place, carry)
        return carry

    return lax.fori_loop(0, count // unroll, group, init)


def rcp(x):
    return pl.reciprocal(x, approx=True)


def by_code(code, table, scale=1.0):
    result = jnp.full(code.shape, table[4] * scale, F32)
    for entry in range(4):
        result = jnp.where(code == entry, F32(table[entry] * scale), result)
    return result


def cap_by_k(k):
    result = jnp.full(k.shape, cap_unit * cap_table[4], F32)
    for entry in range(4):
        result = jnp.where(k == F32(k_table[entry]), F32(cap_unit * cap_table[entry]), result)
    return result


def conductance(p, q, scale=1.0):
    return (2.0 * scale) * p * q * rcp(jnp.maximum(p + q, 1e-6))


VMEM = pl.BlockSpec(memory_space=pltpu.VMEM)
HBM = pl.BlockSpec(memory_space=pltpu.HBM)
ANY = pl.BlockSpec(memory_space=pl.ANY)


def call(body, ins, outs, name, flops=0, scratch=(), after=(), in_hbm=0, out_hbm=0, aliases=None, vmem=16):
    n_in, n_after = len(ins), len(after)

    def kernel(*refs):
        body(*refs[:n_in], *refs[n_in + n_after :])

    outs = [o if isinstance(o, jax.ShapeDtypeStruct) else jax.ShapeDtypeStruct(o, F32) for o in outs]
    size = sum(a.size * 4 for a in list(ins) + outs)
    return pl.pallas_call(
        kernel if after else body,
        in_specs=[HBM] * in_hbm + [VMEM] * (n_in - in_hbm) + [ANY] * n_after,
        out_specs=[HBM] * out_hbm + [VMEM] * (len(outs) - out_hbm),
        out_shape=outs,
        scratch_shapes=list(scratch),
        input_output_aliases=aliases or {},
        compiler_params=pltpu.CompilerParams(vmem_limit_bytes=vmem * 2**20),
        cost_estimate=pl.CostEstimate(flops=flops, bytes_accessed=size, transcendentals=0),
        name=name,
    )(*ins, *after)


def pair_swaps(axis):
    count = lax.axis_size(axis)
    first = [(i, i + 1) for i in range(0, count - 1, 2)]
    second = [(i, i + 1) for i in range(1, count - 1, 2)]
    return [pairs + [(b, a) for a, b in pairs] for pairs in (first, second)]


def even(axis):
    return lax.rem(lax.axis_index(axis), 2) == 0


def edge_rows(t_in, code_in, q_in, a_ref, b_ref, t, code, q, sem):
    levels, x, width = t_in.shape
    rows = (x - 1, x - 2, x - 3, 0, 1, 2)
    copies = []
    for j, row in enumerate(rows):
        for entry, (source, held) in enumerate(((t_in, t), (code_in, code), (q_in, q))):
            if entry < 2 or j % 3 < 2:
                copies.append(pltpu.make_async_copy(source.at[:, row, :], held.at[j], sem.at[entry, j]))
    for copy in copies:
        copy.start()
    for copy in copies:
        copy.wait()
    is_even = even("plane")

    def side(near):
        k1, k2, k3 = (by_code(code[near + j], k_table) for j in range(3))
        flow = conductance(k2, k3, lat_unit) * (t[near + 2] - t[near + 1])
        return (t[near], t[near + 1], k1, k2, q[near], q[near + 1] + flow)

    top, bottom = side(0), side(3)
    for i in range(6):
        a_ref[i] = jnp.where(is_even, top[i], bottom[i])
        b_ref[i] = jnp.where(is_even, bottom[i], top[i])


def edge_layers(code, flag, dist, creep, hard, g, a_ref, b_ref):
    last = code.shape[0] - 1
    is_even = even("stack")
    for j in range(3):
        a_ref[j] = g[j]
        b_ref[j] = g[j]
    for j, source in enumerate((code, flag, dist, creep, hard)):
        after, before = source[last].astype(F32), source[0].astype(F32)
        a_ref[3 + j] = jnp.where(is_even, after, before)
        b_ref[3 + j] = jnp.where(is_even, before, after)


def end_losses():
    place, count = lax.axis_index("stack"), lax.axis_size("stack")
    return (jnp.where(place == 0, F32(h_conv), F32(0.0)), jnp.where(place == count - 1, F32(h_conv), F32(0.0)))


def lane_edge(tile_pair, i, pack):
    low, high = tile_pair
    at_low = lax.axis_index("phys") == 1
    edge = jnp.where(at_low, low, high)
    shift = jnp.where(at_low, i, lax.rem(i + 1, LANES))
    lane = lax.broadcasted_iota(jnp.int32, edge.shape, 1)
    return jnp.where(lane == i, pltpu.roll(edge, shift, 1), pack)


def lane_edge_of(value, i, pack):
    return lane_edge((value[:, :LANES], value[:, value.shape[1] - LANES :]), i, pack)


def lane_unedge(pack, i):
    at_low = lax.axis_index("phys") == 1
    shift = jnp.where(at_low, lax.rem(LANES - i, LANES), LANES - 1 - i)
    lane = lax.broadcasted_iota(jnp.int32, pack.shape, 1)
    return jnp.where(lane == jnp.where(at_low, 0, LANES - 1), pltpu.roll(pack, shift, 1), 0.0)


def add_at_edge(value, edge):
    at_low = lax.axis_index("phys") == 1
    tiles = [value[:, j : j + LANES] for j in range(0, value.shape[1], LANES)]
    tiles[0] = tiles[0] + jnp.where(at_low, edge, 0.0)
    tiles[-1] = tiles[-1] + jnp.where(at_low, 0.0, edge)
    return jnp.concatenate(tiles, axis=1)


def factor_main(code_ref, t_ref, q_ref, gx_ref, gy_ref, p_ref, pack_ref, k_ref, cap_ref, w_ref, r_ref, yr_ref, left_ref, g_ref):
    levels, x, width = t_ref.shape
    row = lax.broadcasted_iota(jnp.int32, (x, width), 0)
    lane = lax.broadcasted_iota(jnp.int32, (x, width), 1)
    first_loss, last_loss = end_losses()

    def lateral(i, carry):
        pack_t, pack_k = carry
        k = by_code(code_ref[i], k_table)
        k_ref[i] = k
        cap = by_code(code_ref[i], cap_table, cap_unit)
        cap_ref[i] = cap
        gx = conductance(k, pltpu.roll(k, x - 1, 0), lat_unit)
        gx = jnp.where(row == x - 1, 0.0, gx)
        gx_ref[i] = gx
        gy = conductance(k, pltpu.roll(k, width - 1, 1), lat_unit)
        gy = jnp.where(lane == width - 1, 0.0, gy)
        gy_ref[i] = gy
        t = t_ref[i]
        fy = gy * (pltpu.roll(t, width - 1, 1) - t)
        fx = gx * (pltpu.roll(t, x - 1, 0) - t)
        p_ref[i] = cap * t + q_ref[i] + fx - pltpu.roll(fx, 1, 0) + fy - pltpu.roll(fy, 1, 1)
        return (lane_edge_of(t, i, pack_t), lane_edge_of(k, i, pack_k))

    tile = jnp.zeros((x, LANES), F32)
    pack_ref[0], pack_ref[1] = loop(levels, lateral, (tile, tile), unroll=8)
    zero = jnp.zeros((x, width), F32)

    def forward(i, carry):
        ws, y, k_here = carry
        k_next = k_ref[jnp.minimum(i + 1, levels - 1)]
        loss = jnp.where(i == 0, first_loss, 0.0) + jnp.where(i == levels - 1, last_loss, 0.0)
        s = cap_ref[i] + loss + ws
        u = jnp.where(i == levels - 1, 0.0, conductance(k_here, k_next))
        r = rcp(s + u)
        w = u * r
        w_ref[i] = w
        r_ref[i] = r
        yr_ref[i] = y * r
        return (w * s, y * w, k_next)

    loop(levels, forward, (zero, zero + 1.0, k_ref[0]))

    def backward(i, carry):
        left, right, pack_l, pack_r = carry
        w = w_ref[i]
        left = yr_ref[i] + w * left
        right = jnp.where(i == levels - 1, r_ref[i], w * right)
        left_ref[i] = left
        return (left, right, lane_edge_of(left, i, pack_l), lane_edge_of(right, i, pack_r))

    left, _, pack_ref[2], pack_ref[3] = loop(levels, backward, (zero, zero, tile, tile), reverse=True)
    g_ref[0] = left + 0.5 * rcp(k_ref[0])
    g_ref[1] = yr_ref[levels - 1]
    g_ref[2] = r_ref[levels - 1] + 0.5 * rcp(k_ref[levels - 1])


def assemble_halo(a_ref, b_ref, kh_ref, th_ref, qh_ref, pack_ref):
    is_even = even("plane")
    levels, _, width = kh_ref.shape
    row = lax.broadcasted_iota(jnp.int32, (SUB, width), 0)
    a_rows = [row == jnp.where(is_even, j, SUB - 1 - j) for j in (0, 1)]
    b_rows = [row == jnp.where(is_even, SUB - 1 - j, j) for j in (0, 1)]

    def level(i, carry):
        pack_t, pack_k = carry
        halos = []
        for first, ref in ((0, th_ref), (2, kh_ref), (4, qh_ref)):
            halo = jnp.zeros((SUB, width), F32)
            for source, rows in ((a_ref, a_rows), (b_ref, b_rows)):
                for j in (0, 1):
                    halo = jnp.where(rows[j], source[first + j, pl.ds(i, 1), :], halo)
            ref[i] = halo
            halos.append(halo)
        return (lane_edge_of(halos[0], i, pack_t), lane_edge_of(halos[1], i, pack_k))

    zero = jnp.zeros((SUB, LANES), F32)
    pack_ref[0], pack_ref[1] = loop(levels, level, (zero, zero))


def first_side(p, t, k, w, r, left, th, kh, qh, gx_in, gx_ref, gxh, gyh, caph, wh, rh, yrh, lefth, z, zh, send, pack_ref):
    levels, x, width = t.shape
    row = lax.broadcasted_iota(jnp.int32, (SUB, width), 0)
    lane = lax.broadcasted_iota(jnp.int32, (SUB, width), 1)
    first_loss, last_loss = end_losses()

    def forward(i, carry):
        ws, yy, wy, k_here, wy_main, bf = carry
        k_next = kh[jnp.minimum(i + 1, levels - 1)]
        cap = cap_by_k(k_here)
        caph[i] = cap
        loss = jnp.where(i == 0, first_loss, 0.0) + jnp.where(i == levels - 1, last_loss, 0.0)
        s = cap + loss + ws
        u = jnp.where(i == levels - 1, 0.0, conductance(k_here, k_next))
        rr = rcp(s + u)
        ww = u * rr
        wh[i] = ww
        rh[i] = rr
        yrh[i] = yy * rr

        temp, t_main, k_main = th[i], t[i], k[i]
        gx = conductance(k_here, jnp.where(row == SUB - 1, k_main[0:1], pltpu.roll(k_here, SUB - 1, 0)), lat_unit)
        gxh[i] = gx
        fx = gx * (jnp.where(row == SUB - 1, t_main[0:1], pltpu.roll(temp, SUB - 1, 0)) - temp)
        g_top = conductance(k_main[x - SUB :], pltpu.roll(k_here, SUB - 1, 0), lat_unit)
        gx_ref[i, x - 1 : x, :] = g_top[SUB - 1 :]
        f_top = g_top * (pltpu.roll(temp, SUB - 1, 0) - t_main[x - SUB :])
        gy = conductance(k_here, pltpu.roll(k_here, width - 1, 1), lat_unit)
        gy = jnp.where(lane == width - 1, 0.0, gy)
        gyh[i] = gy
        fy = gy * (pltpu.roll(temp, width - 1, 1) - temp)
        f_low = pltpu.roll(fx, 1, 0)
        lateral = fx - jnp.where(row == 0, pltpu.roll(f_top, 1, 0), f_low) + fy - pltpu.roll(fy, 1, 1)
        y = cap * temp + qh[i] + lateral + wy
        zh[i] = y * rr

        rhs = p[i]
        parts = [rhs[j : j + SUB] for j in range(0, x, SUB)]
        parts[0] = parts[0] - jnp.where(row == 0, f_low, 0.0)
        parts[-1] = parts[-1] + jnp.where(row == SUB - 1, f_top, 0.0)
        rhs = jnp.concatenate(parts, axis=0)
        y_main = rhs + wy_main
        z[i] = y_main * r[i]
        return (ww * s, yy * ww, ww * y, k_next, w[i] * y_main, bf + left[i] * rhs)

    zero, zero_main = jnp.zeros((SUB, width), F32), jnp.zeros((x, width), F32)
    *_, bf = loop(levels, forward, (zero, zero + 1.0, zero, kh[0], zero_main, zero_main), unroll=8)

    def backward(i, carry):
        ll, right, value, pack_l, pack_r = carry
        ww = wh[i]
        ll = yrh[i] + ww * ll
        right = jnp.where(i == levels - 1, rh[i], ww * right)
        lefth[i] = ll
        return (ll, right, zh[i] + ww * value, lane_edge_of(ll, i, pack_l), lane_edge_of(right, i, pack_r))

    tile = jnp.zeros((SUB, LANES), F32)
    ll, _, bfh, pack_ref[0], pack_ref[1] = loop(levels, backward, (zero, zero, zero, tile, tile), reverse=True)
    for j in range(0, x, SUB):
        send[j // SUB] = bf[j : j + SUB]
        send[(x + j) // SUB] = z[levels - 1, j : j + SUB, :]
    send[2 * x // SUB] = packed(bfh, zh[levels - 1])
    half = [0.5 * rcp(jnp.maximum(kh[i], 1e-3)) for i in (0, levels - 1)]
    send[2 * x // SUB + 1] = packed(ll + half[0], yrh[levels - 1])
    send[2 * x // SUB + 2] = packed(rh[levels - 1] + half[1], rh[levels - 1])


def both(main_ref, halo_ref, i):
    return jnp.concatenate([main_ref[i], halo_ref[i]], axis=0)


def right_side(last, *refs):
    t, th, q, qh, cap, caph, gx, gxh, gy, gyh, w, wh, r, rh, left, lefth, *out = refs
    levels, x, width = t.shape
    z, send = out[0], out[-1]
    rows = x if last else x + SUB

    def pick(main_ref, halo_ref, i):
        return main_ref[i] if last else both(main_ref, halo_ref, i)

    def level(i, carry):
        wy, bf = carry
        temp = both(t, th, i)
        here = temp[:rows]
        fy = pick(gy, gyh, i) * (pltpu.roll(here, width - 1, 1) - here)
        fx = both(gx, gxh, i) * (pltpu.roll(temp, x + SUB - 1, 0) - temp)
        lateral = (fx - pltpu.roll(fx, 1, 0))[:rows] + fy - pltpu.roll(fy, 1, 1)
        rhs = pick(cap, caph, i) * here + pick(q, qh, i) + lateral
        y = rhs + wy
        zz = y * pick(r, rh, i)
        z[i] = zz[:x]
        if not last:
            out[1][i] = zz[x:]
        return (pick(w, wh, i) * y, bf + pick(left, lefth, i) * rhs)

    zero = jnp.zeros((rows, width), F32)
    _, bf = loop(levels, level, (zero, zero), unroll=16 if last else 8)
    parts = [bf, pick(z, None if last else out[1], levels - 1)]
    groups = [part[j : j + SUB] for part in parts for j in range(0, x, SUB)]
    if not last:
        groups.append(packed(*[part[x:] for part in parts]))
    for j, group in enumerate(groups):
        send[j] = group


def edge_flow(first, x, rows, *refs):
    raw, pack, packh, packh_lr, other, otherh, *refs = refs
    own_k, other_k = (jnp.concatenate([a[1], b[1]], axis=0)[:rows] for a, b in ((pack, packh), (other, otherh)))
    if first:
        own_t, other_t = (jnp.concatenate([a[0], b[0]], axis=0)[:rows] for a, b in ((pack, packh), (other, otherh)))
    else:
        own_t, other_t = refs[0][:rows], refs[1][:rows]
    flow_ref, send = refs[-2:]
    flow = conductance(own_k, other_k, lat_unit) * (other_t - own_t)
    flow_ref[...] = flow
    at_low = lax.axis_index("phys") == 1
    lane = lax.broadcasted_iota(jnp.int32, flow.shape, 1)
    changes = []
    for j in (0, 1):
        response = jnp.concatenate([pack[2 + j], packh_lr[j]], axis=0)[:rows]
        change = jnp.sum(flow * response, axis=1, keepdims=True)
        changes.append(jnp.where(lane == jnp.where(at_low, 0, LANES - 1), change, 0.0))
    groups = [change[j : j + SUB] for change in changes for j in range(0, x, SUB)]
    if rows > x:
        groups.append(packed(*[change[x:] for change in changes]))
    for j in range(send.shape[0]):
        send[j] = add_at_edge(raw[j], groups[j]) if j < len(groups) else raw[j]


def fix_sweep(flow, *refs):
    half = (len(refs) - 0) // 4
    w, r, z_in, z = (refs[j * half : (j + 1) * half] for j in range(4))
    levels, x, width = z[0].shape
    start = pl.multiple_of(jnp.where(lax.axis_index("phys") == 1, 0, width - LANES), LANES)
    tile = pl.ds(start, LANES)

    def pick(pair, i):
        return jnp.concatenate([ref[i, :, tile] for ref in pair], axis=0)

    def level(i, wy):
        y = lane_unedge(flow[...], i) + wy
        value = pick(z_in, i) + pick(r, i) * y
        z[0][i, :, tile] = value[:x]
        if half > 1:
            z[1][i, :, tile] = value[x:]
        return pick(w, i) * y

    loop(levels, level, jnp.zeros(flow.shape, F32))


def packed(a, b):
    row = lax.broadcasted_iota(jnp.int32, a.shape, 0)
    return jnp.where((row >= 2) & (row < 6), pltpu.roll(b, 4, 0), a)


def block_flows(g_sets, h_sets, b_sets, x, rows):
    place, count = lax.axis_index("stack"), lax.axis_size("stack")

    def at(sets, block, read):
        value = read(sets[0])
        for j in range(1, count):
            value = jnp.where((place ^ j) == block, read(sets[j]), value)
        return value

    def ends(block):
        group = at(b_sets, block, lambda ref: ref[0 : 2 * x // SUB])
        group = group.reshape(2, x, group.shape[-1])
        if rows == x:
            return (group[0], group[1])
        tail = at(b_sets, block, lambda ref: ref[2 * x // SUB])
        return (
            jnp.concatenate([group[0], tail], axis=0),
            jnp.concatenate([group[1], pltpu.roll(tail, 4, 0)], axis=0),
        )

    def responses(block):
        group = at(g_sets, block, lambda ref: ref[0:3])
        if rows == x:
            return group
        tail = at(h_sets, block, lambda ref: ref[2 * x // SUB + 1 : 2 * x // SUB + 3])
        tails = (tail[0], pltpu.roll(tail[0], 4, 0), tail[1])
        return [jnp.concatenate([group[j], tails[j]], axis=0) for j in range(3)]

    end = [ends(block) for block in range(count)]
    g = [responses(block) for block in range(count)]
    ups, flows = [], []
    for j in range(count - 1):
        pivot = g[j][2] + g[j + 1][0]
        value = end[j + 1][0] - end[j][1]
        if j:
            pivot = pivot - g[j][1] * ups[j - 1]
            value = value + g[j][1] * flows[j - 1]
        inverse = rcp(pivot)
        ups.append(g[j + 1][1] * inverse)
        flows.append(value * inverse)
    for j in reversed(range(count - 2)):
        flows[j] = flows[j] + ups[j] * flows[j + 1]
    top = jnp.zeros_like(flows[0])
    bottom = top
    for j in range(count - 1):
        top = jnp.where(place == j + 1, -flows[j], top)
        bottom = jnp.where(place == j, flows[j], bottom)
    return top, bottom


def beside(edge, flow, k_edge, code_beside):
    return edge + flow * (0.5 * rcp(k_edge) + 0.5 * rcp(by_code(code_beside, k_table)))


def layers_beside(za, zb):
    is_even = even("stack")
    sides = []
    for j in (0, 1):
        value = [jnp.where(is_even, (zb, za)[j][3 + e], (za, zb)[j][3 + e]) for e in range(5)]
        value[4] = jnp.maximum(value[4], 0.1)
        sides.append(value)
    return sides


def rate_by_flag(active):
    return jnp.where(active, F32(0.5 * creep_rate * inv_e), F32(0.0))


def column_solve(count, first, *refs):
    g_sets, h_sets, refs = refs[:count], refs[count : 2 * count], refs[2 * count :]
    b_sets = h_sets
    if not first:
        b_sets, refs = refs[:count], refs[count:]
    z, zh, w, wh, r, rh, yr, yrh, t, th, pack_ref, flow_ref = refs
    levels, x, width = z.shape
    rows = x + SUB
    top, bottom = block_flows(g_sets, h_sets, b_sets, x, rows)
    flow_ref[0], flow_ref[1] = top[:x], bottom[:x]

    def level(i, carry):
        add, pack = carry
        value = both(z, zh, i) + top * both(yr, yrh, i) + add
        t[i] = value[:x]
        th[i] = value[x:]
        pack = lane_edge_of(value, i, pack)
        return (both(w, wh, jnp.maximum(i - 1, 0)) * value, pack)

    init = (bottom * both(r, rh, levels - 1), jnp.zeros((rows, LANES), F32))
    _, pack_ref[...] = loop(levels, level, init, reverse=True)


def prepare_creep(code_ref, flag_ref, mod, exp, rate):
    def level(i, carry):
        code = code_ref[i]
        mod[i] = by_code(code, mod_table)
        exp[i] = by_code(code, expand_table)
        rate[i] = rate_by_flag(flag_ref[i] == 1)
        return carry

    loop(code_ref.shape[0], level, 0)


def creep_cells(temp, mod, exp, rate, dist, creep, hard):
    elastic = dist - exp * temp
    drive = jnp.exp2((0.5 * log2e) * mod * (elastic - creep) * rcp(hard))
    drive = drive - rcp(drive)
    size = jnp.abs(drive)
    rate = rate * jnp.exp2(-log2e * rcp(jnp.exp2((0.5 * log2e) * temp + 1.0) + 1.0))
    gap = 1.0 - hard * jnp.exp2(-0.1 * jnp.log2(1.0 + size) - 0.9)
    gap_size = jnp.abs(gap)
    root = gap_size * lax.rsqrt(jnp.maximum(gap_size, 1e-30))
    creep = creep + rate * drive
    hard = hard + gap * root * (rate * size)
    return (elastic, creep, hard)


def creep_beside(t, flow, k, za, zb, state):
    ends, results = (0, t.shape[0] - 1), []
    for j, (code, flag, dist, creep, hard) in enumerate(layers_beside(za, zb)):
        if state is not None:
            creep, hard = state[j], state[2 + j]
        temp = beside(t[ends[j]], flow[j], k[ends[j]], code)
        mod = by_code(code, mod_table)
        cells = creep_cells(temp, mod, by_code(code, expand_table), rate_by_flag(flag == 1.0), dist, creep, hard)
        results.append((*cells, mod))
    return results


def creep_step(first, *refs):
    main, refs = refs[:7], refs[7:]
    flow, k, za, zb = refs[:4]
    state, out = (None, refs[4:]) if first else (refs[4], refs[5:])

    def level(i, carry):
        _, out[0][i], out[1][i] = creep_cells(*[ref[i] for ref in main])
        return carry

    loop(main[0].shape[0], level, 0, unroll=8)
    for j, (_, creep, hard, _) in enumerate(creep_beside(main[0], flow, k, za, zb, state)):
        out[2][j] = creep
        out[2][2 + j] = hard


def solve_and_creep(count, *refs):
    g_sets, b_sets, refs = refs[:count], refs[count : 2 * count], refs[2 * count :]
    z, w, r, yr, k, za, zb, state = refs[:8]
    mod, exp, rate, dist, creep, hard = refs[8:14]
    t, creep_out, hard_out, s, zs, xa, xb, pack_ref = refs[14:]
    levels, x, width = z.shape
    top, bottom = block_flows(g_sets, None, b_sets, x, x)

    def level(i, carry):
        add, pack = carry
        value = z[i] + top * yr[i] + add
        t[i] = value
        m = mod[i]
        elastic, new, hard_out[i] = creep_cells(value, m, exp[i], rate[i], dist[i], creep[i], hard[i])
        creep_out[i] = new
        stress = m * (elastic - new)
        s[i] = stress
        pack = lane_edge_of(stress, i, pack)
        return (w[jnp.maximum(i - 1, 0)] * value, pack)

    init = (bottom * r[levels - 1], jnp.zeros((x, LANES), F32))
    _, pack_ref[...] = loop(levels, level, init, unroll=8, reverse=True)
    place = lax.axis_index("stack")
    for j, (elastic, new, _, m) in enumerate(creep_beside(t, (top, bottom), k, za, zb, state)):
        zs[j] = jnp.where(place == (0, count - 1)[j], 0.0, m * (elastic - new))
    is_even = even("plane")
    upper, lower = s[:, x - 1, :], s[:, 0, :]
    xa[...] = jnp.where(is_even, upper, lower)
    xb[...] = jnp.where(is_even, lower, upper)


def balance_inside(s, zs, t, creep, hard, t_out, creep_out, hard_out, inside, sem):
    copies = [
        pltpu.make_async_copy(held, out, sem.at[j])
        for j, (held, out) in enumerate(((t, t_out), (creep, creep_out), (hard, hard_out)))
    ]
    for copy in copies:
        copy.start()
    levels, x, width = s.shape
    row = lax.broadcasted_iota(jnp.int32, (x, width), 0)
    lane = lax.broadcasted_iota(jnp.int32, (x, width), 1)

    def level(i, before):
        here = s[i]
        after = jnp.where(i == levels - 1, zs[1], s[jnp.minimum(i + 1, levels - 1)])
        total = before + after - 6.0 * here
        total = total + jnp.where(row == 0, 0.0, pltpu.roll(here, 1, 0))
        total = total + jnp.where(row == x - 1, 0.0, pltpu.roll(here, x - 1, 0))
        total = total + jnp.where(lane == 0, 0.0, pltpu.roll(here, 1, 1))
        inside[i] = total + jnp.where(lane == width - 1, 0.0, pltpu.roll(here, width - 1, 1))
        return here

    loop(levels, level, zs[0])
    for copy in copies:
        copy.wait()


def balance_edges(inside, xa, xb, other, out, held, sem):
    levels, x, width = inside.shape
    is_even = even("plane")
    row = lax.broadcasted_iota(jnp.int32, (x, width), 0)
    a_row = row == jnp.where(is_even, x - 1, 0)
    b_row = row == jnp.where(is_even, 0, x - 1)
    chunks = sem.shape[0]
    part = levels // chunks
    copies = []
    for chunk in range(chunks):

        def level(j, carry, chunk=chunk):
            i = chunk * part + j
            total = inside[i] + jnp.where(a_row, xa[pl.ds(i, 1), :], 0.0)
            total = total + jnp.where(b_row, xb[pl.ds(i, 1), :], 0.0)
            held[i] = add_at_edge(total, lane_unedge(other[...], i))
            return carry

        loop(part, level, 0)
        place = pl.ds(chunk * part, part)
        copies.append(pltpu.make_async_copy(held.at[place], out.at[place], sem.at[chunk]))
        copies[-1].start()
    for copy in copies:
        copy.wait()


def per_device(temp, source, code, flag, distortion, creep, hard):
    levels, x, width = temp.shape
    count = lax.axis_size("stack")
    if lax.axis_size("phys") != 2 or count != 4 or levels > LANES or x % SUB or width % LANES:
        raise ValueError("unsupported sizes")
    main, halo, layers = (levels, x, width), (levels, SUB, width), (2, x, width)
    cells = levels * x * width
    swap = [(0, 1), (1, 0)]
    plane_swaps = pair_swaps("plane")
    peers = [[(i, i ^ j) for i in range(count)] for j in range(1, count)]
    dma = pltpu.SemaphoreType.DMA

    edge = (6, levels, width)
    rows_a, rows_b = call(
        edge_rows,
        (temp, code, source),
        [edge] * 2,
        "edge_rows",
        cells,
        [pltpu.VMEM(edge, F32), pltpu.VMEM(edge, jnp.int32), pltpu.VMEM(edge, F32), dma((3, 6))],
        in_hbm=3,
        vmem=60,
    )
    rows_a = lax.ppermute(rows_a, "plane", plane_swaps[0])
    rows_b = lax.ppermute(rows_b, "plane", plane_swaps[1])
    gx, gy, part, pack, k, cap, w, r, yr, left, g = call(
        factor_main,
        (code, temp, source),
        [main] * 3 + [(4, x, LANES)] + [main] * 6 + [(3, x, width)],
        "factor_main",
        60 * cells,
    )
    za, zb = call(edge_layers, (code, flag, distortion, creep, hard, g), [(8, x, width)] * 2, "edge_layers", cells)
    za, g_two, zb = lax.ppermute(za, "stack", peers[0]), lax.ppermute(g, "stack", peers[1]), lax.ppermute(zb, "stack", peers[2])
    g_sets = [g, za, g_two, zb]
    other_pack = lax.ppermute(pack[:2], "phys", swap)

    kh, th, qh, packh = call(
        assemble_halo, (rows_a, rows_b), [halo] * 3 + [(2, SUB, LANES)], "assemble_halo", cells
    )
    other_packh = lax.ppermute(packh, "phys", swap)
    rows = x + SUB
    groups = 2 * x // SUB
    gx, gxh, gyh, caph, wh, rh, yrh, lefth, z, zh, send, packh_lr = call(
        first_side,
        (part, temp, k, w, r, left, th, kh, qh, gx),
        [main] + [halo] * 7 + [main, halo, (groups + 3, SUB, width), (2, SUB, LANES)],
        "first_side",
        40 * cells,
        aliases={9: 0},
    )

    own = other = state = None
    for step in range(TSTEPS):
        first, last = step == 0, step == TSTEPS - 1
        if not first:
            ins = (temp, th, source, qh, cap, caph, gx, gxh, gy, gyh, w, wh, r, rh, left, lefth)
            send = (groups if last else groups + 1, SUB, width)
            z, *zh, send = call(
                functools.partial(right_side, last), ins, [main, send] if last else [main, halo, send], "right_side", 30 * cells
            )
            zh = zh[0] if zh else None
        flow_rows = x if last else rows
        lane_flow, send = call(
            functools.partial(edge_flow, first, x, flow_rows),
            [send, pack, packh, packh_lr, other_pack, other_packh] + ([] if first else [own, other]),
            [(flow_rows, LANES), send.shape],
            "edge_flow",
            cells // 8,
        )
        b_sets = [send] + [lax.ppermute(send, "stack", peer) for peer in peers]
        ins = [lane_flow, w, r, z] if last else [lane_flow, w, wh, r, rh, z, zh]
        fixed = call(
            fix_sweep, ins, [main] if last else [main, halo], "fix_sweep", cells, aliases={3: 0} if last else {5: 0, 6: 1}
        )
        z, zh = (fixed[0], None) if last else fixed
        if first:
            h_sets = b_sets
            mod, exp, rate = call(prepare_creep, (code, flag), [main] * 3, "prepare_creep", 10 * cells, after=(z,))
        else:
            creep, hard, state = call(
                functools.partial(creep_step, step == 1),
                [temp, mod, exp, rate, distortion, creep, hard, flow, k, za, zb] + ([] if step == 1 else [state]),
                [main] * 2 + [(4, x, width)],
                "creep_step",
                60 * cells,
            )
        if last:
            break
        temp, th, own, flow = call(
            functools.partial(column_solve, count, first),
            g_sets + h_sets + ([] if first else b_sets) + [z, zh, w, wh, r, rh, yr, yrh],
            [main, halo, (rows, LANES), layers],
            "column_solve",
            10 * cells,
            after=(rate,) if first else (creep,),
        )
        other = lax.ppermute(own, "phys", swap)

    temp, creep, hard, stress, zs, xa, xb, pack = call(
        functools.partial(solve_and_creep, count),
        g_sets + b_sets + [z, w, r, yr, k, za, zb, state, mod, exp, rate, distortion, creep, hard],
        [main] * 4 + [layers] + [(levels, width)] * 2 + [(x, LANES)],
        "solve_and_creep",
        70 * cells,
    )
    xa = lax.ppermute(xa, "plane", plane_swaps[0])
    xb = lax.ppermute(xb, "plane", plane_swaps[1])
    other = lax.ppermute(pack, "phys", swap)
    temp, creep, hard, inside = call(
        balance_inside, (stress, zs, temp, creep, hard), [main] * 4, "balance_inside", 20 * cells, [dma((3,))], out_hbm=3
    )
    (residual,) = call(
        balance_edges,
        (inside, xa, xb, other),
        [main],
        "balance_edges",
        10 * cells,
        [pltpu.VMEM(main, F32), dma((4,))],
        out_hbm=1,
    )
    return (temp, creep, hard, residual)


def solution(mesh):
    spec = P("stack", "plane", "phys")
    return jax.shard_map(per_device, mesh=mesh, in_specs=(spec,) * 7, out_specs=(spec,) * 4, check_vma=False)
```

```python
import functools

import jax
import jax.numpy as jnp
from jax import lax
from jax.experimental import pallas as pl
from jax.experimental.pallas import tpu as pltpu
from jax.sharding import PartitionSpec as P

TSTEPS = 3

k_table = (4.0, 0.6, 2.5, 1.2, 0.8)
cap_table = (1.6, 1.8, 1.7, 2.0, 1.9)
mod_table = (1.5, 0.6, 0.9, 1.2, 0.8)
expand_table = (0.1, 0.3, 0.25, 0.15, 0.2)
cap_unit = 0.0003
lat_unit = 1.2e-05
h_conv = 0.05
creep_rate = 0.05
log2e = 1.4426950408889634
inv_e = 0.36787944117144233

LANES = 128
SUB = 8
F32 = jnp.float32

U_FACTOR, U_SIDE, U_RIGHT, U_LAST, U_SOLVE, U_CREEP, U_FINAL, U_BACK = 8, 8, 16, 16, 64, 16, 16, 64


def loop(count, body, init, unroll=16, reverse=False):
    while count % unroll:
        unroll -= 1

    def group(step, carry):
        for j in range(unroll):
            place = step * unroll + j
            carry = body(count - 1 - place if reverse else place, carry)
        return carry

    return lax.fori_loop(0, count // unroll, group, init)


def rcp(x):
    return pl.reciprocal(x, approx=True)


def by_code(code, table, scale=1.0):
    result = jnp.full(code.shape, table[4] * scale, F32)
    for entry in range(4):
        result = jnp.where(code == entry, F32(table[entry] * scale), result)
    return result


def cap_by_k(k):
    result = jnp.full(k.shape, cap_unit * cap_table[4], F32)
    for entry in range(4):
        result = jnp.where(k == F32(k_table[entry]), F32(cap_unit * cap_table[entry]), result)
    return result


def conductance(p, q, scale=1.0):
    return (2.0 * scale) * p * q * rcp(jnp.maximum(p + q, 1e-6))


VMEM = pl.BlockSpec(memory_space=pltpu.VMEM)
HBM = pl.BlockSpec(memory_space=pltpu.HBM)
ANY = pl.BlockSpec(memory_space=pl.ANY)


def call(body, ins, outs, name, flops=0, scratch=(), after=(), in_hbm=0, out_hbm=0, aliases=None, vmem=16):
    n_in, n_after = len(ins), len(after)

    def kernel(*refs):
        body(*refs[:n_in], *refs[n_in + n_after :])

    outs = [o if isinstance(o, jax.ShapeDtypeStruct) else jax.ShapeDtypeStruct(o, F32) for o in outs]
    size = sum(a.size * 4 for a in list(ins) + outs)
    return pl.pallas_call(
        kernel if after else body,
        in_specs=[HBM] * in_hbm + [VMEM] * (n_in - in_hbm) + [ANY] * n_after,
        out_specs=[HBM] * out_hbm + [VMEM] * (len(outs) - out_hbm),
        out_shape=outs,
        scratch_shapes=list(scratch),
        input_output_aliases=aliases or {},
        compiler_params=pltpu.CompilerParams(vmem_limit_bytes=vmem * 2**20),
        cost_estimate=pl.CostEstimate(flops=flops, bytes_accessed=size, transcendentals=0),
        name=name,
    )(*ins, *after)


def pair_swaps(axis):
    count = lax.axis_size(axis)
    first = [(i, i + 1) for i in range(0, count - 1, 2)]
    second = [(i, i + 1) for i in range(1, count - 1, 2)]
    return [pairs + [(b, a) for a, b in pairs] for pairs in (first, second)]


def even(axis):
    return lax.rem(lax.axis_index(axis), 2) == 0


def edge_rows(t_in, code_in, q_in, a_ref, b_ref, made, t, code, sem_in, sem_out):
    x = t_in.shape[1]
    is_even = even("plane")
    reads, writes = [], []
    for j in range(2):
        at_top = is_even if j == 0 else ~is_even
        near, far, beyond = (jnp.where(at_top, x - 1 - d, d) for d in range(3))
        for entry, (source, row, held) in enumerate(
            (
                (code_in, near, code.at[j, 0]),
                (code_in, far, code.at[j, 1]),
                (code_in, beyond, code.at[j, 2]),
                (t_in, far, made.at[j, 1]),
                (t_in, beyond, t.at[j]),
                (q_in, far, made.at[j, 5]),
                (t_in, near, made.at[j, 0]),
                (q_in, near, made.at[j, 4]),
            )
        ):
            reads.append(pltpu.make_async_copy(source.at[:, row, :], held, sem_in.at[j, entry]))
    for copy in reads:
        copy.start()
    for j, out in enumerate((a_ref, b_ref)):
        for copy in reads[8 * j : 8 * j + 8]:
            copy.wait()
        made[j, 2] = by_code(code[j, 0], k_table)
        k2, k3 = by_code(code[j, 1], k_table), by_code(code[j, 2], k_table)
        made[j, 3] = k2
        made[j, 5] = made[j, 5] + conductance(k2, k3, lat_unit) * (t[j] - made[j, 1])
        writes.append(pltpu.make_async_copy(made.at[j], out, sem_out.at[j]))
        writes[-1].start()
    for copy in writes:
        copy.wait()


def edge_layers(code, flag, dist, creep, hard, g, a_ref, b_ref):
    last = code.shape[0] - 1
    is_even = even("stack")
    for j in range(3):
        a_ref[j] = g[j]
        b_ref[j] = g[j]
    for j, source in enumerate((code, flag, dist, creep, hard)):
        after, before = source[last].astype(F32), source[0].astype(F32)
        a_ref[3 + j] = jnp.where(is_even, after, before)
        b_ref[3 + j] = jnp.where(is_even, before, after)


def end_losses():
    place, count = lax.axis_index("stack"), lax.axis_size("stack")
    return (jnp.where(place == 0, F32(h_conv), F32(0.0)), jnp.where(place == count - 1, F32(h_conv), F32(0.0)))


def lane_edge(tile_pair, i, pack):
    low, high = tile_pair
    at_low = lax.axis_index("phys") == 1
    edge = jnp.where(at_low, low, high)
    shift = jnp.where(at_low, i, lax.rem(i + 1, LANES))
    lane = lax.broadcasted_iota(jnp.int32, edge.shape, 1)
    return jnp.where(lane == i, pltpu.roll(edge, shift, 1), pack)


def lane_edge_of(value, i, pack):
    return lane_edge((value[:, :LANES], value[:, value.shape[1] - LANES :]), i, pack)


def lane_unedge(pack, i):
    at_low = lax.axis_index("phys") == 1
    shift = jnp.where(at_low, lax.rem(LANES - i, LANES), LANES - 1 - i)
    lane = lax.broadcasted_iota(jnp.int32, pack.shape, 1)
    return jnp.where(lane == jnp.where(at_low, 0, LANES - 1), pltpu.roll(pack, shift, 1), 0.0)


def add_at_edge(value, edge):
    at_low = lax.axis_index("phys") == 1
    tiles = [value[:, j : j + LANES] for j in range(0, value.shape[1], LANES)]
    tiles[0] = tiles[0] + jnp.where(at_low, edge, 0.0)
    tiles[-1] = tiles[-1] + jnp.where(at_low, 0.0, edge)
    return jnp.concatenate(tiles, axis=1)


def from_beside(t, g, axis):
    return g * pltpu.roll(t, t.shape[axis] - 1, axis) + pltpu.roll(g * t, 1, axis)


def lateral_main(k_ref, t_ref, q_ref, gx_ref, gy_ref, diag_ref, p_ref):
    levels, x, width = t_ref.shape
    row = lax.broadcasted_iota(jnp.int32, (x, width), 0)
    lane = lax.broadcasted_iota(jnp.int32, (x, width), 1)

    def level(i, carry):
        k, t = k_ref[i], t_ref[i]
        gx = conductance(k, pltpu.roll(k, x - 1, 0), lat_unit)
        gx = jnp.where(row == x - 1, 0.0, gx)
        gx_ref[i] = gx
        gy = conductance(k, pltpu.roll(k, width - 1, 1), lat_unit)
        gy = jnp.where(lane == width - 1, 0.0, gy)
        gy_ref[i] = gy
        diag = cap_by_k(k) - gx - pltpu.roll(gx, 1, 0) - gy - pltpu.roll(gy, 1, 1)
        diag_ref[i] = diag
        p_ref[i] = diag * t + q_ref[i] + from_beside(t, gx, 0) + from_beside(t, gy, 1)
        return carry

    loop(levels, level, 0, unroll=U_FACTOR)


def factor_main(code_ref, t_ref, pack_ref, k_ref, w_ref, r_ref, yr_ref, left_ref, g_ref):
    levels, x, width = t_ref.shape
    first_loss, last_loss = end_losses()

    def tables(i, carry):
        pack_t, pack_k = carry
        k = by_code(code_ref[i], k_table)
        k_ref[i] = k
        loss = jnp.where(i == 0, first_loss, 0.0) + jnp.where(i == levels - 1, last_loss, 0.0)
        r_ref[i] = by_code(code_ref[i], cap_table, cap_unit) + loss
        return (lane_edge_of(t_ref[i], i, pack_t), lane_edge_of(k, i, pack_k))

    tile = jnp.zeros((x, LANES), F32)
    pack_ref[0], pack_ref[1] = loop(levels, tables, (tile, tile))
    zero = jnp.zeros((x, width), F32)

    def forward(i, carry):
        ws, y, k_here = carry
        k_next = k_ref[jnp.minimum(i + 1, levels - 1)]
        s = r_ref[i] + ws
        u = jnp.where(i == levels - 1, 0.0, conductance(k_here, k_next))
        r = rcp(s + u)
        w = u * r
        w_ref[i] = w
        r_ref[i] = r
        yr_ref[i] = y * r
        return (w * s, y * w, k_next)

    loop(levels, forward, (zero, zero + 1.0, k_ref[0]))

    def backward(i, carry):
        left, right, pack_l, pack_r = carry
        w = w_ref[i]
        left = yr_ref[i] + w * left
        right = jnp.where(i == levels - 1, r_ref[i], w * right)
        left_ref[i] = left
        return (left, right, lane_edge_of(left, i, pack_l), lane_edge_of(right, i, pack_r))

    left, _, pack_ref[2], pack_ref[3] = loop(levels, backward, (zero, zero, tile, tile), reverse=True)
    g_ref[0] = left + 0.5 * rcp(k_ref[0])
    g_ref[1] = yr_ref[levels - 1]
    g_ref[2] = r_ref[levels - 1] + 0.5 * rcp(k_ref[levels - 1])


def assemble_halo(a_ref, b_ref, kh_ref, th_ref, qh_ref, pack_ref):
    is_even = even("plane")
    levels, _, width = kh_ref.shape
    row = lax.broadcasted_iota(jnp.int32, (SUB, width), 0)
    a_rows = [row == jnp.where(is_even, j, SUB - 1 - j) for j in (0, 1)]
    b_rows = [row == jnp.where(is_even, SUB - 1 - j, j) for j in (0, 1)]

    def level(i, carry):
        pack_t, pack_k = carry
        halos = []
        for first, ref in ((0, th_ref), (2, kh_ref), (4, qh_ref)):
            halo = jnp.zeros((SUB, width), F32)
            for source, rows in ((a_ref, a_rows), (b_ref, b_rows)):
                for j in (0, 1):
                    halo = jnp.where(rows[j], source[first + j, pl.ds(i, 1), :], halo)
            ref[i] = halo
            halos.append(halo)
        return (lane_edge_of(halos[0], i, pack_t), lane_edge_of(halos[1], i, pack_k))

    zero = jnp.zeros((SUB, LANES), F32)
    pack_ref[0], pack_ref[1] = loop(levels, level, (zero, zero), unroll=64)


def first_side(p, t, k, w, r, left, th, kh, qh, gxh, gyh, diagh, wh, rh, yrh, lefth, z, zh, send, pack_ref):
    levels, x, width = t.shape
    row = lax.broadcasted_iota(jnp.int32, (SUB, width), 0)
    lane = lax.broadcasted_iota(jnp.int32, (SUB, width), 1)
    first_loss, last_loss = end_losses()

    def forward(i, carry):
        ws, yy, wy, here, wy_main, bf = carry
        temp, t_main, k_main = th[i], t[i], k[i]
        k_next = kh[jnp.minimum(i + 1, levels - 1)]
        cap = cap_by_k(here)
        loss = jnp.where(i == 0, first_loss, 0.0) + jnp.where(i == levels - 1, last_loss, 0.0)
        s = cap + loss + ws
        u = jnp.where(i == levels - 1, 0.0, conductance(here, k_next))
        rr = rcp(s + u)
        ww = u * rr
        wh[i], rh[i], yrh[i] = ww, rr, yy * rr

        gx = conductance(here, jnp.where(row == SUB - 1, k_main[0:1], pltpu.roll(here, SUB - 1, 0)), lat_unit)
        g_low = conductance(here, jnp.where(row == 0, k_main[x - 1 :], pltpu.roll(here, 1, 0)), lat_unit)
        gy = conductance(here, pltpu.roll(here, width - 1, 1), lat_unit)
        gy = jnp.where(lane == width - 1, 0.0, gy)
        gxh[i], gyh[i] = gx, gy
        diag = cap - gx - g_low - gy - pltpu.roll(gy, 1, 1)
        diagh[i] = diag
        step_up = jnp.where(row == SUB - 1, t_main[0:1], pltpu.roll(temp, SUB - 1, 0))
        step_low = jnp.where(row == 0, t_main[x - 1 :], pltpu.roll(temp, 1, 0))
        y = diag * temp + qh[i] + gx * step_up + g_low * step_low + from_beside(temp, gy, 1) + wy
        zh[i] = y * rr
        to_first = pltpu.roll(gx * (temp - step_up), 1, 0)
        to_last = pltpu.roll(g_low * (temp - step_low), SUB - 1, 0)
        rhs = p[i]
        parts = [rhs[j : j + SUB] for j in range(0, x, SUB)]
        parts[0] = parts[0] + jnp.where(row == 0, to_first, 0.0)
        parts[-1] = parts[-1] + jnp.where(row == SUB - 1, to_last, 0.0)
        rhs = jnp.concatenate(parts, axis=0)
        y_main = rhs + wy_main
        z[i] = y_main * r[i]
        return (ww * s, yy * ww, ww * y, k_next, w[i] * y_main, bf + left[i] * rhs)

    zero, zero_main = jnp.zeros((SUB, width), F32), jnp.zeros((x, width), F32)
    *_, bf = loop(levels, forward, (zero, zero + 1.0, zero, kh[0], zero_main, zero_main), unroll=U_SIDE)

    def backward(i, carry):
        ll, right, value, pack_l, pack_r = carry
        ww = wh[i]
        ll = yrh[i] + ww * ll
        right = jnp.where(i == levels - 1, rh[i], ww * right)
        lefth[i] = ll
        return (ll, right, zh[i] + ww * value, lane_edge_of(ll, i, pack_l), lane_edge_of(right, i, pack_r))

    tile = jnp.zeros((SUB, LANES), F32)
    ll, _, bfh, pack_ref[0], pack_ref[1] = loop(levels, backward, (zero, zero, zero, tile, tile), unroll=U_BACK, reverse=True)
    for j in range(0, x, SUB):
        send[j // SUB] = bf[j : j + SUB]
        send[(x + j) // SUB] = z[levels - 1, j : j + SUB, :]
    send[2 * x // SUB] = packed(bfh, zh[levels - 1])
    half = [0.5 * rcp(jnp.maximum(kh[i], 1e-3)) for i in (0, levels - 1)]
    send[2 * x // SUB + 1] = packed(ll + half[0], yrh[levels - 1])
    send[2 * x // SUB + 2] = packed(rh[levels - 1] + half[1], rh[levels - 1])


def both(main_ref, halo_ref, i):
    return jnp.concatenate([main_ref[i], halo_ref[i]], axis=0)


def join_rows(gxh, k, kh, gx_in, diag_in, gx_ref, diag_ref):
    levels, x, _ = k.shape

    def level(i, carry):
        g_first = gxh[i, SUB - 1 : SUB, :]
        g_last = conductance(k[i, x - 1 : x, :], kh[i, 0:1, :], lat_unit)
        gx_ref[i, x - 1 : x, :] = g_last
        diag_ref[i, 0:1, :] = diag_in[i, 0:1, :] - g_first
        diag_ref[i, x - 1 : x, :] = diag_in[i, x - 1 : x, :] - g_last
        return carry

    loop(levels, level, 0, unroll=64)


def right_side(last, *refs):
    t, th, q, qh, diag, diagh, gx, gxh, gy, gyh, w, wh, r, rh, left, lefth, *out = refs
    levels, x, width = t.shape
    z, send = out[0], out[-1]
    rows = x if last else x + SUB

    def pick(main_ref, halo_ref, i):
        return main_ref[i] if last else both(main_ref, halo_ref, i)

    def level(i, carry):
        wy, bf = carry
        temp = both(t, th, i)
        here = temp[:rows]
        rhs = pick(diag, diagh, i) * here + pick(q, qh, i) + from_beside(temp, both(gx, gxh, i), 0)[:rows]
        rhs = rhs + from_beside(here, pick(gy, gyh, i), 1)
        y = rhs + wy
        zz = y * pick(r, rh, i)
        z[i] = zz[:x]
        if not last:
            out[1][i] = zz[x:]
        return (pick(w, wh, i) * y, bf + pick(left, lefth, i) * rhs)

    zero = jnp.zeros((rows, width), F32)
    _, bf = loop(levels, level, (zero, zero), unroll=U_LAST if last else U_RIGHT)
    parts = [bf, pick(z, None if last else out[1], levels - 1)]
    groups = [part[j : j + SUB] for part in parts for j in range(0, x, SUB)]
    if not last:
        groups.append(packed(*[part[x:] for part in parts]))
    for j, group in enumerate(groups):
        send[j] = group


def edge_flow(first, x, rows, *refs):
    raw, pack, packh, packh_lr, other, otherh, *refs = refs
    own_k, other_k = (jnp.concatenate([a[1], b[1]], axis=0)[:rows] for a, b in ((pack, packh), (other, otherh)))
    if first:
        own_t, other_t = (jnp.concatenate([a[0], b[0]], axis=0)[:rows] for a, b in ((pack, packh), (other, otherh)))
    else:
        own_t, other_t = refs[0][:rows], refs[1][:rows]
    flow_ref, send = refs[-2:]
    flow = conductance(own_k, other_k, lat_unit) * (other_t - own_t)
    flow_ref[...] = flow
    at_low = lax.axis_index("phys") == 1
    lane = lax.broadcasted_iota(jnp.int32, flow.shape, 1)
    changes = []
    for j in (0, 1):
        response = jnp.concatenate([pack[2 + j], packh_lr[j]], axis=0)[:rows]
        change = jnp.sum(flow * response, axis=1, keepdims=True)
        changes.append(jnp.where(lane == jnp.where(at_low, 0, LANES - 1), change, 0.0))
    groups = [change[j : j + SUB] for change in changes for j in range(0, x, SUB)]
    if rows > x:
        groups.append(packed(*[change[x:] for change in changes]))
    for j in range(send.shape[0]):
        send[j] = add_at_edge(raw[j], groups[j]) if j < len(groups) else raw[j]


def fix_sweep(flow, *refs):
    half = (len(refs) - 0) // 4
    w, r, z_in, z = (refs[j * half : (j + 1) * half] for j in range(4))
    levels, x, width = z[0].shape
    start = pl.multiple_of(jnp.where(lax.axis_index("phys") == 1, 0, width - LANES), LANES)
    tile = pl.ds(start, LANES)

    def pick(pair, i):
        return jnp.concatenate([ref[i, :, tile] for ref in pair], axis=0)

    def level(i, wy):
        y = lane_unedge(flow[...], i) + wy
        value = pick(z_in, i) + pick(r, i) * y
        z[0][i, :, tile] = value[:x]
        if half > 1:
            z[1][i, :, tile] = value[x:]
        return pick(w, i) * y

    loop(levels, level, jnp.zeros(flow.shape, F32), unroll=64)


def packed(a, b):
    row = lax.broadcasted_iota(jnp.int32, a.shape, 0)
    return jnp.where((row >= 2) & (row < 6), pltpu.roll(b, 4, 0), a)


def block_flows(g_sets, h_sets, b_sets, x, rows):
    place, count = lax.axis_index("stack"), lax.axis_size("stack")

    def at(sets, block, read):
        value = read(sets[0])
        for j in range(1, count):
            value = jnp.where((place ^ j) == block, read(sets[j]), value)
        return value

    def ends(block):
        group = at(b_sets, block, lambda ref: ref[0 : 2 * x // SUB])
        group = group.reshape(2, x, group.shape[-1])
        if rows == x:
            return (group[0], group[1])
        tail = at(b_sets, block, lambda ref: ref[2 * x // SUB])
        return (
            jnp.concatenate([group[0], tail], axis=0),
            jnp.concatenate([group[1], pltpu.roll(tail, 4, 0)], axis=0),
        )

    def responses(block):
        group = at(g_sets, block, lambda ref: ref[0:3])
        if rows == x:
            return group
        tail = at(h_sets, block, lambda ref: ref[2 * x // SUB + 1 : 2 * x // SUB + 3])
        tails = (tail[0], pltpu.roll(tail[0], 4, 0), tail[1])
        return [jnp.concatenate([group[j], tails[j]], axis=0) for j in range(3)]

    end = [ends(block) for block in range(count)]
    g = [responses(block) for block in range(count)]
    ups, flows = [], []
    for j in range(count - 1):
        pivot = g[j][2] + g[j + 1][0]
        value = end[j + 1][0] - end[j][1]
        if j:
            pivot = pivot - g[j][1] * ups[j - 1]
            value = value + g[j][1] * flows[j - 1]
        inverse = rcp(pivot)
        ups.append(g[j + 1][1] * inverse)
        flows.append(value * inverse)
    for j in reversed(range(count - 2)):
        flows[j] = flows[j] + ups[j] * flows[j + 1]
    top = jnp.zeros_like(flows[0])
    bottom = top
    for j in range(count - 1):
        top = jnp.where(place == j + 1, -flows[j], top)
        bottom = jnp.where(place == j, flows[j], bottom)
    return top, bottom


def beside(edge, flow, k_edge, code_beside):
    return edge + flow * (0.5 * rcp(k_edge) + 0.5 * rcp(by_code(code_beside, k_table)))


def layers_beside(za, zb):
    is_even = even("stack")
    sides = []
    for j in (0, 1):
        value = [jnp.where(is_even, (zb, za)[j][3 + e], (za, zb)[j][3 + e]) for e in range(5)]
        value[4] = jnp.maximum(value[4], 0.1)
        sides.append(value)
    return sides


def rate_by_flag(active):
    return jnp.where(active, F32(0.5 * creep_rate * inv_e), F32(0.0))


def column_solve(count, first, *refs):
    g_sets, h_sets, refs = refs[:count], refs[count : 2 * count], refs[2 * count :]
    b_sets = h_sets
    if not first:
        b_sets, refs = refs[:count], refs[count:]
    z, zh, w, wh, r, rh, yr, yrh, t, th, pack_ref, flow_ref = refs
    levels, x, width = z.shape
    rows = x + SUB
    top, bottom = block_flows(g_sets, h_sets, b_sets, x, rows)
    flow_ref[0], flow_ref[1] = top[:x], bottom[:x]

    def level(i, carry):
        add, pack = carry
        value = both(z, zh, i) + top * both(yr, yrh, i) + add
        t[i] = value[:x]
        th[i] = value[x:]
        pack = lane_edge_of(value, i, pack)
        return (both(w, wh, jnp.maximum(i - 1, 0)) * value, pack)

    init = (bottom * both(r, rh, levels - 1), jnp.zeros((rows, LANES), F32))
    _, pack_ref[...] = loop(levels, level, init, unroll=U_SOLVE, reverse=True)


def prepare_creep(code_ref, flag_ref, mod, exp, rate):
    def level(i, carry):
        code = code_ref[i]
        mod[i] = by_code(code, mod_table)
        exp[i] = by_code(code, expand_table)
        rate[i] = rate_by_flag(flag_ref[i] == 1)
        return carry

    loop(code_ref.shape[0], level, 0)


def creep_cells(temp, mod, exp, rate, dist, creep, hard):
    elastic = dist - exp * temp
    drive = jnp.exp2((0.5 * log2e) * mod * (elastic - creep) * rcp(hard))
    drive = drive - rcp(drive)
    size = jnp.abs(drive)
    rate = rate * jnp.exp2(-log2e * rcp(jnp.exp2((0.5 * log2e) * temp + 1.0) + 1.0))
    gap = 1.0 - hard * jnp.exp2(-0.1 * jnp.log2(1.0 + size) - 0.9)
    gap_size = jnp.abs(gap)
    root = gap_size * lax.rsqrt(jnp.maximum(gap_size, 1e-30))
    creep = creep + rate * drive
    hard = hard + gap * root * (rate * size)
    return (elastic, creep, hard)


def creep_beside(t, flow, k, za, zb, state):
    ends, results = (0, t.shape[0] - 1), []
    for j, (code, flag, dist, creep, hard) in enumerate(layers_beside(za, zb)):
        if state is not None:
            creep, hard = state[j], state[2 + j]
        temp = beside(t[ends[j]], flow[j], k[ends[j]], code)
        mod = by_code(code, mod_table)
        cells = creep_cells(temp, mod, by_code(code, expand_table), rate_by_flag(flag == 1.0), dist, creep, hard)
        results.append((*cells, mod))
    return results


def creep_step(first, *refs):
    main, refs = refs[:7], refs[7:]
    flow, k, za, zb = refs[:4]
    state, out = (None, refs[4:]) if first else (refs[4], refs[5:])

    def level(i, carry):
        _, out[0][i], out[1][i] = creep_cells(*[ref[i] for ref in main])
        return carry

    loop(main[0].shape[0], level, 0, unroll=U_CREEP)
    for j, (_, creep, hard, _) in enumerate(creep_beside(main[0], flow, k, za, zb, state)):
        out[2][j] = creep
        out[2][2 + j] = hard


def solve_and_creep(count, *refs):
    g_sets, b_sets, refs = refs[:count], refs[count : 2 * count], refs[2 * count :]
    z, w, r, yr, k, za, zb, state = refs[:8]
    mod, exp, rate, dist, creep, hard = refs[8:14]
    t, creep_out, hard_out, s, zs, xa, xb, pack_ref = refs[14:]
    levels, x, width = z.shape
    top, bottom = block_flows(g_sets, None, b_sets, x, x)

    def level(i, carry):
        add, pack = carry
        value = z[i] + top * yr[i] + add
        t[i] = value
        m = mod[i]
        elastic, new, hard_out[i] = creep_cells(value, m, exp[i], rate[i], dist[i], creep[i], hard[i])
        creep_out[i] = new
        stress = m * (elastic - new)
        s[i] = stress
        pack = lane_edge_of(stress, i, pack)
        return (w[jnp.maximum(i - 1, 0)] * value, pack)

    init = (bottom * r[levels - 1], jnp.zeros((x, LANES), F32))
    _, pack_ref[...] = loop(levels, level, init, unroll=U_FINAL, reverse=True)
    place = lax.axis_index("stack")
    for j, (elastic, new, _, m) in enumerate(creep_beside(t, (top, bottom), k, za, zb, state)):
        zs[j] = jnp.where(place == (0, count - 1)[j], 0.0, m * (elastic - new))
    is_even = even("plane")
    upper, lower = s[:, x - 1, :], s[:, 0, :]
    xa[...] = jnp.where(is_even, upper, lower)
    xb[...] = jnp.where(is_even, lower, upper)


def balance_inside(s, zs, t, creep, hard, t_out, creep_out, hard_out, inside, sem):
    copies = [
        pltpu.make_async_copy(held, out, sem.at[j])
        for j, (held, out) in enumerate(((t, t_out), (creep, creep_out), (hard, hard_out)))
    ]
    for copy in copies:
        copy.start()
    levels, x, width = s.shape
    row = lax.broadcasted_iota(jnp.int32, (x, width), 0)
    lane = lax.broadcasted_iota(jnp.int32, (x, width), 1)

    def level(i, before):
        here = s[i]
        after = jnp.where(i == levels - 1, zs[1], s[jnp.minimum(i + 1, levels - 1)])
        total = before + after - 6.0 * here
        total = total + jnp.where(row == 0, 0.0, pltpu.roll(here, 1, 0))
        total = total + jnp.where(row == x - 1, 0.0, pltpu.roll(here, x - 1, 0))
        total = total + jnp.where(lane == 0, 0.0, pltpu.roll(here, 1, 1))
        inside[i] = total + jnp.where(lane == width - 1, 0.0, pltpu.roll(here, width - 1, 1))
        return here

    loop(levels, level, zs[0])
    for copy in copies:
        copy.wait()


def balance_edges(inside, xa, xb, other, out, held, sem):
    levels, x, width = inside.shape
    is_even = even("plane")
    row = lax.broadcasted_iota(jnp.int32, (x, width), 0)
    a_row = row == jnp.where(is_even, x - 1, 0)
    b_row = row == jnp.where(is_even, 0, x - 1)
    chunks = sem.shape[0]
    part = levels // chunks
    copies = []
    for chunk in range(chunks):

        def level(j, carry, chunk=chunk):
            i = chunk * part + j
            total = inside[i] + jnp.where(a_row, xa[pl.ds(i, 1), :], 0.0)
            total = total + jnp.where(b_row, xb[pl.ds(i, 1), :], 0.0)
            held[i] = add_at_edge(total, lane_unedge(other[...], i))
            return carry

        loop(part, level, 0)
        place = pl.ds(chunk * part, part)
        copies.append(pltpu.make_async_copy(held.at[place], out.at[place], sem.at[chunk]))
        copies[-1].start()
    for copy in copies:
        copy.wait()


def per_device(temp, source, code, flag, distortion, creep, hard):
    levels, x, width = temp.shape
    count = lax.axis_size("stack")
    if lax.axis_size("phys") != 2 or count != 4 or levels > LANES or x % SUB or width % LANES:
        raise ValueError("unsupported sizes")
    main, halo, layers = (levels, x, width), (levels, SUB, width), (2, x, width)
    cells = levels * x * width
    swap = [(0, 1), (1, 0)]
    plane_swaps = pair_swaps("plane")
    peers = [[(i, i ^ j) for i in range(count)] for j in range(1, count)]
    dma = pltpu.SemaphoreType.DMA

    edge = (6, levels, width)
    rows_a, rows_b = call(
        edge_rows,
        (temp, code, source),
        [edge] * 2,
        "edge_rows",
        cells,
        [
            pltpu.VMEM((2, *edge), F32),
            pltpu.VMEM((2, levels, width), F32),
            pltpu.VMEM((2, 3, levels, width), jnp.int32),
            dma((2, 8)),
            dma((2,)),
        ],
        in_hbm=3,
        out_hbm=2,
        vmem=60,
    )
    rows_a = lax.ppermute(rows_a, "plane", plane_swaps[0])
    rows_b = lax.ppermute(rows_b, "plane", plane_swaps[1])
    pack, k, w, r, yr, left, g = call(
        factor_main, (code, temp), [(4, x, LANES)] + [main] * 5 + [(3, x, width)], "factor_main", 30 * cells
    )
    gx, gy, diag, part = call(lateral_main, (k, temp, source), [main] * 4, "lateral_main", 40 * cells)
    za, zb = call(edge_layers, (code, flag, distortion, creep, hard, g), [(8, x, width)] * 2, "edge_layers", cells, after=(part,))
    za, g_two, zb = lax.ppermute(za, "stack", peers[0]), lax.ppermute(g, "stack", peers[1]), lax.ppermute(zb, "stack", peers[2])
    g_sets = [g, za, g_two, zb]
    other_pack = lax.ppermute(pack[:2], "phys", swap)

    kh, th, qh, packh = call(
        assemble_halo, (rows_a, rows_b), [halo] * 3 + [(2, SUB, LANES)], "assemble_halo", cells, after=(part,)
    )
    other_packh = lax.ppermute(packh, "phys", swap)
    rows = x + SUB
    groups = 2 * x // SUB
    gxh, gyh, diagh, wh, rh, yrh, lefth, z, zh, send, packh_lr = call(
        first_side,
        (part, temp, k, w, r, left, th, kh, qh),
        [halo] * 7 + [main, halo, (groups + 3, SUB, width), (2, SUB, LANES)],
        "first_side",
        40 * cells,
    )

    own = other = state = None
    for step in range(TSTEPS):
        first, last = step == 0, step == TSTEPS - 1
        if not first:
            ins = (temp, th, source, qh, diag, diagh, gx, gxh, gy, gyh, w, wh, r, rh, left, lefth)
            send = (groups if last else groups + 1, SUB, width)
            z, *zh, send = call(
                functools.partial(right_side, last), ins, [main, send] if last else [main, halo, send], "right_side", 30 * cells
            )
            zh = zh[0] if zh else None
        flow_rows = x if last else rows
        lane_flow, send = call(
            functools.partial(edge_flow, first, x, flow_rows),
            [send, pack, packh, packh_lr, other_pack, other_packh] + ([] if first else [own, other]),
            [(flow_rows, LANES), send.shape],
            "edge_flow",
            cells // 8,
        )
        b_sets = [send] + [lax.ppermute(send, "stack", peer) for peer in peers]
        ins = [lane_flow, w, r, z] if last else [lane_flow, w, wh, r, rh, z, zh]
        fixed = call(
            fix_sweep, ins, [main] if last else [main, halo], "fix_sweep", cells, aliases={3: 0} if last else {5: 0, 6: 1}
        )
        z, zh = (fixed[0], None) if last else fixed
        if first:
            h_sets = b_sets
            mod, exp, rate = call(prepare_creep, (code, flag), [main] * 3, "prepare_creep", 10 * cells, after=(z,))
            gx, diag = call(join_rows, (gxh, k, kh, gx, diag), [main] * 2, "join_rows", cells, aliases={3: 0, 4: 1}, after=(rate,))
        else:
            creep, hard, state = call(
                functools.partial(creep_step, step == 1),
                [temp, mod, exp, rate, distortion, creep, hard, flow, k, za, zb] + ([] if step == 1 else [state]),
                [main] * 2 + [(4, x, width)],
                "creep_step",
                60 * cells,
            )
        if last:
            break
        temp, th, own, flow = call(
            functools.partial(column_solve, count, first),
            g_sets + h_sets + ([] if first else b_sets) + [z, zh, w, wh, r, rh, yr, yrh],
            [main, halo, (rows, LANES), layers],
            "column_solve",
            10 * cells,
            after=(rate, diag) if first else (creep,),
        )
        other = lax.ppermute(own, "phys", swap)

    temp, creep, hard, stress, zs, xa, xb, pack = call(
        functools.partial(solve_and_creep, count),
        g_sets + b_sets + [z, w, r, yr, k, za, zb, state, mod, exp, rate, distortion, creep, hard],
        [main] * 4 + [layers] + [(levels, width)] * 2 + [(x, LANES)],
        "solve_and_creep",
        70 * cells,
    )
    xa = lax.ppermute(xa, "plane", plane_swaps[0])
    xb = lax.ppermute(xb, "plane", plane_swaps[1])
    other = lax.ppermute(pack, "phys", swap)
    temp, creep, hard, inside = call(
        balance_inside, (stress, zs, temp, creep, hard), [main] * 4, "balance_inside", 20 * cells, [dma((3,))], out_hbm=3
    )
    (residual,) = call(
        balance_edges,
        (inside, xa, xb, other),
        [main],
        "balance_edges",
        10 * cells,
        [pltpu.VMEM(main, F32), dma((4,))],
        out_hbm=1,
    )
    return (temp, creep, hard, residual)


def solution(mesh):
    spec = P("stack", "plane", "phys")
    return jax.shard_map(per_device, mesh=mesh, in_specs=(spec,) * 7, out_specs=(spec,) * 4, check_vma=False)
```

```python
import functools

import jax
import jax.numpy as jnp
from jax import lax
from jax.experimental import pallas as pl
from jax.experimental.pallas import tpu as pltpu
from jax.sharding import PartitionSpec as P

TSTEPS = 3

k_table = (4.0, 0.6, 2.5, 1.2, 0.8)
cap_table = (1.6, 1.8, 1.7, 2.0, 1.9)
mod_table = (1.5, 0.6, 0.9, 1.2, 0.8)
expand_table = (0.1, 0.3, 0.25, 0.15, 0.2)
cap_unit = 0.0003
lat_unit = 1.2e-05
h_conv = 0.05
creep_rate = 0.05
log2e = 1.4426950408889634
inv_e = 0.36787944117144233

LANES = 128
SUB = 8
F32 = jnp.float32

U_FACTOR, U_SIDE, U_RIGHT, U_LAST, U_SOLVE, U_CREEP, U_FINAL, U_BACK = 8, 8, 16, 16, 64, 16, 16, 64


def loop(count, body, init, unroll=16, reverse=False):
    while count % unroll:
        unroll -= 1

    def group(step, carry):
        for j in range(unroll):
            place = step * unroll + j
            carry = body(count - 1 - place if reverse else place, carry)
        return carry

    return lax.fori_loop(0, count // unroll, group, init)


def rcp(x):
    return pl.reciprocal(x, approx=True)


def by_code(code, table, scale=1.0):
    result = jnp.full(code.shape, table[4] * scale, F32)
    for entry in range(4):
        result = jnp.where(code == entry, F32(table[entry] * scale), result)
    return result


def cap_by_k(k):
    result = jnp.full(k.shape, cap_unit * cap_table[4], F32)
    for entry in range(4):
        result = jnp.where(k == F32(k_table[entry]), F32(cap_unit * cap_table[entry]), result)
    return result


def conductance(p, q, scale=1.0):
    return (2.0 * scale) * p * q * rcp(jnp.maximum(p + q, 1e-6))


VMEM = pl.BlockSpec(memory_space=pltpu.VMEM)
HBM = pl.BlockSpec(memory_space=pltpu.HBM)
ANY = pl.BlockSpec(memory_space=pl.ANY)


def call(body, ins, outs, name, flops=0, scratch=(), after=(), in_hbm=0, out_hbm=0, aliases=None, vmem=16):
    n_in, n_after = len(ins), len(after)

    def kernel(*refs):
        body(*refs[:n_in], *refs[n_in + n_after :])

    outs = [o if isinstance(o, jax.ShapeDtypeStruct) else jax.ShapeDtypeStruct(o, F32) for o in outs]
    size = sum(a.size * 4 for a in list(ins) + outs)
    return pl.pallas_call(
        kernel if after else body,
        in_specs=[HBM] * in_hbm + [VMEM] * (n_in - in_hbm) + [ANY] * n_after,
        out_specs=[HBM] * out_hbm + [VMEM] * (len(outs) - out_hbm),
        out_shape=outs,
        scratch_shapes=list(scratch),
        input_output_aliases=aliases or {},
        compiler_params=pltpu.CompilerParams(vmem_limit_bytes=vmem * 2**20),
        cost_estimate=pl.CostEstimate(flops=flops, bytes_accessed=size, transcendentals=0),
        name=name,
    )(*ins, *after)


def plane_exchange(a, b):
    count, cores = lax.axis_size("plane"), lax.axis_size("phys")
    pairs = [(i, i + 1) for i in range(0, count - 1, 2)]
    a = lax.ppermute(a, "plane", pairs + [(j, i) for i, j in pairs])
    pairs = [(i * cores + f, (i + 1) * cores + f) for i in range(1, count - 1, 2) for f in range(cores)]
    pairs += [(i * cores, i * cores + 1) for i in (0, count - 1)]
    b = lax.ppermute(b, ("plane", "phys"), pairs + [(j, i) for i, j in pairs])
    return a, b


def has_b():
    place, count = lax.axis_index("plane"), lax.axis_size("plane")
    return (place > 0) & (place < count - 1)


def even(axis):
    return lax.rem(lax.axis_index(axis), 2) == 0


def edge_rows(t_in, code_in, q_in, a_ref, b_ref, made, t, code, sem_in, sem_out):
    x = t_in.shape[1]
    is_even = even("plane")
    reads, writes = [], []
    for j in range(2):
        at_top = is_even if j == 0 else ~is_even
        near, far, beyond = (jnp.where(at_top, x - 1 - d, d) for d in range(3))
        for entry, (source, row, held) in enumerate(
            (
                (code_in, near, code.at[j, 0]),
                (code_in, far, code.at[j, 1]),
                (code_in, beyond, code.at[j, 2]),
                (t_in, far, made.at[j, 1]),
                (t_in, beyond, t.at[j]),
                (q_in, far, made.at[j, 5]),
                (t_in, near, made.at[j, 0]),
                (q_in, near, made.at[j, 4]),
            )
        ):
            reads.append(pltpu.make_async_copy(source.at[:, row, :], held, sem_in.at[j, entry]))
    for copy in reads:
        copy.start()
    for j, out in enumerate((a_ref, b_ref)):
        for copy in reads[8 * j : 8 * j + 8]:
            copy.wait()
        made[j, 2] = by_code(code[j, 0], k_table)
        k2, k3 = by_code(code[j, 1], k_table), by_code(code[j, 2], k_table)
        made[j, 3] = k2
        made[j, 5] = made[j, 5] + conductance(k2, k3, lat_unit) * (t[j] - made[j, 1])
        writes.append(pltpu.make_async_copy(made.at[j], out, sem_out.at[j]))
        writes[-1].start()
    for copy in writes:
        copy.wait()


def edge_layers(code, flag, dist, creep, hard, g, a_ref, b_ref):
    last = code.shape[0] - 1
    is_even = even("stack")
    for j in range(3):
        a_ref[j] = g[j]
        b_ref[j] = g[j]
    for j, source in enumerate((code, flag, dist, creep, hard)):
        after, before = source[last].astype(F32), source[0].astype(F32)
        a_ref[3 + j] = jnp.where(is_even, after, before)
        b_ref[3 + j] = jnp.where(is_even, before, after)


def end_losses():
    place, count = lax.axis_index("stack"), lax.axis_size("stack")
    return (jnp.where(place == 0, F32(h_conv), F32(0.0)), jnp.where(place == count - 1, F32(h_conv), F32(0.0)))


def lane_edge(tile_pair, i, pack):
    low, high = tile_pair
    at_low = lax.axis_index("phys") == 1
    edge = jnp.where(at_low, low, high)
    shift = jnp.where(at_low, i, lax.rem(i + 1, LANES))
    lane = lax.broadcasted_iota(jnp.int32, edge.shape, 1)
    return jnp.where(lane == i, pltpu.roll(edge, shift, 1), pack)


def lane_edge_of(value, i, pack):
    return lane_edge((value[:, :LANES], value[:, value.shape[1] - LANES :]), i, pack)


def lane_unedge(pack, i):
    at_low = lax.axis_index("phys") == 1
    shift = jnp.where(at_low, lax.rem(LANES - i, LANES), LANES - 1 - i)
    lane = lax.broadcasted_iota(jnp.int32, pack.shape, 1)
    return jnp.where(lane == jnp.where(at_low, 0, LANES - 1), pltpu.roll(pack, shift, 1), 0.0)


def add_at_edge(value, edge):
    at_low = lax.axis_index("phys") == 1
    tiles = [value[:, j : j + LANES] for j in range(0, value.shape[1], LANES)]
    tiles[0] = tiles[0] + jnp.where(at_low, edge, 0.0)
    tiles[-1] = tiles[-1] + jnp.where(at_low, 0.0, edge)
    return jnp.concatenate(tiles, axis=1)


def from_beside(t, g, axis):
    return g * pltpu.roll(t, t.shape[axis] - 1, axis) + pltpu.roll(g * t, 1, axis)


def lateral_main(k_ref, t_ref, q_ref, gx_ref, gy_ref, diag_ref, p_ref):
    levels, x, width = t_ref.shape
    row = lax.broadcasted_iota(jnp.int32, (x, width), 0)
    lane = lax.broadcasted_iota(jnp.int32, (x, width), 1)

    def level(i, carry):
        k, t = k_ref[i], t_ref[i]
        gx = conductance(k, pltpu.roll(k, x - 1, 0), lat_unit)
        gx = jnp.where(row == x - 1, 0.0, gx)
        gx_ref[i] = gx
        gy = conductance(k, pltpu.roll(k, width - 1, 1), lat_unit)
        gy = jnp.where(lane == width - 1, 0.0, gy)
        gy_ref[i] = gy
        diag = cap_by_k(k) - gx - pltpu.roll(gx, 1, 0) - gy - pltpu.roll(gy, 1, 1)
        diag_ref[i] = diag
        p_ref[i] = diag * t + q_ref[i] + from_beside(t, gx, 0) + from_beside(t, gy, 1)
        return carry

    loop(levels, level, 0, unroll=U_FACTOR)


def factor_main(code_ref, t_ref, pack_ref, k_ref, w_ref, r_ref, yr_ref, left_ref, g_ref):
    levels, x, width = t_ref.shape
    first_loss, last_loss = end_losses()

    def tables(i, carry):
        pack_t, pack_k = carry
        k = by_code(code_ref[i], k_table)
        k_ref[i] = k
        loss = jnp.where(i == 0, first_loss, 0.0) + jnp.where(i == levels - 1, last_loss, 0.0)
        r_ref[i] = by_code(code_ref[i], cap_table, cap_unit) + loss
        return (lane_edge_of(t_ref[i], i, pack_t), lane_edge_of(k, i, pack_k))

    tile = jnp.zeros((x, LANES), F32)
    pack_ref[0], pack_ref[1] = loop(levels, tables, (tile, tile))
    zero = jnp.zeros((x, width), F32)

    def forward(i, carry):
        ws, y, k_here = carry
        k_next = k_ref[jnp.minimum(i + 1, levels - 1)]
        s = r_ref[i] + ws
        u = jnp.where(i == levels - 1, 0.0, conductance(k_here, k_next))
        r = rcp(s + u)
        w = u * r
        w_ref[i] = w
        r_ref[i] = r
        yr_ref[i] = y * r
        return (w * s, y * w, k_next)

    loop(levels, forward, (zero, zero + 1.0, k_ref[0]))

    def backward(i, carry):
        left, right, pack_l, pack_r = carry
        w = w_ref[i]
        left = yr_ref[i] + w * left
        right = jnp.where(i == levels - 1, r_ref[i], w * right)
        left_ref[i] = left
        return (left, right, lane_edge_of(left, i, pack_l), lane_edge_of(right, i, pack_r))

    left, _, pack_ref[2], pack_ref[3] = loop(levels, backward, (zero, zero, tile, tile), reverse=True)
    g_ref[0] = left + 0.5 * rcp(k_ref[0])
    g_ref[1] = yr_ref[levels - 1]
    g_ref[2] = r_ref[levels - 1] + 0.5 * rcp(k_ref[levels - 1])


def assemble_halo(a_ref, b_ref, kh_ref, th_ref, qh_ref, pack_ref):
    is_even = even("plane")
    levels, _, width = kh_ref.shape
    row = lax.broadcasted_iota(jnp.int32, (SUB, width), 0)
    a_rows = [row == jnp.where(is_even, j, SUB - 1 - j) for j in (0, 1)]
    b_rows = [(row == jnp.where(is_even, SUB - 1 - j, j)) & has_b() for j in (0, 1)]

    def level(i, carry):
        pack_t, pack_k = carry
        halos = []
        for first, ref in ((0, th_ref), (2, kh_ref), (4, qh_ref)):
            halo = jnp.zeros((SUB, width), F32)
            for source, rows in ((a_ref, a_rows), (b_ref, b_rows)):
                for j in (0, 1):
                    halo = jnp.where(rows[j], source[first + j, pl.ds(i, 1), :], halo)
            ref[i] = halo
            halos.append(halo)
        return (lane_edge_of(halos[0], i, pack_t), lane_edge_of(halos[1], i, pack_k))

    zero = jnp.zeros((SUB, LANES), F32)
    pack_ref[0], pack_ref[1] = loop(levels, level, (zero, zero), unroll=64)


def first_side(p, t, k, w, r, left, th, kh, qh, gxh, gyh, diagh, wh, rh, yrh, lefth, z, zh, send, pack_ref):
    levels, x, width = t.shape
    row = lax.broadcasted_iota(jnp.int32, (SUB, width), 0)
    lane = lax.broadcasted_iota(jnp.int32, (SUB, width), 1)
    first_loss, last_loss = end_losses()

    def forward(i, carry):
        ws, yy, wy, here, wy_main, bf = carry
        temp, t_main, k_main = th[i], t[i], k[i]
        k_next = kh[jnp.minimum(i + 1, levels - 1)]
        cap = cap_by_k(here)
        loss = jnp.where(i == 0, first_loss, 0.0) + jnp.where(i == levels - 1, last_loss, 0.0)
        s = cap + loss + ws
        u = jnp.where(i == levels - 1, 0.0, conductance(here, k_next))
        rr = rcp(s + u)
        ww = u * rr
        wh[i], rh[i], yrh[i] = ww, rr, yy * rr

        gx = conductance(here, jnp.where(row == SUB - 1, k_main[0:1], pltpu.roll(here, SUB - 1, 0)), lat_unit)
        g_low = conductance(here, jnp.where(row == 0, k_main[x - 1 :], pltpu.roll(here, 1, 0)), lat_unit)
        gy = conductance(here, pltpu.roll(here, width - 1, 1), lat_unit)
        gy = jnp.where(lane == width - 1, 0.0, gy)
        gxh[i], gyh[i] = gx, gy
        diag = cap - gx - g_low - gy - pltpu.roll(gy, 1, 1)
        diagh[i] = diag
        step_up = jnp.where(row == SUB - 1, t_main[0:1], pltpu.roll(temp, SUB - 1, 0))
        step_low = jnp.where(row == 0, t_main[x - 1 :], pltpu.roll(temp, 1, 0))
        y = diag * temp + qh[i] + gx * step_up + g_low * step_low + from_beside(temp, gy, 1) + wy
        zh[i] = y * rr
        to_first = pltpu.roll(gx * (temp - step_up), 1, 0)
        to_last = pltpu.roll(g_low * (temp - step_low), SUB - 1, 0)
        rhs = p[i]
        parts = [rhs[j : j + SUB] for j in range(0, x, SUB)]
        parts[0] = parts[0] + jnp.where(row == 0, to_first, 0.0)
        parts[-1] = parts[-1] + jnp.where(row == SUB - 1, to_last, 0.0)
        rhs = jnp.concatenate(parts, axis=0)
        y_main = rhs + wy_main
        z[i] = y_main * r[i]
        return (ww * s, yy * ww, ww * y, k_next, w[i] * y_main, bf + left[i] * rhs)

    zero, zero_main = jnp.zeros((SUB, width), F32), jnp.zeros((x, width), F32)
    *_, bf = loop(levels, forward, (zero, zero + 1.0, zero, kh[0], zero_main, zero_main), unroll=U_SIDE)

    def backward(i, carry):
        ll, right, value, pack_l, pack_r = carry
        ww = wh[i]
        ll = yrh[i] + ww * ll
        right = jnp.where(i == levels - 1, rh[i], ww * right)
        lefth[i] = ll
        return (ll, right, zh[i] + ww * value, lane_edge_of(ll, i, pack_l), lane_edge_of(right, i, pack_r))

    tile = jnp.zeros((SUB, LANES), F32)
    ll, _, bfh, pack_ref[0], pack_ref[1] = loop(levels, backward, (zero, zero, zero, tile, tile), unroll=U_BACK, reverse=True)
    for j in range(0, x, SUB):
        send[j // SUB] = bf[j : j + SUB]
        send[(x + j) // SUB] = z[levels - 1, j : j + SUB, :]
    send[2 * x // SUB] = packed(bfh, zh[levels - 1])
    half = [0.5 * rcp(jnp.maximum(kh[i], 1e-3)) for i in (0, levels - 1)]
    send[2 * x // SUB + 1] = packed(ll + half[0], yrh[levels - 1])
    send[2 * x // SUB + 2] = packed(rh[levels - 1] + half[1], rh[levels - 1])


def both(main_ref, halo_ref, i):
    return jnp.concatenate([main_ref[i], halo_ref[i]], axis=0)


def join_rows(gxh, k, kh, gx_in, diag_in, gx_ref, diag_ref):
    levels, x, _ = k.shape

    def level(i, carry):
        g_first = gxh[i, SUB - 1 : SUB, :]
        g_last = conductance(k[i, x - 1 : x, :], kh[i, 0:1, :], lat_unit)
        gx_ref[i, x - 1 : x, :] = g_last
        diag_ref[i, 0:1, :] = diag_in[i, 0:1, :] - g_first
        diag_ref[i, x - 1 : x, :] = diag_in[i, x - 1 : x, :] - g_last
        return carry

    loop(levels, level, 0, unroll=64)


def right_side(last, *refs):
    t, th, q, qh, diag, diagh, gx, gxh, gy, gyh, w, wh, r, rh, left, lefth, *out = refs
    levels, x, width = t.shape
    z, send = out[0], out[-1]
    rows = x if last else x + SUB

    def pick(main_ref, halo_ref, i):
        return main_ref[i] if last else both(main_ref, halo_ref, i)

    def level(i, carry):
        wy, bf = carry
        temp = both(t, th, i)
        here = temp[:rows]
        rhs = pick(diag, diagh, i) * here + pick(q, qh, i) + from_beside(temp, both(gx, gxh, i), 0)[:rows]
        rhs = rhs + from_beside(here, pick(gy, gyh, i), 1)
        y = rhs + wy
        zz = y * pick(r, rh, i)
        z[i] = zz[:x]
        if not last:
            out[1][i] = zz[x:]
        return (pick(w, wh, i) * y, bf + pick(left, lefth, i) * rhs)

    zero = jnp.zeros((rows, width), F32)
    _, bf = loop(levels, level, (zero, zero), unroll=U_LAST if last else U_RIGHT)
    parts = [bf, pick(z, None if last else out[1], levels - 1)]
    groups = [part[j : j + SUB] for part in parts for j in range(0, x, SUB)]
    if not last:
        groups.append(packed(*[part[x:] for part in parts]))
    for j, group in enumerate(groups):
        send[j] = group


def edge_flow(first, x, rows, *refs):
    raw, pack, packh, packh_lr, other, otherh, *refs = refs
    own_k, other_k = (jnp.concatenate([a[1], b[1]], axis=0)[:rows] for a, b in ((pack, packh), (other, otherh)))
    if first:
        own_t, other_t = (jnp.concatenate([a[0], b[0]], axis=0)[:rows] for a, b in ((pack, packh), (other, otherh)))
    else:
        own_t, other_t = refs[0][:rows], refs[1][:rows]
    flow_ref, send = refs[-2:]
    flow = conductance(own_k, other_k, lat_unit) * (other_t - own_t)
    flow_ref[...] = flow
    at_low = lax.axis_index("phys") == 1
    lane = lax.broadcasted_iota(jnp.int32, flow.shape, 1)
    changes = []
    for j in (0, 1):
        response = jnp.concatenate([pack[2 + j], packh_lr[j]], axis=0)[:rows]
        change = jnp.sum(flow * response, axis=1, keepdims=True)
        changes.append(jnp.where(lane == jnp.where(at_low, 0, LANES - 1), change, 0.0))
    groups = [change[j : j + SUB] for change in changes for j in range(0, x, SUB)]
    if rows > x:
        groups.append(packed(*[change[x:] for change in changes]))
    for j in range(send.shape[0]):
        send[j] = add_at_edge(raw[j], groups[j]) if j < len(groups) else raw[j]


def fix_sweep(flow, *refs):
    half = (len(refs) - 0) // 4
    w, r, z_in, z = (refs[j * half : (j + 1) * half] for j in range(4))
    levels, x, width = z[0].shape
    start = pl.multiple_of(jnp.where(lax.axis_index("phys") == 1, 0, width - LANES), LANES)
    tile = pl.ds(start, LANES)

    def pick(pair, i):
        return jnp.concatenate([ref[i, :, tile] for ref in pair], axis=0)

    def level(i, wy):
        y = lane_unedge(flow[...], i) + wy
        value = pick(z_in, i) + pick(r, i) * y
        z[0][i, :, tile] = value[:x]
        if half > 1:
            z[1][i, :, tile] = value[x:]
        return pick(w, i) * y

    loop(levels, level, jnp.zeros(flow.shape, F32), unroll=64)


def packed(a, b):
    row = lax.broadcasted_iota(jnp.int32, a.shape, 0)
    return jnp.where((row >= 2) & (row < 6), pltpu.roll(b, 4, 0), a)


def block_flows(g_sets, h_sets, b_sets, x, rows):
    place, count = lax.axis_index("stack"), lax.axis_size("stack")

    def at(sets, block, read):
        value = read(sets[0])
        for j in range(1, count):
            value = jnp.where((place ^ j) == block, read(sets[j]), value)
        return value

    def ends(block):
        group = at(b_sets, block, lambda ref: ref[0 : 2 * x // SUB])
        group = group.reshape(2, x, group.shape[-1])
        if rows == x:
            return (group[0], group[1])
        tail = at(b_sets, block, lambda ref: ref[2 * x // SUB])
        return (
            jnp.concatenate([group[0], tail], axis=0),
            jnp.concatenate([group[1], pltpu.roll(tail, 4, 0)], axis=0),
        )

    def responses(block):
        group = at(g_sets, block, lambda ref: ref[0:3])
        if rows == x:
            return group
        tail = at(h_sets, block, lambda ref: ref[2 * x // SUB + 1 : 2 * x // SUB + 3])
        tails = (tail[0], pltpu.roll(tail[0], 4, 0), tail[1])
        return [jnp.concatenate([group[j], tails[j]], axis=0) for j in range(3)]

    end = [ends(block) for block in range(count)]
    g = [responses(block) for block in range(count)]
    ups, flows = [], []
    for j in range(count - 1):
        pivot = g[j][2] + g[j + 1][0]
        value = end[j + 1][0] - end[j][1]
        if j:
            pivot = pivot - g[j][1] * ups[j - 1]
            value = value + g[j][1] * flows[j - 1]
        inverse = rcp(pivot)
        ups.append(g[j + 1][1] * inverse)
        flows.append(value * inverse)
    for j in reversed(range(count - 2)):
        flows[j] = flows[j] + ups[j] * flows[j + 1]
    top = jnp.zeros_like(flows[0])
    bottom = top
    for j in range(count - 1):
        top = jnp.where(place == j + 1, -flows[j], top)
        bottom = jnp.where(place == j, flows[j], bottom)
    return top, bottom


def beside(edge, flow, k_edge, code_beside):
    return edge + flow * (0.5 * rcp(k_edge) + 0.5 * rcp(by_code(code_beside, k_table)))


def layers_beside(za, zb):
    is_even = even("stack")
    sides = []
    for j in (0, 1):
        value = [jnp.where(is_even, (zb, za)[j][3 + e], (za, zb)[j][3 + e]) for e in range(5)]
        value[4] = jnp.maximum(value[4], 0.1)
        sides.append(value)
    return sides


def rate_by_flag(active):
    return jnp.where(active, F32(0.5 * creep_rate * inv_e), F32(0.0))


def column_solve(count, first, *refs):
    g_sets, h_sets, refs = refs[:count], refs[count : 2 * count], refs[2 * count :]
    b_sets = h_sets
    if not first:
        b_sets, refs = refs[:count], refs[count:]
    z, zh, w, wh, r, rh, yr, yrh, t, th, pack_ref, flow_ref = refs
    levels, x, width = z.shape
    rows = x + SUB
    top, bottom = block_flows(g_sets, h_sets, b_sets, x, rows)
    flow_ref[0], flow_ref[1] = top[:x], bottom[:x]

    def level(i, carry):
        add, pack = carry
        value = both(z, zh, i) + top * both(yr, yrh, i) + add
        t[i] = value[:x]
        th[i] = value[x:]
        pack = lane_edge_of(value, i, pack)
        return (both(w, wh, jnp.maximum(i - 1, 0)) * value, pack)

    init = (bottom * both(r, rh, levels - 1), jnp.zeros((rows, LANES), F32))
    _, pack_ref[...] = loop(levels, level, init, unroll=U_SOLVE, reverse=True)


def prepare_creep(code_ref, flag_ref, mod, exp, rate):
    def level(i, carry):
        code = code_ref[i]
        mod[i] = by_code(code, mod_table)
        exp[i] = by_code(code, expand_table)
        rate[i] = rate_by_flag(flag_ref[i] == 1)
        return carry

    loop(code_ref.shape[0], level, 0)


def creep_cells(temp, mod, exp, rate, dist, creep, hard):
    elastic = dist - exp * temp
    drive = jnp.exp2((0.5 * log2e) * mod * (elastic - creep) * rcp(hard))
    drive = drive - rcp(drive)
    size = jnp.abs(drive)
    rate = rate * jnp.exp2(-log2e * rcp(jnp.exp2((0.5 * log2e) * temp + 1.0) + 1.0))
    gap = 1.0 - hard * jnp.exp2(-0.1 * jnp.log2(1.0 + size) - 0.9)
    gap_size = jnp.abs(gap)
    root = gap_size * lax.rsqrt(jnp.maximum(gap_size, 1e-30))
    creep = creep + rate * drive
    hard = hard + gap * root * (rate * size)
    return (elastic, creep, hard)


def creep_beside(t, flow, k, za, zb, state):
    ends, results = (0, t.shape[0] - 1), []
    for j, (code, flag, dist, creep, hard) in enumerate(layers_beside(za, zb)):
        if state is not None:
            creep, hard = state[j], state[2 + j]
        temp = beside(t[ends[j]], flow[j], k[ends[j]], code)
        mod = by_code(code, mod_table)
        cells = creep_cells(temp, mod, by_code(code, expand_table), rate_by_flag(flag == 1.0), dist, creep, hard)
        results.append((*cells, mod))
    return results


def creep_step(first, *refs):
    main, refs = refs[:7], refs[7:]
    flow, k, za, zb = refs[:4]
    state, out = (None, refs[4:]) if first else (refs[4], refs[5:])

    def level(i, carry):
        _, out[0][i], out[1][i] = creep_cells(*[ref[i] for ref in main])
        return carry

    loop(main[0].shape[0], level, 0, unroll=U_CREEP)
    for j, (_, creep, hard, _) in enumerate(creep_beside(main[0], flow, k, za, zb, state)):
        out[2][j] = creep
        out[2][2 + j] = hard


def solve_and_creep(count, *refs):
    g_sets, b_sets, refs = refs[:count], refs[count : 2 * count], refs[2 * count :]
    z, w, r, yr, k, za, zb, state = refs[:8]
    mod, exp, rate, dist, creep, hard = refs[8:14]
    t, creep_out, hard_out, s, zs, xa, xb, pack_ref = refs[14:]
    levels, x, width = z.shape
    top, bottom = block_flows(g_sets, None, b_sets, x, x)

    def level(i, carry):
        add, pack = carry
        value = z[i] + top * yr[i] + add
        t[i] = value
        m = mod[i]
        elastic, new, hard_out[i] = creep_cells(value, m, exp[i], rate[i], dist[i], creep[i], hard[i])
        creep_out[i] = new
        stress = m * (elastic - new)
        s[i] = stress
        pack = lane_edge_of(stress, i, pack)
        return (w[jnp.maximum(i - 1, 0)] * value, pack)

    init = (bottom * r[levels - 1], jnp.zeros((x, LANES), F32))
    _, pack_ref[...] = loop(levels, level, init, unroll=U_FINAL, reverse=True)
    place = lax.axis_index("stack")
    for j, (elastic, new, _, m) in enumerate(creep_beside(t, (top, bottom), k, za, zb, state)):
        zs[j] = jnp.where(place == (0, count - 1)[j], 0.0, m * (elastic - new))
    is_even = even("plane")
    upper, lower = s[:, x - 1, :], s[:, 0, :]
    xa[...] = jnp.where(is_even, upper, lower)
    xb[...] = jnp.where(is_even, lower, upper)


def balance_inside(s, zs, t, creep, hard, t_out, creep_out, hard_out, inside, sem):
    copies = [
        pltpu.make_async_copy(held, out, sem.at[j])
        for j, (held, out) in enumerate(((t, t_out), (creep, creep_out), (hard, hard_out)))
    ]
    for copy in copies:
        copy.start()
    levels, x, width = s.shape
    row = lax.broadcasted_iota(jnp.int32, (x, width), 0)
    lane = lax.broadcasted_iota(jnp.int32, (x, width), 1)

    def level(i, before):
        here = s[i]
        after = jnp.where(i == levels - 1, zs[1], s[jnp.minimum(i + 1, levels - 1)])
        total = before + after - 6.0 * here
        total = total + jnp.where(row == 0, 0.0, pltpu.roll(here, 1, 0))
        total = total + jnp.where(row == x - 1, 0.0, pltpu.roll(here, x - 1, 0))
        total = total + jnp.where(lane == 0, 0.0, pltpu.roll(here, 1, 1))
        inside[i] = total + jnp.where(lane == width - 1, 0.0, pltpu.roll(here, width - 1, 1))
        return here

    loop(levels, level, zs[0])
    for copy in copies:
        copy.wait()


def balance_edges(inside, xa, xb, other, out, held, sem):
    levels, x, width = inside.shape
    is_even = even("plane")
    row = lax.broadcasted_iota(jnp.int32, (x, width), 0)
    a_row = row == jnp.where(is_even, x - 1, 0)
    b_row = (row == jnp.where(is_even, 0, x - 1)) & has_b()
    chunks = sem.shape[0]
    part = levels // chunks
    copies = []
    for chunk in range(chunks):

        def level(j, carry, chunk=chunk):
            i = chunk * part + j
            total = inside[i] + jnp.where(a_row, xa[pl.ds(i, 1), :], 0.0)
            total = total + jnp.where(b_row, xb[pl.ds(i, 1), :], 0.0)
            held[i] = add_at_edge(total, lane_unedge(other[...], i))
            return carry

        loop(part, level, 0)
        place = pl.ds(chunk * part, part)
        copies.append(pltpu.make_async_copy(held.at[place], out.at[place], sem.at[chunk]))
        copies[-1].start()
    for copy in copies:
        copy.wait()


def per_device(temp, source, code, flag, distortion, creep, hard):
    levels, x, width = temp.shape
    count = lax.axis_size("stack")
    if lax.axis_size("phys") != 2 or count != 4 or lax.axis_size("plane") % 2 or levels > LANES or x % SUB or width % LANES:
        raise ValueError("unsupported sizes")
    main, halo, layers = (levels, x, width), (levels, SUB, width), (2, x, width)
    cells = levels * x * width
    swap = [(0, 1), (1, 0)]
    peers = [[(i, i ^ j) for i in range(count)] for j in range(1, count)]
    dma = pltpu.SemaphoreType.DMA

    edge = (6, levels, width)
    rows_a, rows_b = call(
        edge_rows,
        (temp, code, source),
        [edge] * 2,
        "edge_rows",
        cells,
        [
            pltpu.VMEM((2, *edge), F32),
            pltpu.VMEM((2, levels, width), F32),
            pltpu.VMEM((2, 3, levels, width), jnp.int32),
            dma((2, 8)),
            dma((2,)),
        ],
        in_hbm=3,
        out_hbm=2,
        vmem=60,
    )
    rows_a, rows_b = plane_exchange(rows_a, rows_b)
    pack, k, w, r, yr, left, g = call(
        factor_main, (code, temp), [(4, x, LANES)] + [main] * 5 + [(3, x, width)], "factor_main", 30 * cells
    )
    gx, gy, diag, part = call(lateral_main, (k, temp, source), [main] * 4, "lateral_main", 40 * cells)
    za, zb = call(edge_layers, (code, flag, distortion, creep, hard, g), [(8, x, width)] * 2, "edge_layers", cells, after=(part,))
    za, g_two, zb = lax.ppermute(za, "stack", peers[0]), lax.ppermute(g, "stack", peers[1]), lax.ppermute(zb, "stack", peers[2])
    g_sets = [g, za, g_two, zb]
    other_pack = lax.ppermute(pack[:2], "phys", swap)

    kh, th, qh, packh = call(
        assemble_halo, (rows_a, rows_b), [halo] * 3 + [(2, SUB, LANES)], "assemble_halo", cells, after=(part,)
    )
    other_packh = lax.ppermute(packh, "phys", swap)
    rows = x + SUB
    groups = 2 * x // SUB
    gxh, gyh, diagh, wh, rh, yrh, lefth, z, zh, send, packh_lr = call(
        first_side,
        (part, temp, k, w, r, left, th, kh, qh),
        [halo] * 7 + [main, halo, (groups + 3, SUB, width), (2, SUB, LANES)],
        "first_side",
        40 * cells,
    )

    own = other = state = None
    for step in range(TSTEPS):
        first, last = step == 0, step == TSTEPS - 1
        if not first:
            ins = (temp, th, source, qh, diag, diagh, gx, gxh, gy, gyh, w, wh, r, rh, left, lefth)
            send = (groups if last else groups + 1, SUB, width)
            z, *zh, send = call(
                functools.partial(right_side, last), ins, [main, send] if last else [main, halo, send], "right_side", 30 * cells
            )
            zh = zh[0] if zh else None
        flow_rows = x if last else rows
        lane_flow, send = call(
            functools.partial(edge_flow, first, x, flow_rows),
            [send, pack, packh, packh_lr, other_pack, other_packh] + ([] if first else [own, other]),
            [(flow_rows, LANES), send.shape],
            "edge_flow",
            cells // 8,
        )
        b_sets = [send] + [lax.ppermute(send, "stack", peer) for peer in peers]
        ins = [lane_flow, w, r, z] if last else [lane_flow, w, wh, r, rh, z, zh]
        fixed = call(
            fix_sweep, ins, [main] if last else [main, halo], "fix_sweep", cells, aliases={3: 0} if last else {5: 0, 6: 1}
        )
        z, zh = (fixed[0], None) if last else fixed
        if first:
            h_sets = b_sets
            mod, exp, rate = call(prepare_creep, (code, flag), [main] * 3, "prepare_creep", 10 * cells, after=(z,))
            gx, diag = call(join_rows, (gxh, k, kh, gx, diag), [main] * 2, "join_rows", cells, aliases={3: 0, 4: 1}, after=(rate,))
        else:
            creep, hard, state = call(
                functools.partial(creep_step, step == 1),
                [temp, mod, exp, rate, distortion, creep, hard, flow, k, za, zb] + ([] if step == 1 else [state]),
                [main] * 2 + [(4, x, width)],
                "creep_step",
                60 * cells,
            )
        if last:
            break
        temp, th, own, flow = call(
            functools.partial(column_solve, count, first),
            g_sets + h_sets + ([] if first else b_sets) + [z, zh, w, wh, r, rh, yr, yrh],
            [main, halo, (rows, LANES), layers],
            "column_solve",
            10 * cells,
            after=(rate, diag) if first else (creep,),
        )
        other = lax.ppermute(own, "phys", swap)

    temp, creep, hard, stress, zs, xa, xb, pack = call(
        functools.partial(solve_and_creep, count),
        g_sets + b_sets + [z, w, r, yr, k, za, zb, state, mod, exp, rate, distortion, creep, hard],
        [main] * 4 + [layers] + [(levels, width)] * 2 + [(x, LANES)],
        "solve_and_creep",
        70 * cells,
    )
    xa, xb = plane_exchange(xa, xb)
    other = lax.ppermute(pack, "phys", swap)
    temp, creep, hard, inside = call(
        balance_inside, (stress, zs, temp, creep, hard), [main] * 4, "balance_inside", 20 * cells, [dma((3,))], out_hbm=3
    )
    (residual,) = call(
        balance_edges,
        (inside, xa, xb, other),
        [main],
        "balance_edges",
        10 * cells,
        [pltpu.VMEM(main, F32), dma((4,))],
        out_hbm=1,
    )
    return (temp, creep, hard, residual)


def solution(mesh):
    spec = P("stack", "plane", "phys")
    return jax.shard_map(per_device, mesh=mesh, in_specs=(spec,) * 7, out_specs=(spec,) * 4, check_vma=False)
```

```python
import functools

import jax
import jax.numpy as jnp
from jax import lax
from jax.experimental import pallas as pl
from jax.experimental.pallas import tpu as pltpu
from jax.sharding import PartitionSpec as P

TSTEPS = 3

k_table = (4.0, 0.6, 2.5, 1.2, 0.8)
cap_table = (1.6, 1.8, 1.7, 2.0, 1.9)
mod_table = (1.5, 0.6, 0.9, 1.2, 0.8)
expand_table = (0.1, 0.3, 0.25, 0.15, 0.2)
cap_unit = 0.0003
lat_unit = 1.2e-05
h_conv = 0.05
creep_rate = 0.05
log2e = 1.4426950408889634
inv_e = 0.36787944117144233

LANES = 128
SUB = 8
F32 = jnp.float32

U_FACTOR, U_SIDE, U_RIGHT, U_LAST, U_SOLVE, U_CREEP, U_FINAL, U_BACK, U_SWEEP = 8, 16, 64, 16, 64, 32, 64, 64, 64


def loop(count, body, init, unroll=16, reverse=False):
    while count % unroll:
        unroll -= 1

    def group(step, carry):
        for j in range(unroll):
            place = step * unroll + j
            carry = body(count - 1 - place if reverse else place, carry)
        return carry

    return lax.fori_loop(0, count // unroll, group, init)


def rcp(x):
    return pl.reciprocal(x, approx=True)


def by_code(code, table, scale=1.0):
    result = jnp.full(code.shape, table[4] * scale, F32)
    for entry in range(4):
        result = jnp.where(code == entry, F32(table[entry] * scale), result)
    return result


def cap_by_k(k):
    result = jnp.full(k.shape, cap_unit * cap_table[4], F32)
    for entry in range(4):
        result = jnp.where(k == F32(k_table[entry]), F32(cap_unit * cap_table[entry]), result)
    return result


def conductance(p, q, scale=1.0):
    return (2.0 * scale) * p * q * rcp(jnp.maximum(p + q, 1e-6))


VMEM = pl.BlockSpec(memory_space=pltpu.VMEM)
HBM = pl.BlockSpec(memory_space=pltpu.HBM)
ANY = pl.BlockSpec(memory_space=pl.ANY)


def call(body, ins, outs, name, flops=0, scratch=(), after=(), in_hbm=0, out_hbm=0, aliases=None, vmem=16):
    n_in, n_after = len(ins), len(after)

    def kernel(*refs):
        body(*refs[:n_in], *refs[n_in + n_after :])

    outs = [o if isinstance(o, jax.ShapeDtypeStruct) else jax.ShapeDtypeStruct(o, F32) for o in outs]
    size = sum(a.size * 4 for a in list(ins) + outs)
    return pl.pallas_call(
        kernel if after else body,
        in_specs=[HBM] * in_hbm + [VMEM] * (n_in - in_hbm) + [ANY] * n_after,
        out_specs=[HBM] * out_hbm + [VMEM] * (len(outs) - out_hbm),
        out_shape=outs,
        scratch_shapes=list(scratch),
        input_output_aliases=aliases or {},
        compiler_params=pltpu.CompilerParams(vmem_limit_bytes=vmem * 2**20),
        cost_estimate=pl.CostEstimate(flops=flops, bytes_accessed=size, transcendentals=0),
        name=name,
    )(*ins, *after)


def plane_exchange(a, b):
    count, cores = lax.axis_size("plane"), lax.axis_size("phys")
    pairs = [(i, i + 1) for i in range(0, count - 1, 2)]
    a = lax.ppermute(a, "plane", pairs + [(j, i) for i, j in pairs])
    pairs = [(i * cores + f, (i + 1) * cores + f) for i in range(1, count - 1, 2) for f in range(cores)]
    pairs += [(i * cores, i * cores + 1) for i in (0, count - 1)]
    b = lax.ppermute(b, ("plane", "phys"), pairs + [(j, i) for i, j in pairs])
    return a, b


def has_b():
    place, count = lax.axis_index("plane"), lax.axis_size("plane")
    return (place > 0) & (place < count - 1)


def even(axis):
    return lax.rem(lax.axis_index(axis), 2) == 0


def edge_rows(t_in, code_in, q_in, a_ref, b_ref, made, t, code, sem_in, sem_out):
    x = t_in.shape[1]
    is_even = even("plane")
    reads, writes = [], []
    for j in range(2):
        at_top = is_even if j == 0 else ~is_even
        near, far, beyond = (jnp.where(at_top, x - 1 - d, d) for d in range(3))
        for entry, (source, row, held) in enumerate(
            (
                (code_in, near, code.at[j, 0]),
                (code_in, far, code.at[j, 1]),
                (code_in, beyond, code.at[j, 2]),
                (t_in, far, made.at[j, 1]),
                (t_in, beyond, t.at[j]),
                (q_in, far, made.at[j, 5]),
                (t_in, near, made.at[j, 0]),
                (q_in, near, made.at[j, 4]),
            )
        ):
            reads.append(pltpu.make_async_copy(source.at[:, row, :], held, sem_in.at[j, entry]))
    for copy in reads:
        copy.start()
    for j, out in enumerate((a_ref, b_ref)):
        for copy in reads[8 * j : 8 * j + 8]:
            copy.wait()
        made[j, 2] = by_code(code[j, 0], k_table)
        k2, k3 = by_code(code[j, 1], k_table), by_code(code[j, 2], k_table)
        made[j, 3] = k2
        made[j, 5] = made[j, 5] + conductance(k2, k3, lat_unit) * (t[j] - made[j, 1])
        writes.append(pltpu.make_async_copy(made.at[j], out, sem_out.at[j]))
        writes[-1].start()
    for copy in writes:
        copy.wait()


def edge_layers(code, flag, dist, creep, hard, g, a_ref, b_ref):
    last = code.shape[0] - 1
    is_even = even("stack")
    for j in range(3):
        a_ref[j] = g[j]
        b_ref[j] = g[j]
    for j, source in enumerate((code, flag, dist, creep, hard)):
        after, before = source[last].astype(F32), source[0].astype(F32)
        a_ref[3 + j] = jnp.where(is_even, after, before)
        b_ref[3 + j] = jnp.where(is_even, before, after)


def end_losses():
    place, count = lax.axis_index("stack"), lax.axis_size("stack")
    return (jnp.where(place == 0, F32(h_conv), F32(0.0)), jnp.where(place == count - 1, F32(h_conv), F32(0.0)))


def lane_edge(tile_pair, i, pack):
    low, high = tile_pair
    at_low = lax.axis_index("phys") == 1
    edge = jnp.where(at_low, low, high)
    shift = jnp.where(at_low, i, lax.rem(i + 1, LANES))
    lane = lax.broadcasted_iota(jnp.int32, edge.shape, 1)
    return jnp.where(lane == i, pltpu.roll(edge, shift, 1), pack)


def lane_edge_of(value, i, pack):
    return lane_edge((value[:, :LANES], value[:, value.shape[1] - LANES :]), i, pack)


def lane_unedge(pack, i):
    at_low = lax.axis_index("phys") == 1
    shift = jnp.where(at_low, lax.rem(LANES - i, LANES), LANES - 1 - i)
    lane = lax.broadcasted_iota(jnp.int32, pack.shape, 1)
    return jnp.where(lane == jnp.where(at_low, 0, LANES - 1), pltpu.roll(pack, shift, 1), 0.0)


def add_at_edge(value, edge):
    at_low = lax.axis_index("phys") == 1
    tiles = [value[:, j : j + LANES] for j in range(0, value.shape[1], LANES)]
    tiles[0] = tiles[0] + jnp.where(at_low, edge, 0.0)
    tiles[-1] = tiles[-1] + jnp.where(at_low, 0.0, edge)
    return jnp.concatenate(tiles, axis=1)


def from_beside(t, g, axis):
    return g * pltpu.roll(t, t.shape[axis] - 1, axis) + pltpu.roll(g * t, 1, axis)


def lateral_main(k_ref, t_ref, q_ref, gx_ref, gy_ref, diag_ref, p_ref):
    levels, x, width = t_ref.shape
    row = lax.broadcasted_iota(jnp.int32, (x, width), 0)
    lane = lax.broadcasted_iota(jnp.int32, (x, width), 1)

    def level(i, carry):
        k, t = k_ref[i], t_ref[i]
        gx = conductance(k, pltpu.roll(k, x - 1, 0), lat_unit)
        gx = jnp.where(row == x - 1, 0.0, gx)
        gx_ref[i] = gx
        gy = conductance(k, pltpu.roll(k, width - 1, 1), lat_unit)
        gy = jnp.where(lane == width - 1, 0.0, gy)
        gy_ref[i] = gy
        diag = cap_by_k(k) - gx - pltpu.roll(gx, 1, 0) - gy - pltpu.roll(gy, 1, 1)
        diag_ref[i] = diag
        p_ref[i] = diag * t + q_ref[i] + from_beside(t, gx, 0) + from_beside(t, gy, 1)
        return carry

    loop(levels, level, 0, unroll=U_FACTOR)


def factor_main(code_ref, t_ref, pack_ref, k_ref, w_ref, r_ref, yr_ref, left_ref, right_ref, g_ref):
    levels, x, width = t_ref.shape
    first_loss, last_loss = end_losses()

    def tables(i, carry):
        pack_t, pack_k = carry
        k = by_code(code_ref[i], k_table)
        k_ref[i] = k
        loss = jnp.where(i == 0, first_loss, 0.0) + jnp.where(i == levels - 1, last_loss, 0.0)
        r_ref[i] = by_code(code_ref[i], cap_table, cap_unit) + loss
        return (lane_edge_of(t_ref[i], i, pack_t), lane_edge_of(k, i, pack_k))

    tile = jnp.zeros((x, LANES), F32)
    pack_ref[0], pack_ref[1] = loop(levels, tables, (tile, tile))
    zero = jnp.zeros((x, width), F32)

    def forward(i, carry):
        ws, y, k_here = carry
        k_next = k_ref[jnp.minimum(i + 1, levels - 1)]
        s = r_ref[i] + ws
        u = jnp.where(i == levels - 1, 0.0, conductance(k_here, k_next))
        r = rcp(s + u)
        w = u * r
        w_ref[i] = w
        r_ref[i] = r
        yr_ref[i] = y * r
        return (w * s, y * w, k_next)

    loop(levels, forward, (zero, zero + 1.0, k_ref[0]))

    def backward(i, carry):
        left, right, pack_l, pack_r = carry
        w = w_ref[i]
        left = yr_ref[i] + w * left
        right = jnp.where(i == levels - 1, r_ref[i], w * right)
        left_ref[i], right_ref[i] = left, right
        return (left, right, lane_edge_of(left, i, pack_l), lane_edge_of(right, i, pack_r))

    left, _, pack_ref[2], pack_ref[3] = loop(levels, backward, (zero, zero, tile, tile), reverse=True)
    g_ref[0] = left + 0.5 * rcp(k_ref[0])
    g_ref[1] = yr_ref[levels - 1]
    g_ref[2] = r_ref[levels - 1] + 0.5 * rcp(k_ref[levels - 1])


def assemble_halo(a_ref, b_ref, kh_ref, th_ref, qh_ref, pack_ref):
    is_even = even("plane")
    levels, _, width = kh_ref.shape
    row = lax.broadcasted_iota(jnp.int32, (SUB, width), 0)
    a_rows = [row == jnp.where(is_even, j, SUB - 1 - j) for j in (0, 1)]
    b_rows = [(row == jnp.where(is_even, SUB - 1 - j, j)) & has_b() for j in (0, 1)]

    def level(i, carry):
        pack_t, pack_k = carry
        halos = []
        for first, ref in ((0, th_ref), (2, kh_ref), (4, qh_ref)):
            halo = jnp.zeros((SUB, width), F32)
            for source, rows in ((a_ref, a_rows), (b_ref, b_rows)):
                for j in (0, 1):
                    halo = jnp.where(rows[j], source[first + j, pl.ds(i, 1), :], halo)
            ref[i] = halo
            halos.append(halo)
        return (lane_edge_of(halos[0], i, pack_t), lane_edge_of(halos[1], i, pack_k))

    zero = jnp.zeros((SUB, LANES), F32)
    pack_ref[0], pack_ref[1] = loop(levels, level, (zero, zero), unroll=64)


def first_side(p, t, k, left, right, th, kh, qh, gxh, gyh, diagh, wh, rh, yrh, lefth, righth, rhs_ref, rhsh, send, pack_ref):
    levels, x, width = t.shape
    row = lax.broadcasted_iota(jnp.int32, (SUB, width), 0)
    lane = lax.broadcasted_iota(jnp.int32, (SUB, width), 1)
    first_loss, last_loss = end_losses()

    def forward(i, carry):
        ws, yy, here, bf, bl = carry
        temp, t_main, k_main = th[i], t[i], k[i]
        k_next = kh[jnp.minimum(i + 1, levels - 1)]
        cap = cap_by_k(here)
        loss = jnp.where(i == 0, first_loss, 0.0) + jnp.where(i == levels - 1, last_loss, 0.0)
        s = cap + loss + ws
        u = jnp.where(i == levels - 1, 0.0, conductance(here, k_next))
        rr = rcp(s + u)
        ww = u * rr
        wh[i], rh[i], yrh[i] = ww, rr, yy * rr

        gx = conductance(here, jnp.where(row == SUB - 1, k_main[0:1], pltpu.roll(here, SUB - 1, 0)), lat_unit)
        g_low = conductance(here, jnp.where(row == 0, k_main[x - 1 :], pltpu.roll(here, 1, 0)), lat_unit)
        gy = conductance(here, pltpu.roll(here, width - 1, 1), lat_unit)
        gy = jnp.where(lane == width - 1, 0.0, gy)
        gxh[i], gyh[i] = gx, gy
        diag = cap - gx - g_low - gy - pltpu.roll(gy, 1, 1)
        diagh[i] = diag
        step_up = jnp.where(row == SUB - 1, t_main[0:1], pltpu.roll(temp, SUB - 1, 0))
        step_low = jnp.where(row == 0, t_main[x - 1 :], pltpu.roll(temp, 1, 0))
        rhsh[i] = diag * temp + qh[i] + gx * step_up + g_low * step_low + from_beside(temp, gy, 1)
        to_first = pltpu.roll(gx * (temp - step_up), 1, 0)
        to_last = pltpu.roll(g_low * (temp - step_low), SUB - 1, 0)
        rhs = p[i]
        parts = [rhs[j : j + SUB] for j in range(0, x, SUB)]
        parts[0] = parts[0] + jnp.where(row == 0, to_first, 0.0)
        parts[-1] = parts[-1] + jnp.where(row == SUB - 1, to_last, 0.0)
        rhs = jnp.concatenate(parts, axis=0)
        rhs_ref[i] = rhs
        return (ww * s, yy * ww, k_next, bf + left[i] * rhs, bl + right[i] * rhs)

    zero, zero_main = jnp.zeros((SUB, width), F32), jnp.zeros((x, width), F32)
    *_, bf, bl = loop(levels, forward, (zero, zero + 1.0, kh[0], zero_main, zero_main), unroll=U_SIDE)

    def backward(i, carry):
        ll, rr, bfh, blh, pack_l, pack_r = carry
        ww, rhs = wh[i], rhsh[i]
        ll = yrh[i] + ww * ll
        rr = jnp.where(i == levels - 1, rh[i], ww * rr)
        lefth[i], righth[i] = ll, rr
        return (ll, rr, bfh + ll * rhs, blh + rr * rhs, lane_edge_of(ll, i, pack_l), lane_edge_of(rr, i, pack_r))

    tile = jnp.zeros((SUB, LANES), F32)
    init = (zero, zero, zero, zero, tile, tile)
    ll, _, bfh, blh, pack_ref[0], pack_ref[1] = loop(levels, backward, init, unroll=U_BACK, reverse=True)
    for j in range(0, x, SUB):
        send[j // SUB] = bf[j : j + SUB]
        send[(x + j) // SUB] = bl[j : j + SUB]
    send[2 * x // SUB] = packed(bfh, blh)
    half = [0.5 * rcp(jnp.maximum(kh[i], 1e-3)) for i in (0, levels - 1)]
    send[2 * x // SUB + 1] = packed(ll + half[0], yrh[levels - 1])
    send[2 * x // SUB + 2] = packed(rh[levels - 1] + half[1], rh[levels - 1])


def both(main_ref, halo_ref, i):
    return jnp.concatenate([main_ref[i], halo_ref[i]], axis=0)


def join_rows(gxh, k, kh, gx_in, diag_in, gx_ref, diag_ref):
    levels, x, _ = k.shape

    def level(i, carry):
        g_first = gxh[i, SUB - 1 : SUB, :]
        g_last = conductance(k[i, x - 1 : x, :], kh[i, 0:1, :], lat_unit)
        gx_ref[i, x - 1 : x, :] = g_last
        diag_ref[i, 0:1, :] = diag_in[i, 0:1, :] - g_first
        diag_ref[i, x - 1 : x, :] = diag_in[i, x - 1 : x, :] - g_last
        return carry

    loop(levels, level, 0, unroll=64)


def right_side(last, *refs):
    t, th, q, qh, diag, diagh, gx, gxh, gy, gyh, left, lefth, right, righth, *out = refs
    levels, x, width = t.shape
    send = out[-1]
    rows = x if last else x + SUB

    def pick(main_ref, halo_ref, i):
        return main_ref[i] if last else both(main_ref, halo_ref, i)

    def level(i, carry):
        bf, bl = carry
        temp = both(t, th, i)
        here = temp[:rows]
        rhs = pick(diag, diagh, i) * here + pick(q, qh, i) + from_beside(temp, both(gx, gxh, i), 0)[:rows]
        rhs = rhs + from_beside(here, pick(gy, gyh, i), 1)
        out[0][i] = rhs[:x]
        if not last:
            out[1][i] = rhs[x:]
        return (bf + pick(left, lefth, i) * rhs, bl + pick(right, righth, i) * rhs)

    zero = jnp.zeros((rows, width), F32)
    parts = loop(levels, level, (zero, zero), unroll=U_LAST if last else U_RIGHT)
    groups = [part[j : j + SUB] for part in parts for j in range(0, x, SUB)]
    if not last:
        groups.append(packed(*[part[x:] for part in parts]))
    for j, group in enumerate(groups):
        send[j] = group


def edge_flow(first, x, rows, *refs):
    raw, pack, packh, packh_lr, other, otherh, *refs = refs
    own_k, other_k = (jnp.concatenate([a[1], b[1]], axis=0)[:rows] for a, b in ((pack, packh), (other, otherh)))
    if first:
        own_t, other_t = (jnp.concatenate([a[0], b[0]], axis=0)[:rows] for a, b in ((pack, packh), (other, otherh)))
    else:
        own_t, other_t = refs[0][:rows], refs[1][:rows]
    flow_ref, send = refs[-2:]
    flow = conductance(own_k, other_k, lat_unit) * (other_t - own_t)
    flow_ref[...] = flow
    at_low = lax.axis_index("phys") == 1
    lane = lax.broadcasted_iota(jnp.int32, flow.shape, 1)
    changes = []
    for j in (0, 1):
        response = jnp.concatenate([pack[2 + j], packh_lr[j]], axis=0)[:rows]
        change = jnp.sum(flow * response, axis=1, keepdims=True)
        changes.append(jnp.where(lane == jnp.where(at_low, 0, LANES - 1), change, 0.0))
    groups = [change[j : j + SUB] for change in changes for j in range(0, x, SUB)]
    if rows > x:
        groups.append(packed(*[change[x:] for change in changes]))
    for j in range(send.shape[0]):
        send[j] = add_at_edge(raw[j], groups[j]) if j < len(groups) else raw[j]


def forward_sweep(flow, *refs):
    count = len(refs) // 4
    w, r, rhs, z = (refs[j * count : (j + 1) * count] for j in range(4))
    levels, x, width = z[0].shape

    def pick(pair, i):
        return jnp.concatenate([ref[i] for ref in pair], axis=0)

    def level(i, wy):
        y = add_at_edge(pick(rhs, i) + wy, lane_unedge(flow[...], i))
        value = pick(r, i) * y
        z[0][i] = value[:x]
        if count > 1:
            z[1][i] = value[x:]
        return pick(w, i) * y

    loop(levels, level, jnp.zeros((flow.shape[0], width), F32), unroll=U_SWEEP)


def packed(a, b):
    row = lax.broadcasted_iota(jnp.int32, a.shape, 0)
    return jnp.where((row >= 2) & (row < 6), pltpu.roll(b, 4, 0), a)


def block_flows(g_sets, h_sets, b_sets, x, rows):
    place, count = lax.axis_index("stack"), lax.axis_size("stack")

    def at(sets, block, read):
        value = read(sets[0])
        for j in range(1, count):
            value = jnp.where((place ^ j) == block, read(sets[j]), value)
        return value

    def ends(block):
        group = at(b_sets, block, lambda ref: ref[0 : 2 * x // SUB])
        group = group.reshape(2, x, group.shape[-1])
        if rows == x:
            return (group[0], group[1])
        tail = at(b_sets, block, lambda ref: ref[2 * x // SUB])
        return (
            jnp.concatenate([group[0], tail], axis=0),
            jnp.concatenate([group[1], pltpu.roll(tail, 4, 0)], axis=0),
        )

    def responses(block):
        group = at(g_sets, block, lambda ref: ref[0:3])
        if rows == x:
            return group
        tail = at(h_sets, block, lambda ref: ref[2 * x // SUB + 1 : 2 * x // SUB + 3])
        tails = (tail[0], pltpu.roll(tail[0], 4, 0), tail[1])
        return [jnp.concatenate([group[j], tails[j]], axis=0) for j in range(3)]

    end = [ends(block) for block in range(count)]
    g = [responses(block) for block in range(count)]
    ups, flows = [], []
    for j in range(count - 1):
        pivot = g[j][2] + g[j + 1][0]
        value = end[j + 1][0] - end[j][1]
        if j:
            pivot = pivot - g[j][1] * ups[j - 1]
            value = value + g[j][1] * flows[j - 1]
        inverse = rcp(pivot)
        ups.append(g[j + 1][1] * inverse)
        flows.append(value * inverse)
    for j in reversed(range(count - 2)):
        flows[j] = flows[j] + ups[j] * flows[j + 1]
    top = jnp.zeros_like(flows[0])
    bottom = top
    for j in range(count - 1):
        top = jnp.where(place == j + 1, -flows[j], top)
        bottom = jnp.where(place == j, flows[j], bottom)
    return top, bottom


def beside(edge, flow, k_edge, code_beside):
    return edge + flow * (0.5 * rcp(k_edge) + 0.5 * rcp(by_code(code_beside, k_table)))


def layers_beside(za, zb):
    is_even = even("stack")
    sides = []
    for j in (0, 1):
        value = [jnp.where(is_even, (zb, za)[j][3 + e], (za, zb)[j][3 + e]) for e in range(5)]
        value[4] = jnp.maximum(value[4], 0.1)
        sides.append(value)
    return sides


def rate_by_flag(active):
    return jnp.where(active, F32(0.5 * creep_rate * inv_e), F32(0.0))


def column_solve(count, first, *refs):
    g_sets, h_sets, refs = refs[:count], refs[count : 2 * count], refs[2 * count :]
    b_sets = h_sets
    if not first:
        b_sets, refs = refs[:count], refs[count:]
    z, zh, w, wh, r, rh, yr, yrh, t, th, pack_ref, flow_ref = refs
    levels, x, width = z.shape
    rows = x + SUB
    top, bottom = block_flows(g_sets, h_sets, b_sets, x, rows)
    flow_ref[0], flow_ref[1] = top[:x], bottom[:x]

    def level(i, carry):
        add, pack = carry
        value = both(z, zh, i) + top * both(yr, yrh, i) + add
        t[i] = value[:x]
        th[i] = value[x:]
        pack = lane_edge_of(value, i, pack)
        return (both(w, wh, jnp.maximum(i - 1, 0)) * value, pack)

    init = (bottom * both(r, rh, levels - 1), jnp.zeros((rows, LANES), F32))
    _, pack_ref[...] = loop(levels, level, init, unroll=U_SOLVE, reverse=True)


def prepare_creep(code_ref, flag_ref, mod, exp, rate):
    def level(i, carry):
        code = code_ref[i]
        mod[i] = by_code(code, mod_table)
        exp[i] = by_code(code, expand_table)
        rate[i] = rate_by_flag(flag_ref[i] == 1)
        return carry

    loop(code_ref.shape[0], level, 0)


def creep_cells(temp, mod, exp, rate, dist, creep, hard):
    elastic = dist - exp * temp
    drive = jnp.exp2((0.5 * log2e) * mod * (elastic - creep) * rcp(hard))
    drive = drive - rcp(drive)
    size = jnp.abs(drive)
    rate = rate * jnp.exp2(-log2e * rcp(jnp.exp2((0.5 * log2e) * temp + 1.0) + 1.0))
    gap = 1.0 - hard * jnp.exp2(-0.1 * jnp.log2(1.0 + size) - 0.9)
    gap_size = jnp.abs(gap)
    root = gap_size * lax.rsqrt(jnp.maximum(gap_size, 1e-30))
    creep = creep + rate * drive
    hard = hard + gap * root * (rate * size)
    return (elastic, creep, hard)


def creep_beside(t, flow, k, za, zb, state):
    ends, results = (0, t.shape[0] - 1), []
    for j, (code, flag, dist, creep, hard) in enumerate(layers_beside(za, zb)):
        if state is not None:
            creep, hard = state[j], state[2 + j]
        temp = beside(t[ends[j]], flow[j], k[ends[j]], code)
        mod = by_code(code, mod_table)
        cells = creep_cells(temp, mod, by_code(code, expand_table), rate_by_flag(flag == 1.0), dist, creep, hard)
        results.append((*cells, mod))
    return results


def creep_step(first, *refs):
    main, refs = refs[:7], refs[7:]
    flow, k, za, zb = refs[:4]
    state, out = (None, refs[4:]) if first else (refs[4], refs[5:])

    def level(i, carry):
        _, out[0][i], out[1][i] = creep_cells(*[ref[i] for ref in main])
        return carry

    loop(main[0].shape[0], level, 0, unroll=U_CREEP)
    for j, (_, creep, hard, _) in enumerate(creep_beside(main[0], flow, k, za, zb, state)):
        out[2][j] = creep
        out[2][2 + j] = hard


def solve_and_creep(count, *refs):
    g_sets, b_sets, refs = refs[:count], refs[count : 2 * count], refs[2 * count :]
    z, w, r, yr, mod, exp, rate, dist, creep, hard = refs[:10]
    t, creep_out, hard_out, s, flow_ref, xa, xb, pack_ref = refs[10:]
    levels, x, width = z.shape
    top, bottom = block_flows(g_sets, None, b_sets, x, x)

    def level(i, carry):
        add, pack = carry
        value = z[i] + top * yr[i] + add
        t[i] = value
        m = mod[i]
        elastic, new, hard_out[i] = creep_cells(value, m, exp[i], rate[i], dist[i], creep[i], hard[i])
        creep_out[i] = new
        stress = m * (elastic - new)
        s[i] = stress
        pack = lane_edge_of(stress, i, pack)
        return (w[jnp.maximum(i - 1, 0)] * value, pack)

    init = (bottom * r[levels - 1], jnp.zeros((x, LANES), F32))
    _, pack_ref[...] = loop(levels, level, init, unroll=U_FINAL, reverse=True)
    flow_ref[0], flow_ref[1] = top, bottom
    is_even = even("plane")
    upper, lower = s[:, x - 1, :], s[:, 0, :]
    xa[...] = jnp.where(is_even, upper, lower)
    xb[...] = jnp.where(is_even, lower, upper)


def balance_inside(s, t, creep, hard, flow, k, za, zb, state, t_out, creep_out, hard_out, inside, sem):
    copies = [
        pltpu.make_async_copy(held, out, sem.at[j])
        for j, (held, out) in enumerate(((t, t_out), (creep, creep_out), (hard, hard_out)))
    ]
    for copy in copies:
        copy.start()
    levels, x, width = s.shape
    row = lax.broadcasted_iota(jnp.int32, (x, width), 0)
    lane = lax.broadcasted_iota(jnp.int32, (x, width), 1)
    place, count = lax.axis_index("stack"), lax.axis_size("stack")
    zs = [
        jnp.where(place == end, 0.0, m * (elastic - new))
        for end, (elastic, new, _, m) in zip((0, count - 1), creep_beside(t, flow, k, za, zb, state))
    ]

    def level(i, before):
        here = s[i]
        after = jnp.where(i == levels - 1, zs[1], s[jnp.minimum(i + 1, levels - 1)])
        total = before + after - 6.0 * here
        total = total + jnp.where(row == 0, 0.0, pltpu.roll(here, 1, 0))
        total = total + jnp.where(row == x - 1, 0.0, pltpu.roll(here, x - 1, 0))
        total = total + jnp.where(lane == 0, 0.0, pltpu.roll(here, 1, 1))
        inside[i] = total + jnp.where(lane == width - 1, 0.0, pltpu.roll(here, width - 1, 1))
        return here

    loop(levels, level, zs[0], unroll=8)
    for copy in copies:
        copy.wait()


def balance_edges(inside, xa, xb, other, out, held, sem):
    levels, x, width = inside.shape
    is_even = even("plane")
    row = lax.broadcasted_iota(jnp.int32, (x, width), 0)
    a_row = row == jnp.where(is_even, x - 1, 0)
    b_row = (row == jnp.where(is_even, 0, x - 1)) & has_b()
    chunks = sem.shape[0]
    part = levels // chunks
    copies = []
    for chunk in range(chunks):

        def level(j, carry, chunk=chunk):
            i = chunk * part + j
            total = inside[i] + jnp.where(a_row, xa[pl.ds(i, 1), :], 0.0)
            total = total + jnp.where(b_row, xb[pl.ds(i, 1), :], 0.0)
            held[i] = add_at_edge(total, lane_unedge(other[...], i))
            return carry

        loop(part, level, 0)
        place = pl.ds(chunk * part, part)
        copies.append(pltpu.make_async_copy(held.at[place], out.at[place], sem.at[chunk]))
        copies[-1].start()
    for copy in copies:
        copy.wait()


def per_device(temp, source, code, flag, distortion, creep, hard):
    levels, x, width = temp.shape
    count = lax.axis_size("stack")
    if lax.axis_size("phys") != 2 or count != 4 or lax.axis_size("plane") % 2 or levels > LANES or x % SUB or width % LANES:
        raise ValueError("unsupported sizes")
    main, halo, layers = (levels, x, width), (levels, SUB, width), (2, x, width)
    cells = levels * x * width
    swap = [(0, 1), (1, 0)]
    peers = [[(i, i ^ j) for i in range(count)] for j in range(1, count)]
    dma = pltpu.SemaphoreType.DMA

    edge = (6, levels, width)
    rows_a, rows_b = call(
        edge_rows,
        (temp, code, source),
        [edge] * 2,
        "edge_rows",
        cells,
        [
            pltpu.VMEM((2, *edge), F32),
            pltpu.VMEM((2, levels, width), F32),
            pltpu.VMEM((2, 3, levels, width), jnp.int32),
            dma((2, 8)),
            dma((2,)),
        ],
        in_hbm=3,
        out_hbm=2,
        vmem=60,
    )
    rows_a, rows_b = plane_exchange(rows_a, rows_b)
    pack, k, w, r, yr, left, right, g = call(
        factor_main, (code, temp), [(4, x, LANES)] + [main] * 6 + [(3, x, width)], "factor_main", 30 * cells
    )
    gx, gy, diag, part = call(lateral_main, (k, temp, source), [main] * 4, "lateral_main", 40 * cells)
    za, zb = call(edge_layers, (code, flag, distortion, creep, hard, g), [(8, x, width)] * 2, "edge_layers", cells, after=(part,))
    za, g_two, zb = lax.ppermute(za, "stack", peers[0]), lax.ppermute(g, "stack", peers[1]), lax.ppermute(zb, "stack", peers[2])
    g_sets = [g, za, g_two, zb]
    other_pack = lax.ppermute(pack[:2], "phys", swap)

    kh, th, qh, packh = call(
        assemble_halo, (rows_a, rows_b), [halo] * 3 + [(2, SUB, LANES)], "assemble_halo", cells, after=(part,)
    )
    other_packh = lax.ppermute(packh, "phys", swap)
    rows = x + SUB
    groups = 2 * x // SUB
    gxh, gyh, diagh, wh, rh, yrh, lefth, righth, rhs, rhsh, send, packh_lr = call(
        first_side,
        (part, temp, k, left, right, th, kh, qh),
        [halo] * 8 + [main, halo, (groups + 3, SUB, width), (2, SUB, LANES)],
        "first_side",
        40 * cells,
    )

    own = other = state = None
    for step in range(TSTEPS):
        first, last = step == 0, step == TSTEPS - 1
        if not first:
            ins = (temp, th, source, qh, diag, diagh, gx, gxh, gy, gyh, left, lefth, right, righth)
            send = (groups if last else groups + 1, SUB, width)
            rhs, *rhsh, send = call(
                functools.partial(right_side, last), ins, [main, send] if last else [main, halo, send], "right_side", 30 * cells
            )
            rhsh = rhsh[0] if rhsh else None
        flow_rows = x if last else rows
        lane_flow, send = call(
            functools.partial(edge_flow, first, x, flow_rows),
            [send, pack, packh, packh_lr, other_pack, other_packh] + ([] if first else [own, other]),
            [(flow_rows, LANES), send.shape],
            "edge_flow",
            cells // 8,
        )
        b_sets = [send] + [lax.ppermute(send, "stack", peer) for peer in peers]
        ins = [lane_flow, w, r, rhs] if last else [lane_flow, w, wh, r, rh, rhs, rhsh]
        z, *zh = call(
            forward_sweep, ins, [main] if last else [main, halo], "forward_sweep", cells, aliases={3: 0} if last else {5: 0, 6: 1}
        )
        zh = zh[0] if zh else None
        if first:
            h_sets = b_sets
            mod, exp, rate = call(prepare_creep, (code, flag), [main] * 3, "prepare_creep", 10 * cells, after=(z,))
            gx, diag = call(join_rows, (gxh, k, kh, gx, diag), [main] * 2, "join_rows", cells, aliases={3: 0, 4: 1}, after=(rate,))
        else:
            creep, hard, state = call(
                functools.partial(creep_step, step == 1),
                [temp, mod, exp, rate, distortion, creep, hard, flow, k, za, zb] + ([] if step == 1 else [state]),
                [main] * 2 + [(4, x, width)],
                "creep_step",
                60 * cells,
            )
        if last:
            break
        temp, th, own, flow = call(
            functools.partial(column_solve, count, first),
            g_sets + h_sets + ([] if first else b_sets) + [z, zh, w, wh, r, rh, yr, yrh],
            [main, halo, (rows, LANES), layers],
            "column_solve",
            10 * cells,
            after=(rate, diag) if first else (creep,),
        )
        other = lax.ppermute(own, "phys", swap)

    temp, creep, hard, stress, flow, xa, xb, pack = call(
        functools.partial(solve_and_creep, count),
        g_sets + b_sets + [z, w, r, yr, mod, exp, rate, distortion, creep, hard],
        [main] * 4 + [layers] + [(levels, width)] * 2 + [(x, LANES)],
        "solve_and_creep",
        70 * cells,
    )
    xa, xb = plane_exchange(xa, xb)
    other = lax.ppermute(pack, "phys", swap)
    temp, creep, hard, inside = call(
        balance_inside,
        (stress, temp, creep, hard, flow, k, za, zb, state),
        [main] * 4,
        "balance_inside",
        20 * cells,
        [dma((3,))],
        out_hbm=3,
    )
    (residual,) = call(
        balance_edges,
        (inside, xa, xb, other),
        [main],
        "balance_edges",
        10 * cells,
        [pltpu.VMEM(main, F32), dma((4,))],
        out_hbm=1,
    )
    return (temp, creep, hard, residual)


def solution(mesh):
    spec = P("stack", "plane", "phys")
    return jax.shard_map(per_device, mesh=mesh, in_specs=(spec,) * 7, out_specs=(spec,) * 4, check_vma=False)
```

```python
import functools

import jax
import jax.numpy as jnp
from jax import lax
from jax.experimental import pallas as pl
from jax.experimental.pallas import tpu as pltpu
from jax.sharding import PartitionSpec as P

TSTEPS = 3

k_table = (4.0, 0.6, 2.5, 1.2, 0.8)
cap_table = (1.6, 1.8, 1.7, 2.0, 1.9)
mod_table = (1.5, 0.6, 0.9, 1.2, 0.8)
expand_table = (0.1, 0.3, 0.25, 0.15, 0.2)
cap_unit = 0.0003
lat_unit = 1.2e-05
h_conv = 0.05
creep_rate = 0.05
log2e = 1.4426950408889634
inv_e = 0.36787944117144233

LANES = 128
SUB = 8
F32 = jnp.float32

U_FACTOR, U_SIDE, U_RIGHT, U_LAST, U_SOLVE, U_CREEP, U_FINAL, U_BACK, U_SWEEP = 8, 16, 64, 16, 64, 32, 32, 64, 64


def loop(count, body, init, unroll=16, reverse=False):
    while count % unroll:
        unroll -= 1

    def group(step, carry):
        for j in range(unroll):
            place = step * unroll + j
            carry = body(count - 1 - place if reverse else place, carry)
        return carry

    return lax.fori_loop(0, count // unroll, group, init)


def rcp(x):
    return pl.reciprocal(x, approx=True)


def by_code(code, table, scale=1.0):
    result = jnp.full(code.shape, table[4] * scale, F32)
    for entry in range(4):
        result = jnp.where(code == entry, F32(table[entry] * scale), result)
    return result


def cap_by_k(k):
    result = jnp.full(k.shape, cap_unit * cap_table[4], F32)
    for entry in range(4):
        result = jnp.where(k == F32(k_table[entry]), F32(cap_unit * cap_table[entry]), result)
    return result


def conductance(p, q, scale=1.0):
    return (2.0 * scale) * p * q * rcp(jnp.maximum(p + q, 1e-6))


VMEM = pl.BlockSpec(memory_space=pltpu.VMEM)
HBM = pl.BlockSpec(memory_space=pltpu.HBM)
ANY = pl.BlockSpec(memory_space=pl.ANY)


def call(body, ins, outs, name, flops=0, scratch=(), after=(), in_hbm=0, out_hbm=0, aliases=None, vmem=16):
    n_in, n_after = len(ins), len(after)

    def kernel(*refs):
        body(*refs[:n_in], *refs[n_in + n_after :])

    outs = [o if isinstance(o, jax.ShapeDtypeStruct) else jax.ShapeDtypeStruct(o, F32) for o in outs]
    size = sum(a.size * 4 for a in list(ins) + outs)
    return pl.pallas_call(
        kernel if after else body,
        in_specs=[HBM] * in_hbm + [VMEM] * (n_in - in_hbm) + [ANY] * n_after,
        out_specs=[HBM] * out_hbm + [VMEM] * (len(outs) - out_hbm),
        out_shape=outs,
        scratch_shapes=list(scratch),
        input_output_aliases=aliases or {},
        compiler_params=pltpu.CompilerParams(vmem_limit_bytes=vmem * 2**20),
        cost_estimate=pl.CostEstimate(flops=flops, bytes_accessed=size, transcendentals=0),
        name=name,
    )(*ins, *after)


def plane_exchange(a, b):
    count, cores = lax.axis_size("plane"), lax.axis_size("phys")
    pairs = [(i, i + 1) for i in range(0, count - 1, 2)]
    a = lax.ppermute(a, "plane", pairs + [(j, i) for i, j in pairs])
    pairs = [(i * cores + f, (i + 1) * cores + f) for i in range(1, count - 1, 2) for f in range(cores)]
    pairs += [(i * cores, i * cores + 1) for i in (0, count - 1)]
    b = lax.ppermute(b, ("plane", "phys"), pairs + [(j, i) for i, j in pairs])
    return a, b


def has_b():
    place, count = lax.axis_index("plane"), lax.axis_size("plane")
    return (place > 0) & (place < count - 1)


def even(axis):
    return lax.rem(lax.axis_index(axis), 2) == 0


def edge_rows(t_in, code_in, q_in, a_ref, b_ref, made, t, code, sem_in, sem_out):
    x = t_in.shape[1]
    is_even = even("plane")
    reads, writes = [], []
    for j in range(2):
        at_top = is_even if j == 0 else ~is_even
        near, far, beyond = (jnp.where(at_top, x - 1 - d, d) for d in range(3))
        for entry, (source, row, held) in enumerate(
            (
                (code_in, near, code.at[j, 0]),
                (code_in, far, code.at[j, 1]),
                (code_in, beyond, code.at[j, 2]),
                (t_in, far, made.at[j, 1]),
                (t_in, beyond, t.at[j]),
                (q_in, far, made.at[j, 5]),
                (t_in, near, made.at[j, 0]),
                (q_in, near, made.at[j, 4]),
            )
        ):
            reads.append(pltpu.make_async_copy(source.at[:, row, :], held, sem_in.at[j, entry]))
    for copy in reads:
        copy.start()
    for j, out in enumerate((a_ref, b_ref)):
        for copy in reads[8 * j : 8 * j + 8]:
            copy.wait()
        made[j, 2] = by_code(code[j, 0], k_table)
        k2, k3 = by_code(code[j, 1], k_table), by_code(code[j, 2], k_table)
        made[j, 3] = k2
        made[j, 5] = made[j, 5] + conductance(k2, k3, lat_unit) * (t[j] - made[j, 1])
        writes.append(pltpu.make_async_copy(made.at[j], out, sem_out.at[j]))
        writes[-1].start()
    for copy in writes:
        copy.wait()


def edge_layers(code, flag, dist, creep, hard, g, a_ref, b_ref):
    last = code.shape[0] - 1
    is_even = even("stack")
    for j in range(3):
        a_ref[j] = g[j]
        b_ref[j] = g[j]
    for j, source in enumerate((code, flag, dist, creep, hard)):
        after, before = source[last].astype(F32), source[0].astype(F32)
        a_ref[3 + j] = jnp.where(is_even, after, before)
        b_ref[3 + j] = jnp.where(is_even, before, after)


def end_losses():
    place, count = lax.axis_index("stack"), lax.axis_size("stack")
    return (jnp.where(place == 0, F32(h_conv), F32(0.0)), jnp.where(place == count - 1, F32(h_conv), F32(0.0)))


def lane_edge(tile_pair, i, pack):
    low, high = tile_pair
    at_low = lax.axis_index("phys") == 1
    edge = jnp.where(at_low, low, high)
    shift = jnp.where(at_low, i, lax.rem(i + 1, LANES))
    lane = lax.broadcasted_iota(jnp.int32, edge.shape, 1)
    return jnp.where(lane == i, pltpu.roll(edge, shift, 1), pack)


def lane_edge_of(value, i, pack):
    return lane_edge((value[:, :LANES], value[:, value.shape[1] - LANES :]), i, pack)


def lane_unedge(pack, i):
    at_low = lax.axis_index("phys") == 1
    shift = jnp.where(at_low, lax.rem(LANES - i, LANES), LANES - 1 - i)
    lane = lax.broadcasted_iota(jnp.int32, pack.shape, 1)
    return jnp.where(lane == jnp.where(at_low, 0, LANES - 1), pltpu.roll(pack, shift, 1), 0.0)


def add_at_edge(value, edge):
    at_low = lax.axis_index("phys") == 1
    tiles = [value[:, j : j + LANES] for j in range(0, value.shape[1], LANES)]
    tiles[0] = tiles[0] + jnp.where(at_low, edge, 0.0)
    tiles[-1] = tiles[-1] + jnp.where(at_low, 0.0, edge)
    return jnp.concatenate(tiles, axis=1)


def from_beside(t, g, axis):
    return g * pltpu.roll(t, t.shape[axis] - 1, axis) + pltpu.roll(g * t, 1, axis)


def lateral_main(k_ref, t_ref, q_ref, gx_ref, gy_ref, diag_ref, p_ref):
    levels, x, width = t_ref.shape
    row = lax.broadcasted_iota(jnp.int32, (x, width), 0)
    lane = lax.broadcasted_iota(jnp.int32, (x, width), 1)

    def level(i, carry):
        k, t = k_ref[i], t_ref[i]
        gx = conductance(k, pltpu.roll(k, x - 1, 0), lat_unit)
        gx = jnp.where(row == x - 1, 0.0, gx)
        gx_ref[i] = gx
        gy = conductance(k, pltpu.roll(k, width - 1, 1), lat_unit)
        gy = jnp.where(lane == width - 1, 0.0, gy)
        gy_ref[i] = gy
        diag = cap_by_k(k) - gx - pltpu.roll(gx, 1, 0) - gy - pltpu.roll(gy, 1, 1)
        diag_ref[i] = diag
        p_ref[i] = diag * t + q_ref[i] + from_beside(t, gx, 0) + from_beside(t, gy, 1)
        return carry

    loop(levels, level, 0, unroll=U_FACTOR)


def factor_main(code_ref, t_ref, pack_ref, k_ref, w_ref, r_ref, yr_ref, left_ref, right_ref, g_ref):
    levels, x, width = t_ref.shape
    first_loss, last_loss = end_losses()

    def tables(i, carry):
        pack_t, pack_k = carry
        k = by_code(code_ref[i], k_table)
        k_ref[i] = k
        loss = jnp.where(i == 0, first_loss, 0.0) + jnp.where(i == levels - 1, last_loss, 0.0)
        r_ref[i] = by_code(code_ref[i], cap_table, cap_unit) + loss
        return (lane_edge_of(t_ref[i], i, pack_t), lane_edge_of(k, i, pack_k))

    tile = jnp.zeros((x, LANES), F32)
    pack_ref[0], pack_ref[1] = loop(levels, tables, (tile, tile))
    zero = jnp.zeros((x, width), F32)

    def forward(i, carry):
        ws, y, k_here = carry
        k_next = k_ref[jnp.minimum(i + 1, levels - 1)]
        s = r_ref[i] + ws
        u = jnp.where(i == levels - 1, 0.0, conductance(k_here, k_next))
        r = rcp(s + u)
        w = u * r
        w_ref[i] = w
        r_ref[i] = r
        yr_ref[i] = y * r
        return (w * s, y * w, k_next)

    loop(levels, forward, (zero, zero + 1.0, k_ref[0]))

    def backward(i, carry):
        left, right, pack_l, pack_r = carry
        w = w_ref[i]
        left = yr_ref[i] + w * left
        right = jnp.where(i == levels - 1, r_ref[i], w * right)
        left_ref[i], right_ref[i] = left, right
        return (left, right, lane_edge_of(left, i, pack_l), lane_edge_of(right, i, pack_r))

    left, _, pack_ref[2], pack_ref[3] = loop(levels, backward, (zero, zero, tile, tile), reverse=True)
    g_ref[0] = left + 0.5 * rcp(k_ref[0])
    g_ref[1] = yr_ref[levels - 1]
    g_ref[2] = r_ref[levels - 1] + 0.5 * rcp(k_ref[levels - 1])


def assemble_halo(a_ref, b_ref, kh_ref, th_ref, qh_ref, pack_ref):
    is_even = even("plane")
    levels, _, width = kh_ref.shape
    row = lax.broadcasted_iota(jnp.int32, (SUB, width), 0)
    a_rows = [row == jnp.where(is_even, j, SUB - 1 - j) for j in (0, 1)]
    b_rows = [(row == jnp.where(is_even, SUB - 1 - j, j)) & has_b() for j in (0, 1)]

    def level(i, carry):
        pack_t, pack_k = carry
        halos = []
        for first, ref in ((0, th_ref), (2, kh_ref), (4, qh_ref)):
            halo = jnp.zeros((SUB, width), F32)
            for source, rows in ((a_ref, a_rows), (b_ref, b_rows)):
                for j in (0, 1):
                    halo = jnp.where(rows[j], source[first + j, pl.ds(i, 1), :], halo)
            ref[i] = halo
            halos.append(halo)
        return (lane_edge_of(halos[0], i, pack_t), lane_edge_of(halos[1], i, pack_k))

    zero = jnp.zeros((SUB, LANES), F32)
    pack_ref[0], pack_ref[1] = loop(levels, level, (zero, zero), unroll=64)


def first_side(p, t, k, left, right, th, kh, qh, gxh, gyh, diagh, wh, rh, yrh, lefth, righth, rhs_ref, rhsh, send, pack_ref):
    levels, x, width = t.shape
    row = lax.broadcasted_iota(jnp.int32, (SUB, width), 0)
    lane = lax.broadcasted_iota(jnp.int32, (SUB, width), 1)
    first_loss, last_loss = end_losses()

    def forward(i, carry):
        ws, yy, here, bf, bl = carry
        temp, t_main, k_main = th[i], t[i], k[i]
        k_next = kh[jnp.minimum(i + 1, levels - 1)]
        cap = cap_by_k(here)
        loss = jnp.where(i == 0, first_loss, 0.0) + jnp.where(i == levels - 1, last_loss, 0.0)
        s = cap + loss + ws
        u = jnp.where(i == levels - 1, 0.0, conductance(here, k_next))
        rr = rcp(s + u)
        ww = u * rr
        wh[i], rh[i], yrh[i] = ww, rr, yy * rr

        gx = conductance(here, jnp.where(row == SUB - 1, k_main[0:1], pltpu.roll(here, SUB - 1, 0)), lat_unit)
        g_low = conductance(here, jnp.where(row == 0, k_main[x - 1 :], pltpu.roll(here, 1, 0)), lat_unit)
        gy = conductance(here, pltpu.roll(here, width - 1, 1), lat_unit)
        gy = jnp.where(lane == width - 1, 0.0, gy)
        gxh[i], gyh[i] = gx, gy
        diag = cap - gx - g_low - gy - pltpu.roll(gy, 1, 1)
        diagh[i] = diag
        step_up = jnp.where(row == SUB - 1, t_main[0:1], pltpu.roll(temp, SUB - 1, 0))
        step_low = jnp.where(row == 0, t_main[x - 1 :], pltpu.roll(temp, 1, 0))
        rhsh[i] = diag * temp + qh[i] + gx * step_up + g_low * step_low + from_beside(temp, gy, 1)
        to_first = pltpu.roll(gx * (temp - step_up), 1, 0)
        to_last = pltpu.roll(g_low * (temp - step_low), SUB - 1, 0)
        rhs = p[i]
        parts = [rhs[j : j + SUB] for j in range(0, x, SUB)]
        parts[0] = parts[0] + jnp.where(row == 0, to_first, 0.0)
        parts[-1] = parts[-1] + jnp.where(row == SUB - 1, to_last, 0.0)
        rhs = jnp.concatenate(parts, axis=0)
        rhs_ref[i] = rhs
        return (ww * s, yy * ww, k_next, bf + left[i] * rhs, bl + right[i] * rhs)

    zero, zero_main = jnp.zeros((SUB, width), F32), jnp.zeros((x, width), F32)
    *_, bf, bl = loop(levels, forward, (zero, zero + 1.0, kh[0], zero_main, zero_main), unroll=U_SIDE)

    def backward(i, carry):
        ll, rr, bfh, blh, pack_l, pack_r = carry
        ww, rhs = wh[i], rhsh[i]
        ll = yrh[i] + ww * ll
        rr = jnp.where(i == levels - 1, rh[i], ww * rr)
        lefth[i], righth[i] = ll, rr
        return (ll, rr, bfh + ll * rhs, blh + rr * rhs, lane_edge_of(ll, i, pack_l), lane_edge_of(rr, i, pack_r))

    tile = jnp.zeros((SUB, LANES), F32)
    init = (zero, zero, zero, zero, tile, tile)
    ll, _, bfh, blh, pack_ref[0], pack_ref[1] = loop(levels, backward, init, unroll=U_BACK, reverse=True)
    for j in range(0, x, SUB):
        send[j // SUB] = bf[j : j + SUB]
        send[(x + j) // SUB] = bl[j : j + SUB]
    send[2 * x // SUB] = packed(bfh, blh)
    half = [0.5 * rcp(jnp.maximum(kh[i], 1e-3)) for i in (0, levels - 1)]
    send[2 * x // SUB + 1] = packed(ll + half[0], yrh[levels - 1])
    send[2 * x // SUB + 2] = packed(rh[levels - 1] + half[1], rh[levels - 1])


def both(main_ref, halo_ref, i):
    return jnp.concatenate([main_ref[i], halo_ref[i]], axis=0)


def join_rows(gxh, k, kh, gx_in, diag_in, gx_ref, diag_ref):
    levels, x, _ = k.shape

    def level(i, carry):
        g_first = gxh[i, SUB - 1 : SUB, :]
        g_last = conductance(k[i, x - 1 : x, :], kh[i, 0:1, :], lat_unit)
        gx_ref[i, x - 1 : x, :] = g_last
        diag_ref[i, 0:1, :] = diag_in[i, 0:1, :] - g_first
        diag_ref[i, x - 1 : x, :] = diag_in[i, x - 1 : x, :] - g_last
        return carry

    loop(levels, level, 0, unroll=64)


def right_side(last, *refs):
    t, th, q, qh, diag, diagh, gx, gxh, gy, gyh, left, lefth, right, righth, *out = refs
    levels, x, width = t.shape
    send = out[-1]
    rows = x if last else x + SUB

    def pick(main_ref, halo_ref, i):
        return main_ref[i] if last else both(main_ref, halo_ref, i)

    def level(i, carry):
        bf, bl = carry
        temp = both(t, th, i)
        here = temp[:rows]
        rhs = pick(diag, diagh, i) * here + pick(q, qh, i) + from_beside(temp, both(gx, gxh, i), 0)[:rows]
        rhs = rhs + from_beside(here, pick(gy, gyh, i), 1)
        out[0][i] = rhs[:x]
        if not last:
            out[1][i] = rhs[x:]
        return (bf + pick(left, lefth, i) * rhs, bl + pick(right, righth, i) * rhs)

    zero = jnp.zeros((rows, width), F32)
    parts = loop(levels, level, (zero, zero), unroll=U_LAST if last else U_RIGHT)
    groups = [part[j : j + SUB] for part in parts for j in range(0, x, SUB)]
    if not last:
        groups.append(packed(*[part[x:] for part in parts]))
    for j, group in enumerate(groups):
        send[j] = group


def edge_flow(first, x, rows, *refs):
    raw, pack, packh, packh_lr, other, otherh, *refs = refs
    own_k, other_k = (jnp.concatenate([a[1], b[1]], axis=0)[:rows] for a, b in ((pack, packh), (other, otherh)))
    if first:
        own_t, other_t = (jnp.concatenate([a[0], b[0]], axis=0)[:rows] for a, b in ((pack, packh), (other, otherh)))
    else:
        own_t, other_t = refs[0][:rows], refs[1][:rows]
    flow_ref, send = refs[-2:]
    flow = conductance(own_k, other_k, lat_unit) * (other_t - own_t)
    flow_ref[...] = flow
    at_low = lax.axis_index("phys") == 1
    lane = lax.broadcasted_iota(jnp.int32, flow.shape, 1)
    changes = []
    for j in (0, 1):
        response = jnp.concatenate([pack[2 + j], packh_lr[j]], axis=0)[:rows]
        change = jnp.sum(flow * response, axis=1, keepdims=True)
        changes.append(jnp.where(lane == jnp.where(at_low, 0, LANES - 1), change, 0.0))
    groups = [change[j : j + SUB] for change in changes for j in range(0, x, SUB)]
    if rows > x:
        groups.append(packed(*[change[x:] for change in changes]))
    for j in range(send.shape[0]):
        send[j] = add_at_edge(raw[j], groups[j]) if j < len(groups) else raw[j]


def forward_sweep(flow, *refs):
    count = len(refs) // 4
    w, r, rhs, z = (refs[j * count : (j + 1) * count] for j in range(4))
    levels, x, width = z[0].shape

    def pick(pair, i):
        return jnp.concatenate([ref[i] for ref in pair], axis=0)

    def level(i, wy):
        y = add_at_edge(pick(rhs, i) + wy, lane_unedge(flow[...], i))
        value = pick(r, i) * y
        z[0][i] = value[:x]
        if count > 1:
            z[1][i] = value[x:]
        return pick(w, i) * y

    loop(levels, level, jnp.zeros((flow.shape[0], width), F32), unroll=U_SWEEP)


def packed(a, b):
    row = lax.broadcasted_iota(jnp.int32, a.shape, 0)
    return jnp.where((row >= 2) & (row < 6), pltpu.roll(b, 4, 0), a)


def block_flows(g_sets, h_sets, b_sets, x, rows):
    place, count = lax.axis_index("stack"), lax.axis_size("stack")

    def at(sets, block, read):
        value = read(sets[0])
        for j in range(1, count):
            value = jnp.where((place ^ j) == block, read(sets[j]), value)
        return value

    def ends(block):
        group = at(b_sets, block, lambda ref: ref[0 : 2 * x // SUB])
        group = group.reshape(2, x, group.shape[-1])
        if rows == x:
            return (group[0], group[1])
        tail = at(b_sets, block, lambda ref: ref[2 * x // SUB])
        return (
            jnp.concatenate([group[0], tail], axis=0),
            jnp.concatenate([group[1], pltpu.roll(tail, 4, 0)], axis=0),
        )

    def responses(block):
        group = at(g_sets, block, lambda ref: ref[0:3])
        if rows == x:
            return group
        tail = at(h_sets, block, lambda ref: ref[2 * x // SUB + 1 : 2 * x // SUB + 3])
        tails = (tail[0], pltpu.roll(tail[0], 4, 0), tail[1])
        return [jnp.concatenate([group[j], tails[j]], axis=0) for j in range(3)]

    end = [ends(block) for block in range(count)]
    g = [responses(block) for block in range(count)]
    ups, flows = [], []
    for j in range(count - 1):
        pivot = g[j][2] + g[j + 1][0]
        value = end[j + 1][0] - end[j][1]
        if j:
            pivot = pivot - g[j][1] * ups[j - 1]
            value = value + g[j][1] * flows[j - 1]
        inverse = rcp(pivot)
        ups.append(g[j + 1][1] * inverse)
        flows.append(value * inverse)
    for j in reversed(range(count - 2)):
        flows[j] = flows[j] + ups[j] * flows[j + 1]
    top = jnp.zeros_like(flows[0])
    bottom = top
    for j in range(count - 1):
        top = jnp.where(place == j + 1, -flows[j], top)
        bottom = jnp.where(place == j, flows[j], bottom)
    return top, bottom


def beside(edge, flow, k_edge, code_beside):
    return edge + flow * (0.5 * rcp(k_edge) + 0.5 * rcp(by_code(code_beside, k_table)))


def layers_beside(za, zb):
    is_even = even("stack")
    sides = []
    for j in (0, 1):
        value = [jnp.where(is_even, (zb, za)[j][3 + e], (za, zb)[j][3 + e]) for e in range(5)]
        value[4] = jnp.maximum(value[4], 0.1)
        sides.append(value)
    return sides


def rate_by_flag(active):
    return jnp.where(active, F32(creep_rate * inv_e), F32(0.0))


def column_solve(count, first, *refs):
    g_sets, h_sets, refs = refs[:count], refs[count : 2 * count], refs[2 * count :]
    b_sets = h_sets
    if not first:
        b_sets, refs = refs[:count], refs[count:]
    z, zh, w, wh, r, rh, yr, yrh, t, th, pack_ref, flow_ref = refs
    levels, x, width = z.shape
    rows = x + SUB
    top, bottom = block_flows(g_sets, h_sets, b_sets, x, rows)
    flow_ref[0], flow_ref[1] = top[:x], bottom[:x]

    def level(i, carry):
        add, pack = carry
        value = both(z, zh, i) + top * both(yr, yrh, i) + add
        t[i] = value[:x]
        th[i] = value[x:]
        pack = lane_edge_of(value, i, pack)
        return (both(w, wh, jnp.maximum(i - 1, 0)) * value, pack)

    init = (bottom * both(r, rh, levels - 1), jnp.zeros((rows, LANES), F32))
    _, pack_ref[...] = loop(levels, level, init, unroll=U_SOLVE, reverse=True)


def prepare_creep(code_ref, flag_ref, mod, exp, rate):
    def level(i, carry):
        code = code_ref[i]
        mod[i] = by_code(code, mod_table)
        exp[i] = by_code(code, expand_table)
        rate[i] = rate_by_flag(flag_ref[i] == 1)
        return carry

    loop(code_ref.shape[0], level, 0)


def creep_cells(temp, mod, exp, rate, dist, creep, hard):
    elastic = dist - exp * temp
    strain = elastic - creep
    drive = jnp.exp2((0.5 * log2e) * mod * jnp.abs(strain) * rcp(hard) - 1.0)
    drive = drive - 0.25 * rcp(drive)
    rate = rate * jnp.exp2(-log2e * rcp(jnp.exp2((0.5 * log2e) * temp + 1.0) + 1.0)) * drive
    gap = 1.0 - hard * jnp.exp2(-0.1 * jnp.log2(0.5 + drive) - 1.0)
    gap_size = jnp.abs(gap)
    root = gap_size * lax.rsqrt(jnp.maximum(gap_size, 1e-30))
    creep = creep + jnp.where(strain < 0.0, -rate, rate)
    hard = hard + gap * root * rate
    return (elastic, creep, hard)


def creep_beside(t, flow, k, za, zb, state):
    ends, results = (0, t.shape[0] - 1), []
    for j, (code, flag, dist, creep, hard) in enumerate(layers_beside(za, zb)):
        if state is not None:
            creep, hard = state[j], state[2 + j]
        temp = beside(t[ends[j]], flow[j], k[ends[j]], code)
        mod = by_code(code, mod_table)
        cells = creep_cells(temp, mod, by_code(code, expand_table), rate_by_flag(flag == 1.0), dist, creep, hard)
        results.append((*cells, mod))
    return results


def creep_step(first, *refs):
    main, refs = refs[:7], refs[7:]
    flow, k, za, zb = refs[:4]
    state, out = (None, refs[4:]) if first else (refs[4], refs[5:])

    def level(i, carry):
        _, out[0][i], out[1][i] = creep_cells(*[ref[i] for ref in main])
        return carry

    loop(main[0].shape[0], level, 0, unroll=U_CREEP)
    for j, (_, creep, hard, _) in enumerate(creep_beside(main[0], flow, k, za, zb, state)):
        out[2][j] = creep
        out[2][2 + j] = hard


def solve_and_creep(count, *refs):
    g_sets, b_sets, refs = refs[:count], refs[count : 2 * count], refs[2 * count :]
    z, w, r, yr, mod, exp, rate, dist, creep, hard = refs[:10]
    t, creep_out, hard_out, s, flow_ref, xa, xb, pack_ref = refs[10:]
    levels, x, width = z.shape
    top, bottom = block_flows(g_sets, None, b_sets, x, x)

    def level(i, carry):
        add, pack = carry
        value = z[i] + top * yr[i] + add
        t[i] = value
        m = mod[i]
        elastic, new, hard_out[i] = creep_cells(value, m, exp[i], rate[i], dist[i], creep[i], hard[i])
        creep_out[i] = new
        stress = m * (elastic - new)
        s[i] = stress
        pack = lane_edge_of(stress, i, pack)
        return (w[jnp.maximum(i - 1, 0)] * value, pack)

    init = (bottom * r[levels - 1], jnp.zeros((x, LANES), F32))
    _, pack_ref[...] = loop(levels, level, init, unroll=U_FINAL, reverse=True)
    flow_ref[0], flow_ref[1] = top, bottom
    is_even = even("plane")
    upper, lower = s[:, x - 1, :], s[:, 0, :]
    xa[...] = jnp.where(is_even, upper, lower)
    xb[...] = jnp.where(is_even, lower, upper)


def balance_inside(s, t, creep, hard, flow, k, za, zb, state, t_out, creep_out, hard_out, inside, sem):
    copies = [
        pltpu.make_async_copy(held, out, sem.at[j])
        for j, (held, out) in enumerate(((t, t_out), (creep, creep_out), (hard, hard_out)))
    ]
    for copy in copies:
        copy.start()
    levels, x, width = s.shape
    row = lax.broadcasted_iota(jnp.int32, (x, width), 0)
    lane = lax.broadcasted_iota(jnp.int32, (x, width), 1)
    place, count = lax.axis_index("stack"), lax.axis_size("stack")
    zs = [
        jnp.where(place == end, 0.0, m * (elastic - new))
        for end, (elastic, new, _, m) in zip((0, count - 1), creep_beside(t, flow, k, za, zb, state))
    ]

    def level(i, before):
        here = s[i]
        after = jnp.where(i == levels - 1, zs[1], s[jnp.minimum(i + 1, levels - 1)])
        total = before + after - 6.0 * here
        total = total + jnp.where(row == 0, 0.0, pltpu.roll(here, 1, 0))
        total = total + jnp.where(row == x - 1, 0.0, pltpu.roll(here, x - 1, 0))
        total = total + jnp.where(lane == 0, 0.0, pltpu.roll(here, 1, 1))
        inside[i] = total + jnp.where(lane == width - 1, 0.0, pltpu.roll(here, width - 1, 1))
        return here

    loop(levels, level, zs[0], unroll=8)
    for copy in copies:
        copy.wait()


def balance_edges(inside, xa, xb, other, out, held, sem):
    levels, x, width = inside.shape
    is_even = even("plane")
    row = lax.broadcasted_iota(jnp.int32, (x, width), 0)
    a_row = row == jnp.where(is_even, x - 1, 0)
    b_row = (row == jnp.where(is_even, 0, x - 1)) & has_b()
    chunks = sem.shape[0]
    part = levels // chunks
    copies = []
    for chunk in range(chunks):

        def level(j, carry, chunk=chunk):
            i = chunk * part + j
            total = inside[i] + jnp.where(a_row, xa[pl.ds(i, 1), :], 0.0)
            total = total + jnp.where(b_row, xb[pl.ds(i, 1), :], 0.0)
            held[i] = add_at_edge(total, lane_unedge(other[...], i))
            return carry

        loop(part, level, 0)
        place = pl.ds(chunk * part, part)
        copies.append(pltpu.make_async_copy(held.at[place], out.at[place], sem.at[chunk]))
        copies[-1].start()
    for copy in copies:
        copy.wait()


def per_device(temp, source, code, flag, distortion, creep, hard):
    levels, x, width = temp.shape
    count = lax.axis_size("stack")
    if lax.axis_size("phys") != 2 or count != 4 or lax.axis_size("plane") % 2 or levels > LANES or x % SUB or width % LANES:
        raise ValueError("unsupported sizes")
    main, halo, layers = (levels, x, width), (levels, SUB, width), (2, x, width)
    cells = levels * x * width
    swap = [(0, 1), (1, 0)]
    peers = [[(i, i ^ j) for i in range(count)] for j in range(1, count)]
    dma = pltpu.SemaphoreType.DMA

    edge = (6, levels, width)
    rows_a, rows_b = call(
        edge_rows,
        (temp, code, source),
        [edge] * 2,
        "edge_rows",
        cells,
        [
            pltpu.VMEM((2, *edge), F32),
            pltpu.VMEM((2, levels, width), F32),
            pltpu.VMEM((2, 3, levels, width), jnp.int32),
            dma((2, 8)),
            dma((2,)),
        ],
        in_hbm=3,
        out_hbm=2,
        vmem=60,
    )
    rows_a, rows_b = plane_exchange(rows_a, rows_b)
    pack, k, w, r, yr, left, right, g = call(
        factor_main, (code, temp), [(4, x, LANES)] + [main] * 6 + [(3, x, width)], "factor_main", 30 * cells
    )
    gx, gy, diag, part = call(lateral_main, (k, temp, source), [main] * 4, "lateral_main", 40 * cells)
    za, zb = call(edge_layers, (code, flag, distortion, creep, hard, g), [(8, x, width)] * 2, "edge_layers", cells, after=(part,))
    za, g_two, zb = lax.ppermute(za, "stack", peers[0]), lax.ppermute(g, "stack", peers[1]), lax.ppermute(zb, "stack", peers[2])
    g_sets = [g, za, g_two, zb]
    other_pack = lax.ppermute(pack[:2], "phys", swap)

    kh, th, qh, packh = call(
        assemble_halo, (rows_a, rows_b), [halo] * 3 + [(2, SUB, LANES)], "assemble_halo", cells, after=(part,)
    )
    other_packh = lax.ppermute(packh, "phys", swap)
    rows = x + SUB
    groups = 2 * x // SUB
    gxh, gyh, diagh, wh, rh, yrh, lefth, righth, rhs, rhsh, send, packh_lr = call(
        first_side,
        (part, temp, k, left, right, th, kh, qh),
        [halo] * 8 + [main, halo, (groups + 3, SUB, width), (2, SUB, LANES)],
        "first_side",
        40 * cells,
    )

    own = other = state = None
    for step in range(TSTEPS):
        first, last = step == 0, step == TSTEPS - 1
        if not first:
            ins = (temp, th, source, qh, diag, diagh, gx, gxh, gy, gyh, left, lefth, right, righth)
            send = (groups if last else groups + 1, SUB, width)
            rhs, *rhsh, send = call(
                functools.partial(right_side, last), ins, [main, send] if last else [main, halo, send], "right_side", 30 * cells
            )
            rhsh = rhsh[0] if rhsh else None
        flow_rows = x if last else rows
        lane_flow, send = call(
            functools.partial(edge_flow, first, x, flow_rows),
            [send, pack, packh, packh_lr, other_pack, other_packh] + ([] if first else [own, other]),
            [(flow_rows, LANES), send.shape],
            "edge_flow",
            cells // 8,
        )
        b_sets = [send] + [lax.ppermute(send, "stack", peer) for peer in peers]
        ins = [lane_flow, w, r, rhs] if last else [lane_flow, w, wh, r, rh, rhs, rhsh]
        z, *zh = call(
            forward_sweep, ins, [main] if last else [main, halo], "forward_sweep", cells, aliases={3: 0} if last else {5: 0, 6: 1}
        )
        zh = zh[0] if zh else None
        if first:
            h_sets = b_sets
            mod, exp, rate = call(prepare_creep, (code, flag), [main] * 3, "prepare_creep", 10 * cells, after=(z,))
            gx, diag = call(join_rows, (gxh, k, kh, gx, diag), [main] * 2, "join_rows", cells, aliases={3: 0, 4: 1}, after=(rate,))
        else:
            creep, hard, state = call(
                functools.partial(creep_step, step == 1),
                [temp, mod, exp, rate, distortion, creep, hard, flow, k, za, zb] + ([] if step == 1 else [state]),
                [main] * 2 + [(4, x, width)],
                "creep_step",
                60 * cells,
            )
        if last:
            break
        temp, th, own, flow = call(
            functools.partial(column_solve, count, first),
            g_sets + h_sets + ([] if first else b_sets) + [z, zh, w, wh, r, rh, yr, yrh],
            [main, halo, (rows, LANES), layers],
            "column_solve",
            10 * cells,
            after=(rate, diag) if first else (creep,),
        )
        other = lax.ppermute(own, "phys", swap)

    temp, creep, hard, stress, flow, xa, xb, pack = call(
        functools.partial(solve_and_creep, count),
        g_sets + b_sets + [z, w, r, yr, mod, exp, rate, distortion, creep, hard],
        [main] * 4 + [layers] + [(levels, width)] * 2 + [(x, LANES)],
        "solve_and_creep",
        70 * cells,
    )
    xa, xb = plane_exchange(xa, xb)
    other = lax.ppermute(pack, "phys", swap)
    temp, creep, hard, inside = call(
        balance_inside,
        (stress, temp, creep, hard, flow, k, za, zb, state),
        [main] * 4,
        "balance_inside",
        20 * cells,
        [dma((3,))],
        out_hbm=3,
    )
    (residual,) = call(
        balance_edges,
        (inside, xa, xb, other),
        [main],
        "balance_edges",
        10 * cells,
        [pltpu.VMEM(main, F32), dma((4,))],
        out_hbm=1,
    )
    return (temp, creep, hard, residual)


def solution(mesh):
    spec = P("stack", "plane", "phys")
    return jax.shard_map(per_device, mesh=mesh, in_specs=(spec,) * 7, out_specs=(spec,) * 4, check_vma=False)
```

```python
import functools

import jax
import jax.numpy as jnp
from jax import lax
from jax.experimental import pallas as pl
from jax.experimental.pallas import tpu as pltpu
from jax.sharding import PartitionSpec as P

TSTEPS = 3

k_table = (4.0, 0.6, 2.5, 1.2, 0.8)
cap_table = (1.6, 1.8, 1.7, 2.0, 1.9)
mod_table = (1.5, 0.6, 0.9, 1.2, 0.8)
expand_table = (0.1, 0.3, 0.25, 0.15, 0.2)
cap_unit = 0.0003
lat_unit = 1.2e-05
h_conv = 0.05
creep_rate = 0.05
log2e = 1.4426950408889634
inv_e = 0.36787944117144233

LANES = 128
SUB = 8
F32 = jnp.float32

U_FACTOR, U_SIDE, U_RIGHT, U_LAST, U_SOLVE, U_CREEP, U_FINAL, U_BACK, U_SWEEP = 8, 8, 32, 16, 32, 32, 16, 32, 32


def loop(count, body, init, unroll=16, reverse=False):
    while count % unroll:
        unroll -= 1

    def group(step, carry):
        for j in range(unroll):
            place = step * unroll + j
            carry = body(count - 1 - place if reverse else place, carry)
        return carry

    return lax.fori_loop(0, count // unroll, group, init)


def rcp(x):
    return pl.reciprocal(x, approx=True)


def by_code(code, table, scale=1.0):
    result = jnp.full(code.shape, table[4] * scale, F32)
    for entry in range(4):
        result = jnp.where(code == entry, F32(table[entry] * scale), result)
    return result


def cap_by_k(k):
    result = jnp.full(k.shape, cap_unit * cap_table[4], F32)
    for entry in range(4):
        result = jnp.where(k == F32(k_table[entry]), F32(cap_unit * cap_table[entry]), result)
    return result


def conductance(p, q, scale=1.0):
    return (2.0 * scale) * p * q * rcp(jnp.maximum(p + q, 1e-6))


VMEM = pl.BlockSpec(memory_space=pltpu.VMEM)
HBM = pl.BlockSpec(memory_space=pltpu.HBM)
ANY = pl.BlockSpec(memory_space=pl.ANY)


def call(body, ins, outs, name, flops=0, scratch=(), after=(), in_hbm=0, out_hbm=0, aliases=None, vmem=16):
    n_in, n_after = len(ins), len(after)

    def kernel(*refs):
        body(*refs[:n_in], *refs[n_in + n_after :])

    outs = [o if isinstance(o, jax.ShapeDtypeStruct) else jax.ShapeDtypeStruct(o, F32) for o in outs]
    size = sum(a.size * 4 for a in list(ins) + outs)
    return pl.pallas_call(
        kernel if after else body,
        in_specs=[HBM] * in_hbm + [VMEM] * (n_in - in_hbm) + [ANY] * n_after,
        out_specs=[HBM] * out_hbm + [VMEM] * (len(outs) - out_hbm),
        out_shape=outs,
        scratch_shapes=list(scratch),
        input_output_aliases=aliases or {},
        compiler_params=pltpu.CompilerParams(vmem_limit_bytes=vmem * 2**20),
        cost_estimate=pl.CostEstimate(flops=flops, bytes_accessed=size, transcendentals=0),
        name=name,
    )(*ins, *after)


def plane_exchange(a, b):
    count, cores = lax.axis_size("plane"), lax.axis_size("phys")
    pairs = [(i, i + 1) for i in range(0, count - 1, 2)]
    a = lax.ppermute(a, "plane", pairs + [(j, i) for i, j in pairs])
    pairs = [(i * cores + f, (i + 1) * cores + f) for i in range(1, count - 1, 2) for f in range(cores)]
    pairs += [(i * cores, i * cores + 1) for i in (0, count - 1)]
    b = lax.ppermute(b, ("plane", "phys"), pairs + [(j, i) for i, j in pairs])
    return a, b


def has_b():
    place, count = lax.axis_index("plane"), lax.axis_size("plane")
    return (place > 0) & (place < count - 1)


def even(axis):
    return lax.rem(lax.axis_index(axis), 2) == 0


def edge_rows(t_in, code_in, q_in, a_ref, b_ref, made, t, code, sem_in, sem_out):
    x = t_in.shape[1]
    is_even = even("plane")
    reads, writes = [], []
    for j in range(2):
        at_top = is_even if j == 0 else ~is_even
        near, far, beyond = (jnp.where(at_top, x - 1 - d, d) for d in range(3))
        for entry, (source, row, held) in enumerate(
            (
                (code_in, near, code.at[j, 0]),
                (code_in, far, code.at[j, 1]),
                (code_in, beyond, code.at[j, 2]),
                (t_in, far, made.at[j, 1]),
                (t_in, beyond, t.at[j]),
                (q_in, far, made.at[j, 5]),
                (t_in, near, made.at[j, 0]),
                (q_in, near, made.at[j, 4]),
            )
        ):
            reads.append(pltpu.make_async_copy(source.at[:, row, :], held, sem_in.at[j, entry]))
    for copy in reads:
        copy.start()
    for j, out in enumerate((a_ref, b_ref)):
        for copy in reads[8 * j : 8 * j + 8]:
            copy.wait()
        made[j, 2] = by_code(code[j, 0], k_table)
        k2, k3 = by_code(code[j, 1], k_table), by_code(code[j, 2], k_table)
        made[j, 3] = k2
        made[j, 5] = made[j, 5] + conductance(k2, k3, lat_unit) * (t[j] - made[j, 1])
        writes.append(pltpu.make_async_copy(made.at[j], out, sem_out.at[j]))
        writes[-1].start()
    for copy in writes:
        copy.wait()


def edge_layers(code, flag, dist, creep, hard, g, a_ref, b_ref):
    last = code.shape[0] - 1
    is_even = even("stack")
    for j in range(3):
        a_ref[j] = g[j]
        b_ref[j] = g[j]
    for j, source in enumerate((code, flag, dist, creep, hard)):
        after, before = source[last].astype(F32), source[0].astype(F32)
        a_ref[3 + j] = jnp.where(is_even, after, before)
        b_ref[3 + j] = jnp.where(is_even, before, after)


def end_losses():
    place, count = lax.axis_index("stack"), lax.axis_size("stack")
    return (jnp.where(place == 0, F32(h_conv), F32(0.0)), jnp.where(place == count - 1, F32(h_conv), F32(0.0)))


def lane_edge(tile_pair, i, pack):
    low, high = tile_pair
    at_low = lax.axis_index("phys") == 1
    edge = jnp.where(at_low, low, high)
    shift = jnp.where(at_low, i, lax.rem(i + 1, LANES))
    lane = lax.broadcasted_iota(jnp.int32, edge.shape, 1)
    return jnp.where(lane == i, pltpu.roll(edge, shift, 1), pack)


def lane_edge_of(value, i, pack):
    return lane_edge((value[:, :LANES], value[:, value.shape[1] - LANES :]), i, pack)


def lane_unedge(pack, i):
    at_low = lax.axis_index("phys") == 1
    shift = jnp.where(at_low, lax.rem(LANES - i, LANES), LANES - 1 - i)
    lane = lax.broadcasted_iota(jnp.int32, pack.shape, 1)
    return jnp.where(lane == jnp.where(at_low, 0, LANES - 1), pltpu.roll(pack, shift, 1), 0.0)


def add_at_edge(value, edge):
    at_low = lax.axis_index("phys") == 1
    tiles = [value[:, j : j + LANES] for j in range(0, value.shape[1], LANES)]
    tiles[0] = tiles[0] + jnp.where(at_low, edge, 0.0)
    tiles[-1] = tiles[-1] + jnp.where(at_low, 0.0, edge)
    return jnp.concatenate(tiles, axis=1)


def from_beside(t, g, axis):
    return g * pltpu.roll(t, t.shape[axis] - 1, axis) + pltpu.roll(g * t, 1, axis)


def lateral_main(k_ref, t_ref, q_ref, gx_ref, gy_ref, diag_ref, p_ref):
    levels, x, width = t_ref.shape
    row = lax.broadcasted_iota(jnp.int32, (x, width), 0)
    lane = lax.broadcasted_iota(jnp.int32, (x, width), 1)

    def level(i, carry):
        k, t = k_ref[i], t_ref[i]
        gx = conductance(k, pltpu.roll(k, x - 1, 0), lat_unit)
        gx = jnp.where(row == x - 1, 0.0, gx)
        gx_ref[i] = gx
        gy = conductance(k, pltpu.roll(k, width - 1, 1), lat_unit)
        gy = jnp.where(lane == width - 1, 0.0, gy)
        gy_ref[i] = gy
        diag = cap_by_k(k) - gx - pltpu.roll(gx, 1, 0) - gy - pltpu.roll(gy, 1, 1)
        diag_ref[i] = diag
        p_ref[i] = diag * t + q_ref[i] + from_beside(t, gx, 0) + from_beside(t, gy, 1)
        return carry

    loop(levels, level, 0, unroll=U_FACTOR)


def eliminate(excess, u, y):
    r = rcp(excess + u)
    w = u * r
    return r, w, y * r, w * excess, w * y


def middle(s, sb, u, r, rb):
    return rcp((s * sb + u * (s + sb)) * r * rb)


def middle_responses(yr, yrb, w, wb, d):
    left, rightb = d * yr, d * yrb
    return (wb * left, rightb, left, w * rightb)


def factor_main(code_ref, t_ref, pack_ref, k_ref, w_ref, r_ref, yr_ref, left_ref, right_ref, g_ref, d_ref):
    levels, x, width = t_ref.shape
    first_loss, last_loss = end_losses()

    def tables(i, carry):
        pack_t, pack_k = carry
        k = by_code(code_ref[i], k_table)
        k_ref[i] = k
        loss = jnp.where(i == 0, first_loss, 0.0) + jnp.where(i == levels - 1, last_loss, 0.0)
        r_ref[i] = by_code(code_ref[i], cap_table, cap_unit) + loss
        return (lane_edge_of(t_ref[i], i, pack_t), lane_edge_of(k, i, pack_k))

    tile = jnp.zeros((x, LANES), F32)
    pack_ref[0], pack_ref[1] = loop(levels, tables, (tile, tile))
    zero = jnp.zeros((x, width), F32)

    half = levels // 2

    def inward(i, carry):
        ws, y, wsb, yb, *_ = carry
        b = levels - 1 - i
        u, ub = conductance(k_ref[i], k_ref[i + 1]), conductance(k_ref[b], k_ref[b - 1])
        s, sb = r_ref[i] + ws, r_ref[b] + wsb
        r, w, yr_ref[i], ws, y = eliminate(s, u, y)
        rb, wb, yr_ref[b], wsb, yb = eliminate(sb, ub, yb)
        r_ref[i], w_ref[i], r_ref[b], w_ref[b] = r, w, rb, wb
        return (ws, y, wsb, yb, s, sb, u, r, rb)

    one = zero + 1.0
    *_, s, sb, u, r, rb = loop(half, inward, (zero, one, zero, one) + (zero,) * 5)
    d = middle(s, sb, u, r, rb)
    d_ref[...] = d

    def outward(i, carry):
        left, right, leftb, rightb, pack_l, pack_r = carry
        b = levels - 1 - i
        w, wb = w_ref[i], w_ref[b]
        left, right = yr_ref[i] + w * left, w * right
        leftb, rightb = wb * leftb, yr_ref[b] + wb * rightb
        left_ref[i], right_ref[i], left_ref[b], right_ref[b] = left, right, leftb, rightb
        pack_l = lane_edge_of(leftb, b, lane_edge_of(left, i, pack_l))
        pack_r = lane_edge_of(rightb, b, lane_edge_of(right, i, pack_r))
        return (left, right, leftb, rightb, pack_l, pack_r)

    init = middle_responses(yr_ref[half - 1], yr_ref[half], w_ref[half - 1], w_ref[half], d)
    left, right, _, rightb, pack_ref[2], pack_ref[3] = loop(half, outward, init + (tile, tile), reverse=True)
    g_ref[0] = left + 0.5 * rcp(k_ref[0])
    g_ref[1] = right
    g_ref[2] = rightb + 0.5 * rcp(k_ref[levels - 1])


def assemble_halo(a_ref, b_ref, kh_ref, th_ref, qh_ref, pack_ref):
    is_even = even("plane")
    levels, _, width = kh_ref.shape
    row = lax.broadcasted_iota(jnp.int32, (SUB, width), 0)
    a_rows = [row == jnp.where(is_even, j, SUB - 1 - j) for j in (0, 1)]
    b_rows = [(row == jnp.where(is_even, SUB - 1 - j, j)) & has_b() for j in (0, 1)]

    def level(i, carry):
        pack_t, pack_k = carry
        halos = []
        for first, ref in ((0, th_ref), (2, kh_ref), (4, qh_ref)):
            halo = jnp.zeros((SUB, width), F32)
            for source, rows in ((a_ref, a_rows), (b_ref, b_rows)):
                for j in (0, 1):
                    halo = jnp.where(rows[j], source[first + j, pl.ds(i, 1), :], halo)
            ref[i] = halo
            halos.append(halo)
        return (lane_edge_of(halos[0], i, pack_t), lane_edge_of(halos[1], i, pack_k))

    zero = jnp.zeros((SUB, LANES), F32)
    pack_ref[0], pack_ref[1] = loop(levels, level, (zero, zero), unroll=64)


def first_side(p, t, k, left, right, th, kh, qh, gxh, gyh, diagh, wh, rh, yrh, lefth, righth, dh, rhs_ref, rhsh, send, pack_ref):
    levels, x, width = t.shape
    row = lax.broadcasted_iota(jnp.int32, (SUB, width), 0)
    lane = lax.broadcasted_iota(jnp.int32, (SUB, width), 1)
    first_loss, last_loss = end_losses()

    half = levels // 2

    def lateral(i, here, carry):
        bf, bl = carry
        temp, t_main, k_main = th[i], t[i], k[i]
        cap = cap_by_k(here)
        gx = conductance(here, jnp.where(row == SUB - 1, k_main[0:1], pltpu.roll(here, SUB - 1, 0)), lat_unit)
        g_low = conductance(here, jnp.where(row == 0, k_main[x - 1 :], pltpu.roll(here, 1, 0)), lat_unit)
        gy = conductance(here, pltpu.roll(here, width - 1, 1), lat_unit)
        gy = jnp.where(lane == width - 1, 0.0, gy)
        gxh[i], gyh[i] = gx, gy
        diag = cap - gx - g_low - gy - pltpu.roll(gy, 1, 1)
        diagh[i] = diag
        step_up = jnp.where(row == SUB - 1, t_main[0:1], pltpu.roll(temp, SUB - 1, 0))
        step_low = jnp.where(row == 0, t_main[x - 1 :], pltpu.roll(temp, 1, 0))
        rhsh[i] = diag * temp + qh[i] + gx * step_up + g_low * step_low + from_beside(temp, gy, 1)
        to_first = pltpu.roll(gx * (temp - step_up), 1, 0)
        to_last = pltpu.roll(g_low * (temp - step_low), SUB - 1, 0)
        rhs = p[i]
        parts = [rhs[j : j + SUB] for j in range(0, x, SUB)]
        parts[0] = parts[0] + jnp.where(row == 0, to_first, 0.0)
        parts[-1] = parts[-1] + jnp.where(row == SUB - 1, to_last, 0.0)
        rhs = jnp.concatenate(parts, axis=0)
        rhs_ref[i] = rhs
        return cap, (bf + left[i] * rhs, bl + right[i] * rhs)

    def inward(i, carry):
        ws, y, wsb, yb, here, hereb, ends = carry[:7]
        b = levels - 1 - i
        after, before = kh[i + 1], kh[b - 1]
        u, ub = conductance(here, after), conductance(hereb, before)
        cap, ends = lateral(i, here, ends)
        capb, ends = lateral(b, hereb, ends)
        s = cap + jnp.where(i == 0, first_loss, 0.0) + ws
        sb = capb + jnp.where(i == 0, last_loss, 0.0) + wsb
        r, w, yrh[i], ws, y = eliminate(s, u, y)
        rb, wb, yrh[b], wsb, yb = eliminate(sb, ub, yb)
        rh[i], wh[i], rh[b], wh[b] = r, w, rb, wb
        return (ws, y, wsb, yb, after, before, ends, s, sb, u, r, rb)

    zero, zero_main = jnp.zeros((SUB, width), F32), jnp.zeros((x, width), F32)
    one = zero + 1.0
    init = (zero, one, zero, one, kh[0], kh[levels - 1], (zero_main, zero_main)) + (zero,) * 5
    *_, (bf, bl), s, sb, u, r, rb = loop(half, inward, init, unroll=U_SIDE)
    d = middle(s, sb, u, r, rb)
    dh[...] = d

    def outward(i, carry):
        ll, rr, llb, rrb, bfh, blh, pack_l, pack_r = carry
        b = levels - 1 - i
        w, wb, rhs, rhsb = wh[i], wh[b], rhsh[i], rhsh[b]
        ll, rr = yrh[i] + w * ll, w * rr
        llb, rrb = wb * llb, yrh[b] + wb * rrb
        lefth[i], righth[i], lefth[b], righth[b] = ll, rr, llb, rrb
        pack_l = lane_edge_of(llb, b, lane_edge_of(ll, i, pack_l))
        pack_r = lane_edge_of(rrb, b, lane_edge_of(rr, i, pack_r))
        return (ll, rr, llb, rrb, bfh + ll * rhs + llb * rhsb, blh + rr * rhs + rrb * rhsb, pack_l, pack_r)

    tile = jnp.zeros((SUB, LANES), F32)
    init = middle_responses(yrh[half - 1], yrh[half], wh[half - 1], wh[half], d) + (zero, zero, tile, tile)
    ll, rr, _, rrb, bfh, blh, pack_ref[0], pack_ref[1] = loop(half, outward, init, unroll=U_BACK, reverse=True)
    for j in range(0, x, SUB):
        send[j // SUB] = bf[j : j + SUB]
        send[(x + j) // SUB] = bl[j : j + SUB]
    send[2 * x // SUB] = packed(bfh, blh)
    edges = [0.5 * rcp(jnp.maximum(kh[i], 1e-3)) for i in (0, levels - 1)]
    send[2 * x // SUB + 1] = packed(ll + edges[0], rr)
    send[2 * x // SUB + 2] = packed(rrb + edges[1], rrb)


def both(main_ref, halo_ref, i):
    return jnp.concatenate([main_ref[i], halo_ref[i]], axis=0)


def join_rows(gxh, k, kh, gx_in, diag_in, gx_ref, diag_ref):
    levels, x, _ = k.shape

    def level(i, carry):
        g_first = gxh[i, SUB - 1 : SUB, :]
        g_last = conductance(k[i, x - 1 : x, :], kh[i, 0:1, :], lat_unit)
        gx_ref[i, x - 1 : x, :] = g_last
        diag_ref[i, 0:1, :] = diag_in[i, 0:1, :] - g_first
        diag_ref[i, x - 1 : x, :] = diag_in[i, x - 1 : x, :] - g_last
        return carry

    loop(levels, level, 0, unroll=64)


def right_side(last, *refs):
    t, th, q, qh, diag, diagh, gx, gxh, gy, gyh, left, lefth, right, righth, *out = refs
    levels, x, width = t.shape
    send = out[-1]
    rows = x if last else x + SUB

    def pick(main_ref, halo_ref, i):
        return main_ref[i] if last else both(main_ref, halo_ref, i)

    def level(i, carry):
        bf, bl = carry
        temp = both(t, th, i)
        here = temp[:rows]
        rhs = pick(diag, diagh, i) * here + pick(q, qh, i) + from_beside(temp, both(gx, gxh, i), 0)[:rows]
        rhs = rhs + from_beside(here, pick(gy, gyh, i), 1)
        out[0][i] = rhs[:x]
        if not last:
            out[1][i] = rhs[x:]
        return (bf + pick(left, lefth, i) * rhs, bl + pick(right, righth, i) * rhs)

    zero = jnp.zeros((rows, width), F32)
    parts = loop(levels, level, (zero, zero), unroll=U_LAST if last else U_RIGHT)
    groups = [part[j : j + SUB] for part in parts for j in range(0, x, SUB)]
    if not last:
        groups.append(packed(*[part[x:] for part in parts]))
    for j, group in enumerate(groups):
        send[j] = group


def edge_flow(first, x, rows, *refs):
    raw, pack, packh, packh_lr, other, otherh, *refs = refs
    own_k, other_k = (jnp.concatenate([a[1], b[1]], axis=0)[:rows] for a, b in ((pack, packh), (other, otherh)))
    if first:
        own_t, other_t = (jnp.concatenate([a[0], b[0]], axis=0)[:rows] for a, b in ((pack, packh), (other, otherh)))
    else:
        own_t, other_t = refs[0][:rows], refs[1][:rows]
    flow_ref, send = refs[-2:]
    flow = conductance(own_k, other_k, lat_unit) * (other_t - own_t)
    flow_ref[...] = flow
    at_low = lax.axis_index("phys") == 1
    lane = lax.broadcasted_iota(jnp.int32, flow.shape, 1)
    changes = []
    for j in (0, 1):
        response = jnp.concatenate([pack[2 + j], packh_lr[j]], axis=0)[:rows]
        change = jnp.sum(flow * response, axis=1, keepdims=True)
        changes.append(jnp.where(lane == jnp.where(at_low, 0, LANES - 1), change, 0.0))
    groups = [change[j : j + SUB] for change in changes for j in range(0, x, SUB)]
    if rows > x:
        groups.append(packed(*[change[x:] for change in changes]))
    for j in range(send.shape[0]):
        send[j] = add_at_edge(raw[j], groups[j]) if j < len(groups) else raw[j]


def forward_sweep(flow, *refs):
    count = len(refs) // 4
    w, r, rhs, z = (refs[j * count : (j + 1) * count] for j in range(4))
    levels, x, width = z[0].shape

    def pick(pair, i):
        return jnp.concatenate([ref[i] for ref in pair], axis=0)

    def put(i, wy):
        y = add_at_edge(pick(rhs, i) + wy, lane_unedge(flow[...], i))
        value = pick(r, i) * y
        z[0][i] = value[:x]
        if count > 1:
            z[1][i] = value[x:]
        return pick(w, i) * y

    def level(i, carry):
        return (put(i, carry[0]), put(levels - 1 - i, carry[1]))

    zero = jnp.zeros((flow.shape[0], width), F32)
    loop(levels // 2, level, (zero, zero), unroll=U_SWEEP)


def packed(a, b):
    row = lax.broadcasted_iota(jnp.int32, a.shape, 0)
    return jnp.where((row >= 2) & (row < 6), pltpu.roll(b, 4, 0), a)


def block_flows(g_sets, h_sets, b_sets, x, rows):
    place, count = lax.axis_index("stack"), lax.axis_size("stack")

    def at(sets, block, read):
        value = read(sets[0])
        for j in range(1, count):
            value = jnp.where((place ^ j) == block, read(sets[j]), value)
        return value

    def ends(block):
        group = at(b_sets, block, lambda ref: ref[0 : 2 * x // SUB])
        group = group.reshape(2, x, group.shape[-1])
        if rows == x:
            return (group[0], group[1])
        tail = at(b_sets, block, lambda ref: ref[2 * x // SUB])
        return (
            jnp.concatenate([group[0], tail], axis=0),
            jnp.concatenate([group[1], pltpu.roll(tail, 4, 0)], axis=0),
        )

    def responses(block):
        group = at(g_sets, block, lambda ref: ref[0:3])
        if rows == x:
            return group
        tail = at(h_sets, block, lambda ref: ref[2 * x // SUB + 1 : 2 * x // SUB + 3])
        tails = (tail[0], pltpu.roll(tail[0], 4, 0), tail[1])
        return [jnp.concatenate([group[j], tails[j]], axis=0) for j in range(3)]

    end = [ends(block) for block in range(count)]
    g = [responses(block) for block in range(count)]
    ups, flows = [], []
    for j in range(count - 1):
        pivot = g[j][2] + g[j + 1][0]
        value = end[j + 1][0] - end[j][1]
        if j:
            pivot = pivot - g[j][1] * ups[j - 1]
            value = value + g[j][1] * flows[j - 1]
        inverse = rcp(pivot)
        ups.append(g[j + 1][1] * inverse)
        flows.append(value * inverse)
    for j in reversed(range(count - 2)):
        flows[j] = flows[j] + ups[j] * flows[j + 1]
    top = jnp.zeros_like(flows[0])
    bottom = top
    for j in range(count - 1):
        top = jnp.where(place == j + 1, -flows[j], top)
        bottom = jnp.where(place == j, flows[j], bottom)
    return top, bottom


def beside(edge, flow, k_edge, code_beside):
    return edge + flow * (0.5 * rcp(k_edge) + 0.5 * rcp(by_code(code_beside, k_table)))


def layers_beside(za, zb):
    is_even = even("stack")
    sides = []
    for j in (0, 1):
        value = [jnp.where(is_even, (zb, za)[j][3 + e], (za, zb)[j][3 + e]) for e in range(5)]
        value[4] = jnp.maximum(value[4], 0.1)
        sides.append(value)
    return sides


def rate_by_flag(active):
    return jnp.where(active, F32(creep_rate * inv_e), F32(0.0))


def across(above, below, w, wb, d):
    return (d * (below + wb * above), d * (above + w * below))


def column_solve(count, first, *refs):
    g_sets, h_sets, refs = refs[:count], refs[count : 2 * count], refs[2 * count :]
    b_sets = h_sets
    if not first:
        b_sets, refs = refs[:count], refs[count:]
    z, zh, w, wh, yr, yrh, d, dh, t, th, pack_ref, flow_ref = refs
    levels, x, width = z.shape
    rows = x + SUB
    top, bottom = block_flows(g_sets, h_sets, b_sets, x, rows)
    flow_ref[0], flow_ref[1] = top[:x], bottom[:x]

    def level(i, carry):
        above, below, pack = carry
        b = levels - 1 - i
        above = both(z, zh, i) + top * both(yr, yrh, i) + both(w, wh, i) * above
        below = both(z, zh, b) + bottom * both(yr, yrh, b) + both(w, wh, b) * below
        for place, value in ((i, above), (b, below)):
            t[place] = value[:x]
            th[place] = value[x:]
            pack = lane_edge_of(value, place, pack)
        return (above, below, pack)

    half = levels // 2
    above = both(z, zh, half - 1) + top * both(yr, yrh, half - 1)
    below = both(z, zh, half) + bottom * both(yr, yrh, half)
    d_all = jnp.concatenate([d[...], dh[...]], axis=0)
    init = across(above, below, both(w, wh, half - 1), both(w, wh, half), d_all)
    *_, pack_ref[...] = loop(half, level, init + (jnp.zeros((rows, LANES), F32),), unroll=U_SOLVE, reverse=True)


def prepare_creep(code_ref, flag_ref, mod, exp, rate):
    def level(i, carry):
        code = code_ref[i]
        mod[i] = by_code(code, mod_table)
        exp[i] = by_code(code, expand_table)
        rate[i] = rate_by_flag(flag_ref[i] == 1)
        return carry

    loop(code_ref.shape[0], level, 0)


def creep_cells(temp, mod, exp, rate, dist, creep, hard):
    elastic = dist - exp * temp
    strain = elastic - creep
    drive = jnp.exp2((0.5 * log2e) * mod * jnp.abs(strain) * rcp(hard) - 1.0)
    drive = drive - 0.25 * rcp(drive)
    rate = rate * jnp.exp2(-log2e * rcp(jnp.exp2((0.5 * log2e) * temp + 1.0) + 1.0)) * drive
    gap = 1.0 - hard * jnp.exp2(-0.1 * jnp.log2(0.5 + drive) - 1.0)
    gap_size = jnp.abs(gap)
    root = gap_size * lax.rsqrt(jnp.maximum(gap_size, 1e-30))
    creep = creep + jnp.where(strain < 0.0, -rate, rate)
    hard = hard + gap * root * rate
    return (elastic, creep, hard)


def creep_beside(t, flow, k, za, zb, state):
    ends, results = (0, t.shape[0] - 1), []
    for j, (code, flag, dist, creep, hard) in enumerate(layers_beside(za, zb)):
        if state is not None:
            creep, hard = state[j], state[2 + j]
        temp = beside(t[ends[j]], flow[j], k[ends[j]], code)
        mod = by_code(code, mod_table)
        cells = creep_cells(temp, mod, by_code(code, expand_table), rate_by_flag(flag == 1.0), dist, creep, hard)
        results.append((*cells, mod))
    return results


def creep_step(first, *refs):
    main, refs = refs[:7], refs[7:]
    flow, k, za, zb = refs[:4]
    state, out = (None, refs[4:]) if first else (refs[4], refs[5:])

    def level(i, carry):
        _, out[0][i], out[1][i] = creep_cells(*[ref[i] for ref in main])
        return carry

    loop(main[0].shape[0], level, 0, unroll=U_CREEP)
    for j, (_, creep, hard, _) in enumerate(creep_beside(main[0], flow, k, za, zb, state)):
        out[2][j] = creep
        out[2][2 + j] = hard


def solve_and_creep(count, *refs):
    g_sets, b_sets, refs = refs[:count], refs[count : 2 * count], refs[2 * count :]
    z, w, yr, d, mod, exp, rate, dist, creep, hard = refs[:10]
    t, creep_out, hard_out, s, flow_ref, xa, xb, pack_ref = refs[10:]
    levels, x, width = z.shape
    top, bottom = block_flows(g_sets, None, b_sets, x, x)

    def put(i, value, pack):
        t[i] = value
        m = mod[i]
        elastic, new, hard_out[i] = creep_cells(value, m, exp[i], rate[i], dist[i], creep[i], hard[i])
        creep_out[i] = new
        stress = m * (elastic - new)
        s[i] = stress
        return lane_edge_of(stress, i, pack)

    def level(i, carry):
        above, below, pack = carry
        b = levels - 1 - i
        above = z[i] + top * yr[i] + w[i] * above
        below = z[b] + bottom * yr[b] + w[b] * below
        return (above, below, put(b, below, put(i, above, pack)))

    half = levels // 2
    above, below = z[half - 1] + top * yr[half - 1], z[half] + bottom * yr[half]
    init = across(above, below, w[half - 1], w[half], d[...])
    *_, pack_ref[...] = loop(half, level, init + (jnp.zeros((x, LANES), F32),), unroll=U_FINAL, reverse=True)
    flow_ref[0], flow_ref[1] = top, bottom
    is_even = even("plane")
    upper, lower = s[:, x - 1, :], s[:, 0, :]
    xa[...] = jnp.where(is_even, upper, lower)
    xb[...] = jnp.where(is_even, lower, upper)


def balance_inside(s, t, creep, hard, flow, k, za, zb, state, t_out, creep_out, hard_out, inside, sem):
    copies = [
        pltpu.make_async_copy(held, out, sem.at[j])
        for j, (held, out) in enumerate(((t, t_out), (creep, creep_out), (hard, hard_out)))
    ]
    for copy in copies:
        copy.start()
    levels, x, width = s.shape
    row = lax.broadcasted_iota(jnp.int32, (x, width), 0)
    lane = lax.broadcasted_iota(jnp.int32, (x, width), 1)
    place, count = lax.axis_index("stack"), lax.axis_size("stack")
    zs = [
        jnp.where(place == end, 0.0, m * (elastic - new))
        for end, (elastic, new, _, m) in zip((0, count - 1), creep_beside(t, flow, k, za, zb, state))
    ]

    def level(i, before):
        here = s[i]
        after = jnp.where(i == levels - 1, zs[1], s[jnp.minimum(i + 1, levels - 1)])
        total = before + after - 6.0 * here
        total = total + jnp.where(row == 0, 0.0, pltpu.roll(here, 1, 0))
        total = total + jnp.where(row == x - 1, 0.0, pltpu.roll(here, x - 1, 0))
        total = total + jnp.where(lane == 0, 0.0, pltpu.roll(here, 1, 1))
        inside[i] = total + jnp.where(lane == width - 1, 0.0, pltpu.roll(here, width - 1, 1))
        return here

    loop(levels, level, zs[0], unroll=8)
    for copy in copies:
        copy.wait()


def balance_edges(inside, xa, xb, other, out, held, sem):
    levels, x, width = inside.shape
    is_even = even("plane")
    row = lax.broadcasted_iota(jnp.int32, (x, width), 0)
    a_row = row == jnp.where(is_even, x - 1, 0)
    b_row = (row == jnp.where(is_even, 0, x - 1)) & has_b()
    chunks = sem.shape[0]
    part = levels // chunks
    copies = []
    for chunk in range(chunks):

        def level(j, carry, chunk=chunk):
            i = chunk * part + j
            total = inside[i] + jnp.where(a_row, xa[pl.ds(i, 1), :], 0.0)
            total = total + jnp.where(b_row, xb[pl.ds(i, 1), :], 0.0)
            held[i] = add_at_edge(total, lane_unedge(other[...], i))
            return carry

        loop(part, level, 0)
        place = pl.ds(chunk * part, part)
        copies.append(pltpu.make_async_copy(held.at[place], out.at[place], sem.at[chunk]))
        copies[-1].start()
    for copy in copies:
        copy.wait()


def per_device(temp, source, code, flag, distortion, creep, hard):
    levels, x, width = temp.shape
    count = lax.axis_size("stack")
    if lax.axis_size("phys") != 2 or count != 4 or lax.axis_size("plane") % 2 or levels > LANES or x % SUB or width % LANES:
        raise ValueError("unsupported sizes")
    main, halo, layers = (levels, x, width), (levels, SUB, width), (2, x, width)
    cells = levels * x * width
    swap = [(0, 1), (1, 0)]
    peers = [[(i, i ^ j) for i in range(count)] for j in range(1, count)]
    dma = pltpu.SemaphoreType.DMA

    edge = (6, levels, width)
    rows_a, rows_b = call(
        edge_rows,
        (temp, code, source),
        [edge] * 2,
        "edge_rows",
        cells,
        [
            pltpu.VMEM((2, *edge), F32),
            pltpu.VMEM((2, levels, width), F32),
            pltpu.VMEM((2, 3, levels, width), jnp.int32),
            dma((2, 8)),
            dma((2,)),
        ],
        in_hbm=3,
        out_hbm=2,
        vmem=60,
    )
    rows_a, rows_b = plane_exchange(rows_a, rows_b)
    pack, k, w, r, yr, left, right, g, d = call(
        factor_main, (code, temp), [(4, x, LANES)] + [main] * 6 + [(3, x, width), (x, width)], "factor_main", 30 * cells
    )
    gx, gy, diag, part = call(lateral_main, (k, temp, source), [main] * 4, "lateral_main", 40 * cells)
    za, zb = call(edge_layers, (code, flag, distortion, creep, hard, g), [(8, x, width)] * 2, "edge_layers", cells, after=(part,))
    za, g_two, zb = lax.ppermute(za, "stack", peers[0]), lax.ppermute(g, "stack", peers[1]), lax.ppermute(zb, "stack", peers[2])
    g_sets = [g, za, g_two, zb]
    other_pack = lax.ppermute(pack[:2], "phys", swap)

    kh, th, qh, packh = call(
        assemble_halo, (rows_a, rows_b), [halo] * 3 + [(2, SUB, LANES)], "assemble_halo", cells, after=(part,)
    )
    other_packh = lax.ppermute(packh, "phys", swap)
    rows = x + SUB
    groups = 2 * x // SUB
    gxh, gyh, diagh, wh, rh, yrh, lefth, righth, dh, rhs, rhsh, send, packh_lr = call(
        first_side,
        (part, temp, k, left, right, th, kh, qh),
        [halo] * 8 + [(SUB, width), main, halo, (groups + 3, SUB, width), (2, SUB, LANES)],
        "first_side",
        40 * cells,
    )

    own = other = state = None
    for step in range(TSTEPS):
        first, last = step == 0, step == TSTEPS - 1
        if not first:
            ins = (temp, th, source, qh, diag, diagh, gx, gxh, gy, gyh, left, lefth, right, righth)
            send = (groups if last else groups + 1, SUB, width)
            rhs, *rhsh, send = call(
                functools.partial(right_side, last), ins, [main, send] if last else [main, halo, send], "right_side", 30 * cells
            )
            rhsh = rhsh[0] if rhsh else None
        flow_rows = x if last else rows
        lane_flow, send = call(
            functools.partial(edge_flow, first, x, flow_rows),
            [send, pack, packh, packh_lr, other_pack, other_packh] + ([] if first else [own, other]),
            [(flow_rows, LANES), send.shape],
            "edge_flow",
            cells // 8,
        )
        b_sets = [send] + [lax.ppermute(send, "stack", peer) for peer in peers]
        ins = [lane_flow, w, r, rhs] if last else [lane_flow, w, wh, r, rh, rhs, rhsh]
        z, *zh = call(
            forward_sweep, ins, [main] if last else [main, halo], "forward_sweep", cells, aliases={3: 0} if last else {5: 0, 6: 1}
        )
        zh = zh[0] if zh else None
        if first:
            h_sets = b_sets
            mod, exp, rate = call(prepare_creep, (code, flag), [main] * 3, "prepare_creep", 10 * cells, after=(z,))
            gx, diag = call(join_rows, (gxh, k, kh, gx, diag), [main] * 2, "join_rows", cells, aliases={3: 0, 4: 1}, after=(rate,))
        else:
            creep, hard, state = call(
                functools.partial(creep_step, step == 1),
                [temp, mod, exp, rate, distortion, creep, hard, flow, k, za, zb] + ([] if step == 1 else [state]),
                [main] * 2 + [(4, x, width)],
                "creep_step",
                60 * cells,
            )
        if last:
            break
        temp, th, own, flow = call(
            functools.partial(column_solve, count, first),
            g_sets + h_sets + ([] if first else b_sets) + [z, zh, w, wh, yr, yrh, d, dh],
            [main, halo, (rows, LANES), layers],
            "column_solve",
            10 * cells,
            after=(rate, diag) if first else (creep,),
        )
        other = lax.ppermute(own, "phys", swap)

    temp, creep, hard, stress, flow, xa, xb, pack = call(
        functools.partial(solve_and_creep, count),
        g_sets + b_sets + [z, w, yr, d, mod, exp, rate, distortion, creep, hard],
        [main] * 4 + [layers] + [(levels, width)] * 2 + [(x, LANES)],
        "solve_and_creep",
        70 * cells,
    )
    xa, xb = plane_exchange(xa, xb)
    other = lax.ppermute(pack, "phys", swap)
    temp, creep, hard, inside = call(
        balance_inside,
        (stress, temp, creep, hard, flow, k, za, zb, state),
        [main] * 4,
        "balance_inside",
        20 * cells,
        [dma((3,))],
        out_hbm=3,
    )
    (residual,) = call(
        balance_edges,
        (inside, xa, xb, other),
        [main],
        "balance_edges",
        10 * cells,
        [pltpu.VMEM(main, F32), dma((4,))],
        out_hbm=1,
    )
    return (temp, creep, hard, residual)


def solution(mesh):
    spec = P("stack", "plane", "phys")
    return jax.shard_map(per_device, mesh=mesh, in_specs=(spec,) * 7, out_specs=(spec,) * 4, check_vma=False)
```
